512 devices in a mesh: lat: 16 (over z_lo, core), lon: 32 (over y, x, z_hi).
Axes of the slice: x: 4, y: 4, z: 16 (z_hi: 2, z_lo: 8; z = z_hi * 8 + z_lo), core: 2. Of those that a mesh axis runs over, the one named last changes fastest.
Arguments:
- tokens: bfloat16 [768, 1152, 512], P('lat', 'lon'), may hold values from -6 to 6
- region: int32 [768, 1152], P('lat', 'lon'), may hold values from 0 to 2
- ln_gain: float32 [512], replicated, may hold values from 0.1 to 1.9
- qkv_weight: bfloat16 [512, 1536], P('lon'), may hold values from -1.5 to 1.5, as said below
- proj_weight: bfloat16 [512, 512], P('lon'), may hold values from -0.25 to 0.25
- position_bias: float32 [16, 72, 72], replicated, may hold values from -4 to 4
Outputs:
- mixed: bfloat16 [768, 1152, 512], P('lat', 'lon')
The draws below stay inside these ranges and needn't reach their ends.
Inputs may be any that keep to these rules, and one draw needn't show every extreme that they name: `qkv_weight`: entries of order C ** -0.5, except that the query and key columns of some heads may be up to 7 times larger.
All inputs are finite; a program needn't handle non-finite values.
Results may differ from the reference program's by a relative error of at most 0.0055.
Values may be sent and summed in bfloat16 or wider, within the bound.
A program may use at most 64 MiB of HBM per device.

```python
import jax
import jax.numpy as jnp
from jax import lax

HEADS = 16
HD = 32
C = 512
WIN_LAT = 6
WIN_LON = 12
WIN = 72
SHIFT_LAT = 3
SHIFT_LON = 6
NLAT = 768
NLON = 1152


def draw_qkv_weight(key, part):
    key = jax.random.fold_in(key, 11)
    k_base = jax.random.fold_in(key, 0)
    base = jax.random.normal(k_base, (C, 3 * C), jnp.float32) * C ** (-0.5)
    return jnp.clip(base, -1.5, 1.5).astype(jnp.bfloat16)


def place_ends(drawn, stream_key, smallest, top_value):
    longest = drawn.shape.index(max(drawn.shape))
    spots = []
    for shift in (0, 1):
        where = [jax.random.randint(jax.random.fold_in(stream_key, axis), (), 0, length) for axis, length in enumerate(drawn.shape)]
        where[longest] = (where[longest] + shift) % drawn.shape[longest]
        spots.append(tuple(where))
    return drawn.at[spots[0]].set(smallest).at[spots[1]].set(top_value)


def block_scale(own_key, dims, cuts, least, top_value):
    level = 1.0
    for dim, blocks in cuts:
        steps = jax.random.uniform(jax.random.fold_in(jax.random.fold_in(own_key, 6), dim), (blocks,), jnp.float32, least / len(cuts), top_value / len(cuts))
        level = level * jnp.repeat(jnp.exp(steps), dims[dim] // blocks).reshape((-1,) + (1,) * (len(dims) - 1 - dim))
    return level


def gaussian(key, dims, scale, limit, cuts=(), held_as=jnp.bfloat16):
    entries = scale * jax.random.normal(key, dims, jnp.float32)
    if cuts:
        entries = entries * block_scale(key, dims, cuts, -0.22, 0.18)
    return jnp.clip(entries, -limit, limit).astype(held_as)


def setup_inputs(seed: int = 0) -> dict:
    splits = jax.random.split(jax.random.key(seed), 7)
    return {
        "tokens": gaussian(splits[0], (NLAT, NLON, C), 1.0, 6.0, ((0, 16), (1, 32))),
        "region": place_ends(jax.random.randint(splits[1], (NLAT, NLON), 0, 3), jax.random.fold_in(splits[1], 1), 0, 2).astype(jnp.int32),
        "ln_gain": jnp.clip(1.0 + 0.18 * jax.random.normal(splits[2], (C,), jnp.float32), 0.1, 1.9),
        "qkv_weight": draw_qkv_weight(jax.random.fold_in(splits[6], 71), 0),
        "proj_weight": gaussian(splits[4], (C, C), C ** -0.5, 0.25, ((0, 32),)),
        "position_bias": gaussian(splits[5], (HEADS, WIN, WIN), 1.0, 4.0, (), jnp.float32),
    }


def layer_norm(x, gain):
    xf = x.astype(jnp.float32)
    mean = lax.optimization_barrier(jnp.mean(xf, axis=-1, keepdims=True))
    var = lax.optimization_barrier(jnp.mean((xf - mean) ** 2, axis=-1, keepdims=True))
    return ((xf - mean) * lax.rsqrt(var + 1e-05) * gain).astype(jnp.bfloat16)

def attend_windows(win, regw, loww, qkv_weight, proj_weight, position_bias):
    count = win.shape[0]
    width = win.shape[2]
    qkv = jnp.dot(win.reshape(count * WIN, width), qkv_weight, preferred_element_type=jnp.float32).astype(jnp.bfloat16)
    qkv = qkv.reshape(count, WIN, 3, HEADS, HD)
    query = qkv[:, :, 0].astype(jnp.float32)
    keys = qkv[:, :, 1].astype(jnp.float32)
    values = qkv[:, :, 2].astype(jnp.float32)
    scores = jnp.einsum('gqhd,gkhd->ghqk', query, keys) * HD ** (-0.5) + position_bias[None]
    allowed = (regw[:, :, None] == regw[:, None, :]) & (loww[:, :, None] == loww[:, None, :])
    scores = jnp.where(allowed[:, None], scores, -1e+30)
    top = lax.optimization_barrier(jnp.max(scores, axis=-1, keepdims=True))
    expo = jnp.exp(scores - top)
    probs = (expo / lax.optimization_barrier(jnp.sum(expo, axis=-1, keepdims=True))).astype(jnp.bfloat16)
    context = jnp.einsum('ghqk,gkhd->gqhd', probs.astype(jnp.float32), values).astype(jnp.bfloat16)
    out = jnp.dot(context.reshape(count * WIN, width), proj_weight, preferred_element_type=jnp.float32)
    return out.astype(jnp.bfloat16).reshape(count, WIN, width)

def to_windows(x, rows, cols):
    nr = rows // WIN_LAT
    nc = cols // WIN_LON
    rest = x.shape[2:]
    y = x.reshape((nr, WIN_LAT, nc, WIN_LON) + rest)
    y = jnp.moveaxis(y, 2, 1)
    return y.reshape((nr * nc, WIN) + rest)

def from_windows(y, rows, cols):
    nr = rows // WIN_LAT
    nc = cols // WIN_LON
    width = y.shape[-1]
    x = y.reshape(nr, nc, WIN_LAT, WIN_LON, width)
    x = jnp.moveaxis(x, 1, 2)
    return x.reshape(rows, cols, width)

def reference(tokens, region, ln_gain, qkv_weight, proj_weight, position_bias):
    rows, cols, width = tokens.shape
    normed = layer_norm(tokens, ln_gain)
    shifted = jnp.roll(normed, (-SHIFT_LAT, -SHIFT_LON), (0, 1))
    labels = jnp.roll(region, (-SHIFT_LAT, -SHIFT_LON), (0, 1))
    low = jnp.roll(jnp.arange(rows) < SHIFT_LAT, -SHIFT_LAT).astype(jnp.int32)
    lowgrid = jnp.broadcast_to(low[:, None], (rows, cols))
    band_h = shifted.reshape(rows // WIN_LAT, WIN_LAT, cols, width)
    band_r = labels.reshape(rows // WIN_LAT, WIN_LAT, cols)
    band_l = lowgrid.reshape(rows // WIN_LAT, WIN_LAT, cols)

    def one_band(args):
        hb, rb, lb = args
        win = to_windows(hb, WIN_LAT, cols)
        out = attend_windows(win, to_windows(rb, WIN_LAT, cols), to_windows(lb, WIN_LAT, cols), qkv_weight, proj_weight, position_bias)
        return from_windows(out, WIN_LAT, cols)
    bands = lax.map(one_band, (band_h, band_r, band_l))
    attended = jnp.roll(bands.reshape(rows, cols, width), (SHIFT_LAT, SHIFT_LON), (0, 1))
    return (tokens.astype(jnp.float32) + attended.astype(jnp.float32)).astype(jnp.bfloat16)
```

```python
import functools
import math

import jax
import jax.numpy as jnp
from jax import lax
from jax.experimental import pallas as pl
from jax.experimental.pallas import tpu as pltpu
from jax.sharding import PartitionSpec as P

HEADS = 16
HD = 32
C = 512
WIN = 72
ROWS = 48
COLS = 36
EXT = 48
FEAT = 128
WIDE = C + FEAT
LOG2E = math.log2(math.e)
SCALE = HD**-0.5 * LOG2E
MASKED = -1e30
UNITS = 18
BF = jnp.bfloat16
F32 = jnp.float32
I32 = jnp.int32
MESH = pl.DeviceIdType.MESH
NT = (((1,), (1,)), ((), ()))


def dot(a, b):
    return jnp.dot(a, b, preferred_element_type=F32)


def dot_nt(a, b, precision=None):
    return lax.dot_general(a, b, NT, preferred_element_type=F32, precision=precision)


def token_parts(t):
    half = (t >= 36).astype(I32)
    u = t - 36 * half
    c = (u * 43) >> 7
    return half, c, u - 3 * c


def block_place(t):
    half, c, r = token_parts(t)
    return c * 16 + half * 3 + r


def normed_rows(x, gain):
    mean = jnp.sum(x, axis=-1, keepdims=True) * (1.0 / C)
    d = x - mean
    var = jnp.sum(d * d, axis=-1, keepdims=True) * (1.0 / C)
    return (d * lax.rsqrt(var + 1e-05) * gain).astype(BF).astype(F32)


def kernel(
    nlat,
    nlon,
    tok,
    reg,
    gain_hbm,
    wqkv,
    wproj,
    bias_hbm,
    out,
    xo,
    halo,
    relay,
    lab_own,
    lab_send,
    lab_recv,
    lab_ext,
    lab_t,
    gain,
    bias_raw,
    bias,
    wbuf,
    wvt,
    wpt,
    xn,
    acc,
    xwin,
    pk_top,
    pk_bot,
    qk,
    vt,
    ctx,
    loc_sem,
    out_sem,
    z_send,
    z_recv,
    own_send,
    own_recv,
    par_send,
    par_recv,
    sib_send,
    sib_recv,
    leg_send,
    leg_recv,
    halo_send,
    halo_recv,
    lab_ssem,
    lab_rsem,
    lat_send,
    lat_recv,
):
    shard = C // nlon
    plane = nlon // 2
    lat = lax.axis_index("lat")
    lon = lax.axis_index("lon")
    core = lax.rem(lat, 2)
    zhi = lax.rem(lon, 2)
    m = lon // 2
    lat_up = lax.rem(lat + 1, nlat)
    lat_dn = lax.rem(lat + nlat - 1, nlat)
    lon_up = lax.rem(lon + 1, nlon)
    lon_dn = lax.rem(lon + nlon - 1, nlon)
    lon_pair = lon + 1 - 2 * zhi
    lat_mirror = (nlat // 2 - 1 - lat // 2) * 2 + core
    lat_sib = lat + 1 - 2 * core

    zlo = nlat // 2
    ring = 2 * zlo
    leg = zlo // 2
    z = zhi * zlo + lat // 2

    def chip_at(column, place):
        place = lax.rem(place + 2 * ring, ring)
        return lax.rem(place, zlo) * 2 + core, column * 2 + place // zlo

    above = chip_at(m, z + leg)
    below = chip_at(m, z - leg)

    def beyond(place, by):
        lat_s, lon_s = chip_at(m, place)
        return lat_s, lax.rem(lon_s + by + nlon, nlon)

    onward = (beyond(z - leg, 1), beyond(z + leg, -1))
    relays_here = (
        chip_at(lon_dn // 2, lax.rem(lon_dn, 2) * zlo + lat // 2 + leg),
        chip_at(lon_up // 2, lax.rem(lon_up, 2) * zlo + lat // 2 - leg),
    )

    loads = [
        pltpu.make_async_copy(wqkv.at[:, 0:1024], wbuf.at[0, pl.ds(lon * shard, shard), :], loc_sem.at[0]),
        pltpu.make_async_copy(
            wqkv.at[:, 1024:1536], wbuf.at[1, pl.ds(lon * shard, shard), 0:512], loc_sem.at[1]
        ),
        pltpu.make_async_copy(wproj, wbuf.at[1, pl.ds(lon * shard, shard), 512:1024], loc_sem.at[2]),
        pltpu.make_async_copy(reg, lab_own, loc_sem.at[3]),
        pltpu.make_async_copy(tok, xo, loc_sem.at[4]),
        pltpu.make_async_copy(gain_hbm, gain, loc_sem.at[5]),
        pltpu.make_async_copy(bias_hbm, bias_raw, loc_sem.at[6]),
    ]
    for copy in loads:
        copy.start()

    barrier = pltpu.get_barrier_semaphore()
    greeted = (
        (lat, lon_up),
        (lat, lon_dn),
        (lat_up, lon),
        (lat_dn, lon),
        (lat_mirror, lon_pair),
        above,
        below,
    )
    greeted = greeted + relays_here
    for there in greeted:
        pl.semaphore_signal(barrier, inc=1, device_id=there, device_id_type=MESH)

    def greet(d, carry):
        pl.semaphore_signal(
            barrier,
            inc=1,
            device_id=(lat, lax.rem(m + d, plane) * 2 + zhi),
            device_id_type=MESH,
        )
        return carry

    lax.fori_loop(1, plane, greet, 0)
    pl.semaphore_wait(barrier, len(greeted) + plane - 1)

    def mirror_copy(rows_of):
        rows = pl.ds(rows_of * shard, shard)
        return pltpu.make_async_remote_copy(
            src_ref=wbuf.at[core, rows, :],
            dst_ref=wbuf.at[core, rows, :],
            send_sem=z_send,
            recv_sem=z_recv,
            device_id=(lat_mirror, lon_pair),
            device_id_type=MESH,
        )

    def plane_copy(rows_of, other, mark, send, recv):
        rows = pl.ds(rows_of * shard, shard)
        return pltpu.make_async_remote_copy(
            src_ref=wbuf.at[core, rows, :],
            dst_ref=wbuf.at[core, rows, :],
            send_sem=send,
            recv_sem=recv.at[mark],
            device_id=(lat, other * 2 + zhi),
            device_id_type=MESH,
        )

    def sibling_copy(half, owner):
        rows = pl.ds(owner * 2 * shard, 2 * shard)
        return pltpu.make_async_remote_copy(
            src_ref=wbuf.at[half, rows, :],
            dst_ref=wbuf.at[half, rows, :],
            send_sem=sib_send.at[owner],
            recv_sem=sib_recv.at[owner],
            device_id=(lat_sib, lon),
            device_id_type=MESH,
        )

    def sibling_pair_copy(half):
        rows = pl.ds(lon_pair * shard, shard)
        return pltpu.make_async_remote_copy(
            src_ref=wbuf.at[half, rows, :],
            dst_ref=wbuf.at[half, rows, :],
            send_sem=sib_send.at[m],
            recv_sem=sib_recv.at[m],
            device_id=(lat_sib, lon),
            device_id_type=MESH,
        )

    for k in range(3):
        loads[k].wait()
    mirror_copy(lon).start()

    def send_own(d, carry):
        plane_copy(lon, lax.rem(m + d, plane), m, own_send.at[d], own_recv).start()
        return carry

    lax.fori_loop(1, plane, send_own, 0)

    def leg_copy(side, k):
        rows = pl.ds((0, 32, 16)[k], 16)
        cols = pl.ds(COLS - 6, 6) if side == 0 else pl.ds(0, 6)
        return pltpu.make_async_remote_copy(
            src_ref=tok.at[cols, rows, :],
            dst_ref=relay.at[side, :, rows, :],
            send_sem=leg_send.at[side, k],
            recv_sem=leg_recv.at[side, k],
            device_id=(above, below)[side],
            device_id_type=MESH,
        )

    def halo_copy(side, k):
        rows = pl.ds((0, 32, 16)[k], 16)
        return pltpu.make_async_remote_copy(
            src_ref=relay.at[side, :, rows, :],
            dst_ref=halo.at[side, :, rows, :],
            send_sem=halo_send.at[side, k],
            recv_sem=halo_recv.at[side, k],
            device_id=onward[side],
            device_id_type=MESH,
        )

    def set_out(k):
        for side in range(2):
            leg_copy(side, k).start()

    def forward(k):
        for side in range(2):
            leg_copy(side, k).wait_recv()
            halo_copy(side, k).start()

    def label_copy(side):
        return pltpu.make_async_remote_copy(
            src_ref=lab_send.at[side],
            dst_ref=lab_recv.at[side],
            send_sem=lab_ssem.at[side],
            recv_sem=lab_rsem.at[side],
            device_id=(lat, lon_up if side == 0 else lon_dn),
            device_id_type=MESH,
        )

    loads[3].wait()
    lab_send[...] = jnp.zeros_like(lab_send)
    lab_send[0, 0:6, 0:ROWS] = lab_own[COLS - 6 : COLS, :]
    lab_send[1, 0:6, 0:ROWS] = lab_own[0:6, :]
    for side in range(2):
        label_copy(side).start()
    set_out(0)

    mirror_copy(lon_pair).wait_recv()

    def send_pair(d, carry):
        plane_copy(lon_pair, lax.rem(m + d, plane), m, par_send.at[d], par_recv).start()
        return carry

    lax.fori_loop(1, plane, send_pair, 0)
    sibling_pair_copy(core).start()

    loads[4].wait()
    loads[5].wait()
    loads[6].wait()

    def own_column(c, carry):
        x = xo[c].astype(F32)
        acc[c + 6] = x
        xn[c + 6, :, 0:C] = normed_rows(x, gain[...])
        return carry

    lax.fori_loop(0, COLS, own_column, 0)

    def place_rows(count):
        half, c, r = token_parts(lax.broadcasted_iota(I32, (count, WIN), 0))
        place = jnp.where(
            lax.broadcasted_iota(I32, (count, WIN), 0) < WIN, (half * 3 + r) * 12 + c, -1
        )
        return (lax.broadcasted_iota(I32, (count, WIN), 1) == place).astype(F32)

    def bias_of(h, carry):
        keys_first = dot_nt(place_rows(WIN), bias_raw[h], lax.Precision.HIGHEST)
        bias[h] = dot_nt(keys_first, place_rows(128), lax.Precision.HIGHEST) * LOG2E
        return carry

    lax.fori_loop(0, HEADS, bias_of, 0)
    ctx[...] = jnp.zeros_like(ctx)

    for side in range(2):
        label_copy(side).wait_recv()
    lab_ext[0:6, :] = lab_recv[0, 0:6, 0:ROWS]
    lab_ext[6 : 6 + COLS, :] = lab_own[...]
    lab_ext[6 + COLS : EXT, :] = lab_recv[1, 0:6, 0:ROWS]
    eye = (
        lax.broadcasted_iota(I32, (ROWS, ROWS), 0) == lax.broadcasted_iota(I32, (ROWS, ROWS), 1)
    ).astype(BF)
    low = ((lax.broadcasted_iota(I32, (ROWS, EXT), 0) < 3) & (lat == 0)).astype(F32)
    lab_t[...] = dot_nt(eye, lab_ext[...].astype(F32).astype(BF)) + 3.0 * low

    def features(e, carry):
        lane = lax.broadcasted_iota(I32, (ROWS, EXT), 1)
        code = jnp.sum(jnp.where(lane == e, lab_t[...], 0.0), axis=1, keepdims=True)
        wide = lax.broadcasted_iota(I32, (ROWS, FEAT), 1).astype(F32)
        xn[e, :, C:WIDE] = (wide == code).astype(F32)
        return carry

    lax.fori_loop(0, EXT, features, 0)
    set_out(1)
    forward(0)

    def start_and_offset(i):
        start = 8 * ((13 * i) // 16)
        return start, 3 + 6 * i - start

    def gather(i, j, u, w):
        start, offset = start_and_offset(i)
        start = pl.multiple_of(start, 8)
        block = xn[pl.ds(12 * j, 12), pl.ds(start, 16), :].reshape(192, WIDE).astype(BF)
        t = lax.broadcasted_iota(I32, (128, 192), 0)
        place = jnp.where(t < WIN, block_place(t), -1000) + offset
        select = (lax.broadcasted_iota(I32, (128, 192), 1) == place).astype(F32).astype(BF)
        xwin[u, 128 * w : 128 * w + 128, :] = dot(select, block).astype(BF)

    def gather_inner(i, carry):
        gather(i, 1, i, 0)
        gather(i, 2, i, 1)
        return carry

    lax.fori_loop(0, 7, gather_inner, 0)

    def pass_on(d, carry):
        source = lax.rem(m + d, plane)
        plane_copy(source * 2 + zhi, source, source, own_send.at[d], own_recv).wait_recv()
        plane_copy(source * 2 + 1 - zhi, source, source, par_send.at[d], par_recv).wait_recv()
        sibling_copy(core, source).start()
        return carry

    lax.fori_loop(1, plane, pass_on, 0)

    def await_sibling(d, carry):
        sibling_copy(1 - core, lax.rem(m + d, plane)).wait_recv()
        return carry

    sibling_pair_copy(1 - core).wait_recv()
    lax.fori_loop(1, plane, await_sibling, 0)
    set_out(2)
    forward(1)
    eye_c = (
        lax.broadcasted_iota(I32, (C, C), 0) == lax.broadcasted_iota(I32, (C, C), 1)
    ).astype(F32).astype(BF)
    wvt[...] = dot_nt(eye_c, wbuf[1, :, 0:512]).astype(BF)
    wpt[...] = dot_nt(eye_c, wbuf[1, :, 512:1024]).astype(BF)

    def halo_chunk(k):
        row = (0, 32, 16)[k]
        for side in range(2):
            halo_copy(side, k).wait_recv()

        def one(c, carry):
            for side in range(2):
                x = halo[side, c, row : row + 16, :].astype(F32)
                xn[c + side * (EXT - 6), row : row + 16, 0:C] = normed_rows(x, gain[...])
            return carry

        lax.fori_loop(0, 6, one, 0)

    def pack(row, offset):
        block = xn[:, row : row + 16, :].reshape(EXT * 16, WIDE).astype(BF)
        u = lax.broadcasted_iota(I32, (144, EXT * 16), 0)
        c = (u * 171) >> 9
        place = c * 16 + (u - 3 * c) + offset
        select = (lax.broadcasted_iota(I32, (144, EXT * 16), 1) == place).astype(F32).astype(BF)
        return dot(select, block).astype(BF)

    def lat_copy(up):
        if up:
            return pltpu.make_async_remote_copy(
                src_ref=pk_bot.at[0:144],
                dst_ref=pk_top.at[0:144],
                send_sem=lat_send.at[0],
                recv_sem=lat_recv.at[0],
                device_id=(lat_up, lon),
                device_id_type=MESH,
            )
        return pltpu.make_async_remote_copy(
            src_ref=pk_top.at[144:288],
            dst_ref=pk_bot.at[144:288],
            send_sem=lat_send.at[1],
            recv_sem=lat_recv.at[1],
            device_id=(lat_dn, lon),
            device_id_type=MESH,
        )

    def gather_edges():
        t = lax.broadcasted_iota(I32, (128, 288), 0)
        lane = lax.broadcasted_iota(I32, (128, 288), 1)
        place = jnp.where(t < WIN, t + 108 * (t >= 36).astype(I32), -1000)
        for j in range(4):
            select = (lane == place + 36 * j).astype(F32).astype(BF)
            for k, rows in enumerate((pk_top, pk_bot)):
                xwin[11 + 2 * k + j // 2, 128 * (j % 2) : 128 * (j % 2) + 128, :] = dot(
                    select, rows[...]
                ).astype(BF)

    lane128 = lax.broadcasted_iota(I32, (80, 128), 1)

    def attend(u):
        first = xwin[u, 0:80, :]
        second = xwin[u, 128:208, :]
        both = jnp.concatenate([first[:, 0:C], second[:, 0:C]], axis=0)
        qk[...] = dot(both, wbuf[0]).astype(BF)
        vt[...] = dot_nt(wvt[...], xwin[u, :, 0:C]).astype(BF)
        for w in range(2):
            hot = (first, second)[w][:, C:WIDE]
            differs = jnp.where(lane128 < 6, MASKED * (1.0 - hot.astype(F32)), 0.0).astype(BF)
            for g in range(4):
                query = qk[80 * w : 80 * w + 80, 128 * g : 128 * g + 128]
                key = qk[80 * w : 80 * w + 80, 512 + 128 * g : 640 + 128 * g]
                stacked = jnp.concatenate(
                    [
                        jnp.concatenate(
                            [
                                jnp.where(lane128 // HD == k, key, jnp.zeros_like(key)),
                                hot,
                            ],
                            axis=1,
                        )
                        for k in range(4)
                    ],
                    axis=0,
                )
                scores = dot_nt(stacked, jnp.concatenate([query, differs], axis=1))
                for k in range(4):
                    h = 4 * g + k
                    s = scores[80 * k : 80 * k + WIN] * SCALE + bias[h, :, 0:80]
                    e = jnp.exp2(s - jnp.max(s, axis=0, keepdims=True))
                    total = jnp.sum(e, axis=0, keepdims=True)
                    probs = jnp.concatenate([e, jnp.zeros((8, 80), F32)], axis=0).astype(BF)
                    part = dot(vt[HD * h : HD * h + HD, 128 * w : 128 * w + 80], probs)
                    ctx[HD * h : HD * h + HD, 128 * w : 128 * w + 80] = (part * (1.0 / total)).astype(BF)
        return dot(wpt[...], ctx[...]).astype(BF)

    def unit(u, carry):
        @pl.when(u == 2)
        def _():
            forward(2)

        @pl.when(u == 7)
        def _():
            halo_chunk(0)
            pk_top[144:288, :] = pack(0, 0)
            lat_copy(False).start()
            for n in range(2):
                gather(n, 0, 7 + n, 0)
                gather(n, 3, 7 + n, 1)

        @pl.when(u == 9)
        def _():
            halo_chunk(1)
            pk_bot[0:144, :] = pack(32, 13)
            lat_copy(True).start()
            for n in range(2):
                gather(5 + n, 0, 9 + n, 0)
                gather(5 + n, 3, 9 + n, 1)

        @pl.when(u == 11)
        def _():
            lat_copy(True).wait_recv()
            lat_copy(False).wait_recv()
            gather_edges()

        @pl.when(u == 15)
        def _():
            halo_chunk(2)
            for n in range(3):
                gather(2 + n, 0, 15 + n, 0)
                gather(2 + n, 3, 15 + n, 1)

        att = attend(u)
        inner = u < 7
        edge = (u >= 11) & (u < 15)
        top = edge & (u < 13)
        bottom = edge & (u >= 13)
        i = jnp.where(inner, u, jnp.where(u < 9, u - 7, jnp.where(u < 11, u - 4, u - 13)))
        start, offset = start_and_offset(i)
        start = jnp.where(edge, jnp.where(top, 0, 32), start)
        offset = jnp.where(edge, jnp.where(top, -3, 13), offset)
        least = jnp.where(top, 36, 0)
        most = jnp.where(bottom, 36, WIN)
        start = pl.multiple_of(start, 8)
        t = lax.broadcasted_iota(I32, (192, 80), 1)
        place = jnp.where((t >= least) & (t < most), block_place(t) + offset, -1000)
        select = (lax.broadcasted_iota(I32, (192, 80), 0) == place).astype(F32).astype(BF)
        for w in range(2):
            j = jnp.where(inner, 1 + w, jnp.where(edge, 2 * ((u - 11) % 2) + w, 3 * w))
            back = dot_nt(select, att[:, 128 * w : 128 * w + 80])
            spot = (pl.ds(12 * j, 12), pl.ds(start, 16), slice(None))
            acc[spot] = acc[spot] + back.reshape(12, 16, C)
        return carry

    lax.fori_loop(0, UNITS, unit, 0)

    def finish(c, carry):
        xo[c] = acc[c + 6].astype(BF)
        return carry

    lax.fori_loop(0, COLS, finish, 0)
    store = pltpu.make_async_copy(xo, out, out_sem)
    store.start()

    mirror_copy(lon).wait_send()

    def sent(d, carry):
        plane_copy(lon, lax.rem(m + d, plane), m, own_send.at[d], own_recv).wait_send()
        plane_copy(lon_pair, lax.rem(m + d, plane), m, par_send.at[d], par_recv).wait_send()
        return carry

    lax.fori_loop(1, plane, sent, 0)

    def sent_on(d, carry):
        sibling_copy(core, lax.rem(m + d, plane)).wait_send()
        return carry

    sibling_pair_copy(core).wait_send()
    lax.fori_loop(1, plane, sent_on, 0)
    for side in range(2):
        label_copy(side).wait_send()
        for k in range(3):
            leg_copy(side, k).wait_send()
            halo_copy(side, k).wait_send()
    lat_copy(True).wait_send()
    lat_copy(False).wait_send()
    store.wait()


def local(tokens, region, ln_gain, qkv_weight, proj_weight, position_bias):
    nlat = lax.axis_size("lat")
    nlon = lax.axis_size("lon")
    plane = nlon // 2
    dma = pltpu.SemaphoreType.DMA
    vm = pltpu.VMEM
    mixed = pl.pallas_call(
        functools.partial(kernel, nlat, nlon),
        out_shape=jax.ShapeDtypeStruct((COLS, ROWS, C), BF),
        in_specs=[pl.BlockSpec(memory_space=pl.ANY)] * 6,
        out_specs=pl.BlockSpec(memory_space=pl.ANY),
        scratch_shapes=[
            vm((COLS, ROWS, C), BF),
            vm((2, 6, ROWS, C), BF),
            vm((2, 6, ROWS, C), BF),
            vm((COLS, ROWS), I32),
            vm((2, 8, 128), I32),
            vm((2, 8, 128), I32),
            vm((EXT, ROWS), I32),
            vm((ROWS, EXT), F32),
            vm((1, C), F32),
            vm((HEADS, WIN, WIN), F32),
            vm((HEADS, WIN, 128), F32),
            vm((2, C, 1024), BF),
            vm((C, C), BF),
            vm((C, C), BF),
            vm((EXT, ROWS, WIDE), F32),
            vm((EXT, ROWS, C), F32),
            vm((UNITS, 256, WIDE), BF),
            vm((288, WIDE), BF),
            vm((288, WIDE), BF),
            vm((160, 1024), BF),
            vm((C, 256), BF),
            vm((C, 256), BF),
            dma((7,)),
            dma,
            dma,
            dma,
            dma((plane,)),
            dma((plane,)),
            dma((plane,)),
            dma((plane,)),
            dma((plane,)),
            dma((plane,)),
            dma((2, 3)),
            dma((2, 3)),
            dma((2, 3)),
            dma((2, 3)),
            dma((2,)),
            dma((2,)),
            dma((2,)),
            dma((2,)),
        ],
        compiler_params=pltpu.CompilerParams(
            collective_id=0, has_side_effects=True, vmem_limit_bytes=56 * 2**20
        ),
        cost_estimate=pl.CostEstimate(
            flops=8_000_000_000, bytes_accessed=12_000_000, transcendentals=6_000_000
        ),
    )(
        jnp.transpose(tokens, (1, 0, 2)),
        jnp.transpose(region, (1, 0)),
        ln_gain.reshape(1, C),
        qkv_weight,
        proj_weight,
        position_bias,
    )
    return jnp.transpose(mixed, (1, 0, 2))


def solution(mesh):
    return jax.shard_map(
        local,
        mesh=mesh,
        in_specs=(P("lat", "lon", None), P("lat", "lon"), P(), P("lon", None), P("lon", None), P()),
        out_specs=P("lat", "lon", None),
        check_vma=False,
    )
```

```python
import functools
import math

import jax
import jax.numpy as jnp
from jax import lax
from jax.experimental import pallas as pl
from jax.experimental.pallas import tpu as pltpu
from jax.sharding import PartitionSpec as P

HEADS = 16
HD = 32
C = 512
WIN = 72
ROWS = 48
COLS = 36
EXT = 48
FEAT = 128
WIDE = C + FEAT
LOG2E = math.log2(math.e)
SCALE = HD**-0.5 * LOG2E
MASKED = -1e30
UNITS = 18
BF = jnp.bfloat16
F32 = jnp.float32
I32 = jnp.int32
MESH = pl.DeviceIdType.MESH
NT = (((1,), (1,)), ((), ()))


def dot(a, b):
    return jnp.dot(a, b, preferred_element_type=F32)


def dot_nt(a, b, precision=None):
    return lax.dot_general(a, b, NT, preferred_element_type=F32, precision=precision)


def token_parts(t):
    half = (t >= 36).astype(I32)
    u = t - 36 * half
    c = (u * 43) >> 7
    return half, c, u - 3 * c


def block_place(t):
    half, c, r = token_parts(t)
    return c * 16 + half * 3 + r


def normed_rows(x, gain):
    mean = jnp.sum(x, axis=-1, keepdims=True) * (1.0 / C)
    d = x - mean
    var = jnp.sum(d * d, axis=-1, keepdims=True) * (1.0 / C)
    return (d * lax.rsqrt(var + 1e-05) * gain).astype(BF).astype(F32)


def kernel(
    nlat,
    nlon,
    tok,
    reg,
    gain_hbm,
    wqkv,
    wproj,
    bias_hbm,
    out,
    xo,
    halo,
    relay,
    lab_own,
    lab_send,
    lab_recv,
    lab_ext,
    lab_t,
    gain,
    bias_raw,
    bias,
    wbuf,
    wvt,
    wpt,
    xn,
    acc,
    xwin,
    pk_top,
    pk_bot,
    qk,
    vt,
    ctx,
    head_mask,
    place_in,
    place_out,
    loc_sem,
    out_sem,
    z_send,
    z_recv,
    own_send,
    own_recv,
    par_send,
    par_recv,
    sib_send,
    sib_recv,
    leg_send,
    leg_recv,
    halo_send,
    halo_recv,
    lab_ssem,
    lab_rsem,
    lat_send,
    lat_recv,
):
    shard = C // nlon
    plane = nlon // 2
    lat = lax.axis_index("lat")
    lon = lax.axis_index("lon")
    core = lax.rem(lat, 2)
    zhi = lax.rem(lon, 2)
    m = lon // 2
    lat_up = lax.rem(lat + 1, nlat)
    lat_dn = lax.rem(lat + nlat - 1, nlat)
    lon_up = lax.rem(lon + 1, nlon)
    lon_dn = lax.rem(lon + nlon - 1, nlon)
    lon_pair = lon + 1 - 2 * zhi
    lat_mirror = (nlat // 2 - 1 - lat // 2) * 2 + core
    lat_sib = lat + 1 - 2 * core

    zlo = nlat // 2
    ring = 2 * zlo
    leg = zlo // 2
    z = zhi * zlo + lat // 2

    def chip_at(column, place):
        place = lax.rem(place + 2 * ring, ring)
        return lax.rem(place, zlo) * 2 + core, column * 2 + place // zlo

    above = chip_at(m, z + leg)
    below = chip_at(m, z - leg)

    def beyond(place, by):
        lat_s, lon_s = chip_at(m, place)
        return lat_s, lax.rem(lon_s + by + nlon, nlon)

    onward = (beyond(z - leg, 1), beyond(z + leg, -1))
    relays_here = (
        chip_at(lon_dn // 2, lax.rem(lon_dn, 2) * zlo + lat // 2 + leg),
        chip_at(lon_up // 2, lax.rem(lon_up, 2) * zlo + lat // 2 - leg),
    )

    loads = [
        pltpu.make_async_copy(wqkv.at[:, 0:1024], wbuf.at[0, pl.ds(lon * shard, shard), :], loc_sem.at[0]),
        pltpu.make_async_copy(
            wqkv.at[:, 1024:1536], wbuf.at[1, pl.ds(lon * shard, shard), 0:512], loc_sem.at[1]
        ),
        pltpu.make_async_copy(wproj, wbuf.at[1, pl.ds(lon * shard, shard), 512:1024], loc_sem.at[2]),
        pltpu.make_async_copy(reg, lab_own, loc_sem.at[3]),
        pltpu.make_async_copy(tok, xo, loc_sem.at[4]),
        pltpu.make_async_copy(gain_hbm, gain, loc_sem.at[5]),
        pltpu.make_async_copy(bias_hbm, bias_raw, loc_sem.at[6]),
    ]
    for copy in loads:
        copy.start()

    barrier = pltpu.get_barrier_semaphore()
    greeted = (
        (lat, lon_up),
        (lat, lon_dn),
        (lat_up, lon),
        (lat_dn, lon),
        (lat_mirror, lon_pair),
        above,
        below,
    )
    greeted = greeted + relays_here
    for there in greeted:
        pl.semaphore_signal(barrier, inc=1, device_id=there, device_id_type=MESH)

    def greet(d, carry):
        pl.semaphore_signal(
            barrier,
            inc=1,
            device_id=(lat, lax.rem(m + d, plane) * 2 + zhi),
            device_id_type=MESH,
        )
        return carry

    lax.fori_loop(1, plane, greet, 0)
    pl.semaphore_wait(barrier, len(greeted) + plane - 1)

    def mirror_copy(rows_of):
        rows = pl.ds(rows_of * shard, shard)
        return pltpu.make_async_remote_copy(
            src_ref=wbuf.at[core, rows, :],
            dst_ref=wbuf.at[core, rows, :],
            send_sem=z_send,
            recv_sem=z_recv,
            device_id=(lat_mirror, lon_pair),
            device_id_type=MESH,
        )

    def plane_copy(rows_of, other, mark, send, recv):
        rows = pl.ds(rows_of * shard, shard)
        return pltpu.make_async_remote_copy(
            src_ref=wbuf.at[core, rows, :],
            dst_ref=wbuf.at[core, rows, :],
            send_sem=send,
            recv_sem=recv.at[mark],
            device_id=(lat, other * 2 + zhi),
            device_id_type=MESH,
        )

    def sibling_copy(half, owner):
        rows = pl.ds(owner * 2 * shard, 2 * shard)
        return pltpu.make_async_remote_copy(
            src_ref=wbuf.at[half, rows, :],
            dst_ref=wbuf.at[half, rows, :],
            send_sem=sib_send.at[owner],
            recv_sem=sib_recv.at[owner],
            device_id=(lat_sib, lon),
            device_id_type=MESH,
        )

    def sibling_pair_copy(half):
        rows = pl.ds(lon_pair * shard, shard)
        return pltpu.make_async_remote_copy(
            src_ref=wbuf.at[half, rows, :],
            dst_ref=wbuf.at[half, rows, :],
            send_sem=sib_send.at[m],
            recv_sem=sib_recv.at[m],
            device_id=(lat_sib, lon),
            device_id_type=MESH,
        )

    for k in range(3):
        loads[k].wait()
    mirror_copy(lon).start()

    def send_own(d, carry):
        plane_copy(lon, lax.rem(m + d, plane), m, own_send.at[d], own_recv).start()
        return carry

    lax.fori_loop(1, plane, send_own, 0)

    def leg_copy(side, k):
        rows = pl.ds((0, 32, 16)[k], 16)
        cols = pl.ds(COLS - 6, 6) if side == 0 else pl.ds(0, 6)
        return pltpu.make_async_remote_copy(
            src_ref=tok.at[cols, rows, :],
            dst_ref=relay.at[side, :, rows, :],
            send_sem=leg_send.at[side, k],
            recv_sem=leg_recv.at[side, k],
            device_id=(above, below)[side],
            device_id_type=MESH,
        )

    def halo_copy(side, k):
        rows = pl.ds((0, 32, 16)[k], 16)
        return pltpu.make_async_remote_copy(
            src_ref=relay.at[side, :, rows, :],
            dst_ref=halo.at[side, :, rows, :],
            send_sem=halo_send.at[side, k],
            recv_sem=halo_recv.at[side, k],
            device_id=onward[side],
            device_id_type=MESH,
        )

    def set_out(k):
        for side in range(2):
            leg_copy(side, k).start()

    def forward(k):
        for side in range(2):
            leg_copy(side, k).wait_recv()
            halo_copy(side, k).start()

    def label_copy(side):
        return pltpu.make_async_remote_copy(
            src_ref=lab_send.at[side],
            dst_ref=lab_recv.at[side],
            send_sem=lab_ssem.at[side],
            recv_sem=lab_rsem.at[side],
            device_id=(lat, lon_up if side == 0 else lon_dn),
            device_id_type=MESH,
        )

    loads[3].wait()
    lab_send[...] = jnp.zeros_like(lab_send)
    lab_send[0, 0:6, 0:ROWS] = lab_own[COLS - 6 : COLS, :]
    lab_send[1, 0:6, 0:ROWS] = lab_own[0:6, :]
    for side in range(2):
        label_copy(side).start()
    set_out(0)

    mirror_copy(lon_pair).wait_recv()

    def send_pair(d, carry):
        plane_copy(lon_pair, lax.rem(m + d, plane), m, par_send.at[d], par_recv).start()
        return carry

    lax.fori_loop(1, plane, send_pair, 0)
    sibling_pair_copy(core).start()

    lane80 = lax.broadcasted_iota(I32, (80, 128), 1)
    for k in range(4):
        head_mask[k] = ((lane80 >= HD * k) & (lane80 < HD * k + HD)).astype(F32).astype(BF)
    t_in = lax.broadcasted_iota(I32, (128, 192), 0)
    place_in[...] = jnp.where(t_in < WIN, block_place(t_in), -1000)
    t_out = lax.broadcasted_iota(I32, (192, 80), 1)
    for k, (least, most) in enumerate(((0, WIN), (36, WIN), (0, 36))):
        place_out[k] = jnp.where((t_out >= least) & (t_out < most), block_place(t_out), -1000)

    loads[4].wait()
    loads[5].wait()
    loads[6].wait()

    def own_column(c, carry):
        x = xo[c].astype(F32)
        acc[c + 6] = x
        xn[c + 6, :, 0:C] = normed_rows(x, gain[...])
        return carry

    lax.fori_loop(0, COLS, own_column, 0, unroll=2)
    set_out(1)

    def pass_on(d, carry):
        source = lax.rem(m + d, plane)
        plane_copy(source * 2 + zhi, source, source, own_send.at[d], own_recv).wait_recv()
        plane_copy(source * 2 + 1 - zhi, source, source, par_send.at[d], par_recv).wait_recv()
        sibling_copy(core, source).start()
        return carry

    lax.fori_loop(1, plane // 2, pass_on, 0)
    forward(0)

    def place_rows(count):
        half, c, r = token_parts(lax.broadcasted_iota(I32, (count, WIN), 0))
        place = jnp.where(
            lax.broadcasted_iota(I32, (count, WIN), 0) < WIN, (half * 3 + r) * 12 + c, -1
        )
        return (lax.broadcasted_iota(I32, (count, WIN), 1) == place).astype(F32)

    def bias_of(h, carry):
        keys_first = dot_nt(place_rows(WIN), bias_raw[h], lax.Precision.HIGHEST)
        bias[h] = dot_nt(keys_first, place_rows(128), lax.Precision.HIGHEST) * LOG2E
        return carry

    lax.fori_loop(0, HEADS, bias_of, 0, unroll=4)
    lax.fori_loop(plane // 2, plane, pass_on, 0)
    set_out(2)
    forward(1)
    ctx[...] = jnp.zeros_like(ctx)

    for side in range(2):
        label_copy(side).wait_recv()
    lab_ext[0:6, :] = lab_recv[0, 0:6, 0:ROWS]
    lab_ext[6 : 6 + COLS, :] = lab_own[...]
    lab_ext[6 + COLS : EXT, :] = lab_recv[1, 0:6, 0:ROWS]
    eye = (
        lax.broadcasted_iota(I32, (ROWS, ROWS), 0) == lax.broadcasted_iota(I32, (ROWS, ROWS), 1)
    ).astype(BF)
    low = ((lax.broadcasted_iota(I32, (ROWS, EXT), 0) < 3) & (lat == 0)).astype(F32)
    lab_t[...] = dot_nt(eye, lab_ext[...].astype(F32).astype(BF)) + 3.0 * low

    def features(e, carry):
        lane = lax.broadcasted_iota(I32, (ROWS, EXT), 1)
        code = jnp.sum(jnp.where(lane == e, lab_t[...], 0.0), axis=1, keepdims=True)
        wide = lax.broadcasted_iota(I32, (ROWS, FEAT), 1).astype(F32)
        xn[e, :, C:WIDE] = (wide == code).astype(F32)
        return carry

    lax.fori_loop(0, EXT, features, 0, unroll=4)

    def start_and_offset(i):
        start = 8 * ((13 * i) // 16)
        return start, 3 + 6 * i - start

    lane_in = lax.broadcasted_iota(I32, (128, 192), 1)

    def gather_pair(i, first, second, u):
        start, offset = start_and_offset(i)
        if not isinstance(i, int):
            start = pl.multiple_of(start, 8)
        select = (lane_in - offset == place_in[...]).astype(F32).astype(BF)
        for w, j in enumerate((first, second)):
            block = xn[12 * j : 12 * j + 12, pl.ds(start, 16), :].reshape(192, WIDE).astype(BF)
            xwin[u, 128 * w : 128 * w + 128, :] = dot(select, block).astype(BF)

    def gather_inner(i, carry):
        gather_pair(i, 1, 2, i)
        return carry

    lax.fori_loop(0, 7, gather_inner, 0)

    def await_sibling(d, carry):
        sibling_copy(1 - core, lax.rem(m + d, plane)).wait_recv()
        return carry

    sibling_pair_copy(1 - core).wait_recv()
    lax.fori_loop(1, plane, await_sibling, 0)
    eye_c = (
        lax.broadcasted_iota(I32, (C, C), 0) == lax.broadcasted_iota(I32, (C, C), 1)
    ).astype(F32).astype(BF)
    wvt[...] = dot_nt(eye_c, wbuf[1, :, 0:512]).astype(BF)
    wpt[...] = dot_nt(eye_c, wbuf[1, :, 512:1024]).astype(BF)

    def halo_chunk(k):
        row = (0, 32, 16)[k]
        for side in range(2):
            halo_copy(side, k).wait_recv()

        def one(c, carry):
            for side in range(2):
                x = halo[side, c, row : row + 16, :].astype(F32)
                xn[c + side * (EXT - 6), row : row + 16, 0:C] = normed_rows(x, gain[...])
            return carry

        lax.fori_loop(0, 6, one, 0)

    def pack(row, offset):
        block = xn[:, row : row + 16, :].reshape(EXT * 16, WIDE).astype(BF)
        u = lax.broadcasted_iota(I32, (144, EXT * 16), 0)
        c = (u * 171) >> 9
        place = c * 16 + (u - 3 * c) + offset
        select = (lax.broadcasted_iota(I32, (144, EXT * 16), 1) == place).astype(F32).astype(BF)
        return dot(select, block).astype(BF)

    def lat_copy(up):
        if up:
            return pltpu.make_async_remote_copy(
                src_ref=pk_bot.at[0:144],
                dst_ref=pk_top.at[0:144],
                send_sem=lat_send.at[0],
                recv_sem=lat_recv.at[0],
                device_id=(lat_up, lon),
                device_id_type=MESH,
            )
        return pltpu.make_async_remote_copy(
            src_ref=pk_top.at[144:288],
            dst_ref=pk_bot.at[144:288],
            send_sem=lat_send.at[1],
            recv_sem=lat_recv.at[1],
            device_id=(lat_dn, lon),
            device_id_type=MESH,
        )

    def gather_edges():
        t = lax.broadcasted_iota(I32, (128, 288), 0)
        lane = lax.broadcasted_iota(I32, (128, 288), 1)
        place = jnp.where(t < WIN, t + 108 * (t >= 36).astype(I32), -1000)
        for j in range(4):
            select = (lane == place + 36 * j).astype(F32).astype(BF)
            for k, rows in enumerate((pk_top, pk_bot)):
                xwin[11 + 2 * k + j // 2, 128 * (j % 2) : 128 * (j % 2) + 128, :] = dot(
                    select, rows[...]
                ).astype(BF)

    lane128 = lax.broadcasted_iota(I32, (80, 128), 1)

    def attend(u):
        first = xwin[u, 0:80, :]
        second = xwin[u, 128:208, :]
        both = jnp.concatenate([first[:, 0:C], second[:, 0:C]], axis=0)
        qk[...] = dot(both, wbuf[0]).astype(BF)
        vt[...] = dot_nt(wvt[...], xwin[u, :, 0:C]).astype(BF)
        for w in range(2):
            hot = (first, second)[w][:, C:WIDE]
            differs = jnp.where(lane128 < 6, MASKED * (1.0 - hot.astype(F32)), 0.0).astype(BF)
            for g in range(4):
                query = qk[80 * w : 80 * w + 80, 128 * g : 128 * g + 128]
                key = qk[80 * w : 80 * w + 80, 512 + 128 * g : 640 + 128 * g]
                stacked = jnp.concatenate(
                    [
                        jnp.concatenate(
                            [
                                key * head_mask[k],
                                hot,
                            ],
                            axis=1,
                        )
                        for k in range(4)
                    ],
                    axis=0,
                )
                scores = dot_nt(stacked, jnp.concatenate([query, differs], axis=1))
                for k in range(4):
                    h = 4 * g + k
                    s = scores[80 * k : 80 * k + WIN] * SCALE + bias[h, :, 0:80]
                    e = jnp.exp2(s - jnp.max(s, axis=0, keepdims=True))
                    total = jnp.sum(e, axis=0, keepdims=True)
                    probs = jnp.concatenate([e, jnp.zeros((8, 80), F32)], axis=0).astype(BF)
                    part = dot(vt[HD * h : HD * h + HD, 128 * w : 128 * w + 80], probs)
                    ctx[HD * h : HD * h + HD, 128 * w : 128 * w + 80] = (part * (1.0 / total)).astype(BF)
        return dot(wpt[...], ctx[...]).astype(BF)

    def unit(u, carry):
        @pl.when(u == 1)
        def _():
            forward(2)

        @pl.when(u == 7)
        def _():
            halo_chunk(0)
            pk_top[144:288, :] = pack(0, 0)
            lat_copy(False).start()
            for n in range(2):
                gather_pair(n, 0, 3, 7 + n)

        @pl.when(u == 9)
        def _():
            halo_chunk(1)
            pk_bot[0:144, :] = pack(32, 13)
            lat_copy(True).start()
            for n in range(2):
                gather_pair(5 + n, 0, 3, 9 + n)

        @pl.when(u == 11)
        def _():
            lat_copy(True).wait_recv()
            lat_copy(False).wait_recv()
            gather_edges()

        @pl.when(u == 15)
        def _():
            halo_chunk(2)
            for n in range(3):
                gather_pair(2 + n, 0, 3, 15 + n)

        att = attend(u)
        inner = u < 7
        edge = (u >= 11) & (u < 15)
        top = edge & (u < 13)
        bottom = edge & (u >= 13)
        i = jnp.where(inner, u, jnp.where(u < 9, u - 7, jnp.where(u < 11, u - 4, u - 13)))
        start, offset = start_and_offset(i)
        start = jnp.where(edge, jnp.where(top, 0, 32), start)
        offset = jnp.where(edge, jnp.where(top, -3, 13), offset)
        kind = jnp.where(top, 1, jnp.where(bottom, 2, 0))
        start = pl.multiple_of(start, 8)
        row = lax.broadcasted_iota(I32, (192, 80), 0)
        select = (row - offset == place_out[kind]).astype(F32).astype(BF)
        for w in range(2):
            j = jnp.where(inner, 1 + w, jnp.where(edge, 2 * ((u - 11) % 2) + w, 3 * w))
            back = dot_nt(select, att[:, 128 * w : 128 * w + 80])
            spot = (pl.ds(12 * j, 12), pl.ds(start, 16), slice(None))
            acc[spot] = acc[spot] + back.reshape(12, 16, C)
        return carry

    lax.fori_loop(0, UNITS, unit, 0)

    def finish(c, carry):
        xo[c] = acc[c + 6].astype(BF)
        return carry

    def store(k):
        part = pl.ds(9 * k, 9)
        return pltpu.make_async_copy(xo.at[part], out.at[part], out_sem.at[k])

    for k in range(4):
        lax.fori_loop(9 * k, 9 * k + 9, finish, 0, unroll=3)
        store(k).start()

    mirror_copy(lon).wait_send()

    def sent(d, carry):
        plane_copy(lon, lax.rem(m + d, plane), m, own_send.at[d], own_recv).wait_send()
        plane_copy(lon_pair, lax.rem(m + d, plane), m, par_send.at[d], par_recv).wait_send()
        return carry

    lax.fori_loop(1, plane, sent, 0)

    def sent_on(d, carry):
        sibling_copy(core, lax.rem(m + d, plane)).wait_send()
        return carry

    sibling_pair_copy(core).wait_send()
    lax.fori_loop(1, plane, sent_on, 0)
    for side in range(2):
        label_copy(side).wait_send()
        for k in range(3):
            leg_copy(side, k).wait_send()
            halo_copy(side, k).wait_send()
    lat_copy(True).wait_send()
    lat_copy(False).wait_send()
    for k in range(4):
        store(k).wait()


def local(tokens, region, ln_gain, qkv_weight, proj_weight, position_bias):
    nlat = lax.axis_size("lat")
    nlon = lax.axis_size("lon")
    plane = nlon // 2
    dma = pltpu.SemaphoreType.DMA
    vm = pltpu.VMEM
    mixed = pl.pallas_call(
        functools.partial(kernel, nlat, nlon),
        out_shape=jax.ShapeDtypeStruct((COLS, ROWS, C), BF),
        in_specs=[pl.BlockSpec(memory_space=pl.ANY)] * 6,
        out_specs=pl.BlockSpec(memory_space=pl.ANY),
        scratch_shapes=[
            vm((COLS, ROWS, C), BF),
            vm((2, 6, ROWS, C), BF),
            vm((2, 6, ROWS, C), BF),
            vm((COLS, ROWS), I32),
            vm((2, 8, 128), I32),
            vm((2, 8, 128), I32),
            vm((EXT, ROWS), I32),
            vm((ROWS, EXT), F32),
            vm((1, C), F32),
            vm((HEADS, WIN, WIN), F32),
            vm((HEADS, WIN, 128), F32),
            vm((2, C, 1024), BF),
            vm((C, C), BF),
            vm((C, C), BF),
            vm((EXT, ROWS, WIDE), F32),
            vm((EXT, ROWS, C), F32),
            vm((UNITS, 256, WIDE), BF),
            vm((288, WIDE), BF),
            vm((288, WIDE), BF),
            vm((160, 1024), BF),
            vm((C, 256), BF),
            vm((C, 256), BF),
            vm((4, 80, 128), BF),
            vm((128, 192), I32),
            vm((3, 192, 80), I32),
            dma((7,)),
            dma((4,)),
            dma,
            dma,
            dma((plane,)),
            dma((plane,)),
            dma((plane,)),
            dma((plane,)),
            dma((plane,)),
            dma((plane,)),
            dma((2, 3)),
            dma((2, 3)),
            dma((2, 3)),
            dma((2, 3)),
            dma((2,)),
            dma((2,)),
            dma((2,)),
            dma((2,)),
        ],
        compiler_params=pltpu.CompilerParams(
            collective_id=0, has_side_effects=True, vmem_limit_bytes=56 * 2**20
        ),
        cost_estimate=pl.CostEstimate(
            flops=8_000_000_000, bytes_accessed=12_000_000, transcendentals=6_000_000
        ),
    )(
        jnp.transpose(tokens, (1, 0, 2)),
        jnp.transpose(region, (1, 0)),
        ln_gain.reshape(1, C),
        qkv_weight,
        proj_weight,
        position_bias,
    )
    return jnp.transpose(mixed, (1, 0, 2))


def solution(mesh):
    return jax.shard_map(
        local,
        mesh=mesh,
        in_specs=(P("lat", "lon", None), P("lat", "lon"), P(), P("lon", None), P("lon", None), P()),
        out_specs=P("lat", "lon", None),
        check_vma=False,
    )
```

```python
import functools
import math

import jax
import jax.numpy as jnp
from jax import lax
from jax.experimental import pallas as pl
from jax.experimental.pallas import tpu as pltpu
from jax.sharding import PartitionSpec as P

HEADS = 16
HD = 32
C = 512
WIN = 72
ROWS = 48
COLS = 36
EXT = 48
FEAT = 128
WIDE = C + FEAT
LOG2E = math.log2(math.e)
SCALE = HD**-0.5 * LOG2E
MASKED = -1e30
UNITS = 18
BF = jnp.bfloat16
F32 = jnp.float32
I32 = jnp.int32
MESH = pl.DeviceIdType.MESH
NT = (((1,), (1,)), ((), ()))
TN = (((0,), (0,)), ((), ()))


def dot(a, b):
    return jnp.dot(a, b, preferred_element_type=F32)


def dot_nt(a, b, precision=None):
    return lax.dot_general(a, b, NT, preferred_element_type=F32, precision=precision)


def token_parts(t):
    half = (t >= 36).astype(I32)
    u = t - 36 * half
    c = (u * 43) >> 7
    return half, c, u - 3 * c


def block_place(t):
    half, c, r = token_parts(t)
    return c * 16 + half * 3 + r


def normed_rows(x, gain):
    mean = jnp.sum(x, axis=-1, keepdims=True) * (1.0 / C)
    d = x - mean
    var = jnp.sum(d * d, axis=-1, keepdims=True) * (1.0 / C)
    return (d * lax.rsqrt(var + 1e-05) * gain).astype(BF).astype(F32)


def kernel(
    nlat,
    nlon,
    tok,
    reg,
    gain_hbm,
    wqkv,
    wproj,
    bias_hbm,
    out,
    xo,
    halo,
    relay,
    lab_own,
    lab_send,
    lab_recv,
    lab_ext,
    lab_t,
    gain,
    bias_raw,
    bias,
    wbuf,
    xn,
    acc,
    xwin,
    pk_top,
    pk_bot,
    qkv,
    ctx,
    head_mask,
    place_in,
    place_out,
    loc_sem,
    out_sem,
    z_send,
    z_recv,
    own_send,
    own_recv,
    par_send,
    par_recv,
    sib_send,
    sib_recv,
    leg_send,
    leg_recv,
    halo_send,
    halo_recv,
    lab_ssem,
    lab_rsem,
    lat_send,
    lat_recv,
):
    shard = C // nlon
    plane = nlon // 2
    lat = lax.axis_index("lat")
    lon = lax.axis_index("lon")
    core = lax.rem(lat, 2)
    zhi = lax.rem(lon, 2)
    m = lon // 2
    lat_up = lax.rem(lat + 1, nlat)
    lat_dn = lax.rem(lat + nlat - 1, nlat)
    lon_up = lax.rem(lon + 1, nlon)
    lon_dn = lax.rem(lon + nlon - 1, nlon)
    lon_pair = lon + 1 - 2 * zhi
    lat_mirror = (nlat // 2 - 1 - lat // 2) * 2 + core
    lat_sib = lat + 1 - 2 * core

    zlo = nlat // 2
    ring = 2 * zlo
    leg = zlo // 2
    z = zhi * zlo + lat // 2

    def chip_at(column, place):
        place = lax.rem(place + 2 * ring, ring)
        return lax.rem(place, zlo) * 2 + core, column * 2 + place // zlo

    above = chip_at(m, z + leg)
    below = chip_at(m, z - leg)

    def beyond(place, by):
        lat_s, lon_s = chip_at(m, place)
        return lat_s, lax.rem(lon_s + by + nlon, nlon)

    onward = (beyond(z - leg, 1), beyond(z + leg, -1))
    relays_here = (
        chip_at(lon_dn // 2, lax.rem(lon_dn, 2) * zlo + lat // 2 + leg),
        chip_at(lon_up // 2, lax.rem(lon_up, 2) * zlo + lat // 2 - leg),
    )

    loads = [
        pltpu.make_async_copy(wqkv.at[:, 0:1024], wbuf.at[0, pl.ds(lon * shard, shard), :], loc_sem.at[0]),
        pltpu.make_async_copy(
            wqkv.at[:, 1024:1536], wbuf.at[1, pl.ds(lon * shard, shard), 0:512], loc_sem.at[1]
        ),
        pltpu.make_async_copy(wproj, wbuf.at[1, pl.ds(lon * shard, shard), 512:1024], loc_sem.at[2]),
        pltpu.make_async_copy(reg, lab_own, loc_sem.at[3]),
        pltpu.make_async_copy(tok, xo, loc_sem.at[4]),
        pltpu.make_async_copy(gain_hbm, gain, loc_sem.at[5]),
        pltpu.make_async_copy(bias_hbm, bias_raw, loc_sem.at[6]),
    ]
    for copy in loads:
        copy.start()

    barrier = pltpu.get_barrier_semaphore()
    greeted = (
        (lat, lon_up),
        (lat, lon_dn),
        (lat_up, lon),
        (lat_dn, lon),
        (lat_mirror, lon_pair),
        above,
        below,
    )
    greeted = greeted + relays_here
    for there in greeted:
        pl.semaphore_signal(barrier, inc=1, device_id=there, device_id_type=MESH)

    def greet(d, carry):
        pl.semaphore_signal(
            barrier,
            inc=1,
            device_id=(lat, lax.rem(m + d, plane) * 2 + zhi),
            device_id_type=MESH,
        )
        return carry

    lax.fori_loop(1, plane, greet, 0)
    pl.semaphore_wait(barrier, len(greeted) + plane - 1)

    def mirror_copy(rows_of):
        rows = pl.ds(rows_of * shard, shard)
        return pltpu.make_async_remote_copy(
            src_ref=wbuf.at[core, rows, :],
            dst_ref=wbuf.at[core, rows, :],
            send_sem=z_send,
            recv_sem=z_recv,
            device_id=(lat_mirror, lon_pair),
            device_id_type=MESH,
        )

    def plane_copy(rows_of, other, mark, send, recv):
        rows = pl.ds(rows_of * shard, shard)
        return pltpu.make_async_remote_copy(
            src_ref=wbuf.at[core, rows, :],
            dst_ref=wbuf.at[core, rows, :],
            send_sem=send,
            recv_sem=recv.at[mark],
            device_id=(lat, other * 2 + zhi),
            device_id_type=MESH,
        )

    def sibling_copy(half, owner):
        rows = pl.ds(owner * 2 * shard, 2 * shard)
        return pltpu.make_async_remote_copy(
            src_ref=wbuf.at[half, rows, :],
            dst_ref=wbuf.at[half, rows, :],
            send_sem=sib_send.at[owner],
            recv_sem=sib_recv.at[owner],
            device_id=(lat_sib, lon),
            device_id_type=MESH,
        )

    def sibling_pair_copy(half):
        rows = pl.ds(lon_pair * shard, shard)
        return pltpu.make_async_remote_copy(
            src_ref=wbuf.at[half, rows, :],
            dst_ref=wbuf.at[half, rows, :],
            send_sem=sib_send.at[m],
            recv_sem=sib_recv.at[m],
            device_id=(lat_sib, lon),
            device_id_type=MESH,
        )

    for k in range(3):
        loads[k].wait()
    mirror_copy(lon).start()

    def send_own(d, carry):
        plane_copy(lon, lax.rem(m + d, plane), m, own_send.at[d], own_recv).start()
        return carry

    lax.fori_loop(1, plane, send_own, 0)

    def leg_copy(side, k):
        rows = pl.ds((0, 32, 16)[k], 16)
        cols = pl.ds(COLS - 6, 6) if side == 0 else pl.ds(0, 6)
        return pltpu.make_async_remote_copy(
            src_ref=tok.at[cols, rows, :],
            dst_ref=relay.at[side, :, rows, :],
            send_sem=leg_send.at[side, k],
            recv_sem=leg_recv.at[side, k],
            device_id=(above, below)[side],
            device_id_type=MESH,
        )

    def halo_copy(side, k):
        rows = pl.ds((0, 32, 16)[k], 16)
        return pltpu.make_async_remote_copy(
            src_ref=relay.at[side, :, rows, :],
            dst_ref=halo.at[side, :, rows, :],
            send_sem=halo_send.at[side, k],
            recv_sem=halo_recv.at[side, k],
            device_id=onward[side],
            device_id_type=MESH,
        )

    def set_out(k):
        for side in range(2):
            leg_copy(side, k).start()

    def forward(k):
        for side in range(2):
            leg_copy(side, k).wait_recv()
            halo_copy(side, k).start()

    def label_copy(side):
        return pltpu.make_async_remote_copy(
            src_ref=lab_send.at[side],
            dst_ref=lab_recv.at[side],
            send_sem=lab_ssem.at[side],
            recv_sem=lab_rsem.at[side],
            device_id=(lat, lon_up if side == 0 else lon_dn),
            device_id_type=MESH,
        )

    loads[3].wait()
    lab_send[...] = jnp.zeros_like(lab_send)
    lab_send[0, 0:6, 0:ROWS] = lab_own[COLS - 6 : COLS, :]
    lab_send[1, 0:6, 0:ROWS] = lab_own[0:6, :]
    for side in range(2):
        label_copy(side).start()
    set_out(0)

    mirror_copy(lon_pair).wait_recv()

    def send_pair(d, carry):
        plane_copy(lon_pair, lax.rem(m + d, plane), m, par_send.at[d], par_recv).start()
        return carry

    lax.fori_loop(1, plane, send_pair, 0)
    sibling_pair_copy(core).start()

    lane80 = lax.broadcasted_iota(I32, (80, 128), 1)
    for k in range(4):
        head_mask[k] = ((lane80 >= HD * k) & (lane80 < HD * k + HD)).astype(F32).astype(BF)
    t_in = lax.broadcasted_iota(I32, (80, 192), 0)
    place_in[...] = jnp.where(t_in < WIN, block_place(t_in), -1000)
    t_out = lax.broadcasted_iota(I32, (192, 80), 1)
    for k, (least, most) in enumerate(((0, WIN), (36, WIN), (0, 36))):
        place_out[k] = jnp.where((t_out >= least) & (t_out < most), block_place(t_out), -1000)

    loads[4].wait()
    loads[5].wait()
    loads[6].wait()

    def own_column(c, carry):
        x = xo[c].astype(F32)
        acc[c + 6] = x
        xn[c + 6, :, 0:C] = normed_rows(x, gain[...])
        return carry

    lax.fori_loop(0, COLS, own_column, 0, unroll=2)
    set_out(1)

    def pass_on(d, carry):
        source = lax.rem(m + d, plane)
        plane_copy(source * 2 + zhi, source, source, own_send.at[d], own_recv).wait_recv()
        plane_copy(source * 2 + 1 - zhi, source, source, par_send.at[d], par_recv).wait_recv()
        sibling_copy(core, source).start()
        return carry

    lax.fori_loop(1, plane // 2, pass_on, 0)
    forward(0)

    def place_rows(count):
        half, c, r = token_parts(lax.broadcasted_iota(I32, (count, WIN), 0))
        place = jnp.where(
            lax.broadcasted_iota(I32, (count, WIN), 0) < WIN, (half * 3 + r) * 12 + c, -1
        )
        return (lax.broadcasted_iota(I32, (count, WIN), 1) == place).astype(F32)

    padded = lax.broadcasted_iota(I32, (80, 128), 0) >= WIN

    def bias_of(h, carry):
        keys_first = dot_nt(place_rows(80), bias_raw[h], lax.Precision.HIGHEST)
        placed = dot_nt(keys_first, place_rows(128), lax.Precision.HIGHEST)
        bias[h] = jnp.where(padded, MASKED, placed * LOG2E)
        return carry

    lax.fori_loop(0, HEADS, bias_of, 0, unroll=4)
    lax.fori_loop(plane // 2, plane, pass_on, 0)
    set_out(2)
    forward(1)

    for side in range(2):
        label_copy(side).wait_recv()
    lab_ext[0:6, :] = lab_recv[0, 0:6, 0:ROWS]
    lab_ext[6 : 6 + COLS, :] = lab_own[...]
    lab_ext[6 + COLS : EXT, :] = lab_recv[1, 0:6, 0:ROWS]
    eye = (
        lax.broadcasted_iota(I32, (ROWS, ROWS), 0) == lax.broadcasted_iota(I32, (ROWS, ROWS), 1)
    ).astype(BF)
    low = ((lax.broadcasted_iota(I32, (ROWS, EXT), 0) < 3) & (lat == 0)).astype(F32)
    lab_t[...] = dot_nt(eye, lab_ext[...].astype(F32).astype(BF)) + 3.0 * low

    def features(e, carry):
        lane = lax.broadcasted_iota(I32, (ROWS, EXT), 1)
        code = jnp.sum(jnp.where(lane == e, lab_t[...], 0.0), axis=1, keepdims=True)
        wide = lax.broadcasted_iota(I32, (ROWS, FEAT), 1).astype(F32)
        xn[e, :, C:WIDE] = (wide == code).astype(F32)
        return carry

    lax.fori_loop(0, EXT, features, 0, unroll=4)

    def start_and_offset(i):
        start = 8 * ((13 * i) // 16)
        return start, 3 + 6 * i - start

    lane_in = lax.broadcasted_iota(I32, (80, 192), 1)

    def gather_pair(i, first, second, u):
        start, offset = start_and_offset(i)
        if not isinstance(i, int):
            start = pl.multiple_of(start, 8)
        select = (lane_in - offset == place_in[...]).astype(F32).astype(BF)
        for w, j in enumerate((first, second)):
            block = xn[12 * j : 12 * j + 12, pl.ds(start, 16), :].reshape(192, WIDE).astype(BF)
            xwin[u, 80 * w : 80 * w + 80, :] = dot(select, block).astype(BF)

    def gather_inner(i, carry):
        gather_pair(i, 1, 2, i)
        return carry

    lax.fori_loop(0, 7, gather_inner, 0)

    def await_sibling(d, carry):
        sibling_copy(1 - core, lax.rem(m + d, plane)).wait_recv()
        return carry

    sibling_pair_copy(1 - core).wait_recv()
    lax.fori_loop(1, plane, await_sibling, 0)
    def halo_chunk(k):
        row = (0, 32, 16)[k]
        for side in range(2):
            halo_copy(side, k).wait_recv()

        def one(c, carry):
            for side in range(2):
                x = halo[side, c, row : row + 16, :].astype(F32)
                xn[c + side * (EXT - 6), row : row + 16, 0:C] = normed_rows(x, gain[...])
            return carry

        lax.fori_loop(0, 6, one, 0)

    def pack(row, offset):
        block = xn[:, row : row + 16, :].reshape(EXT * 16, WIDE).astype(BF)
        u = lax.broadcasted_iota(I32, (144, EXT * 16), 0)
        c = (u * 171) >> 9
        place = c * 16 + (u - 3 * c) + offset
        select = (lax.broadcasted_iota(I32, (144, EXT * 16), 1) == place).astype(F32).astype(BF)
        return dot(select, block).astype(BF)

    def lat_copy(up):
        if up:
            return pltpu.make_async_remote_copy(
                src_ref=pk_bot.at[0:144],
                dst_ref=pk_top.at[0:144],
                send_sem=lat_send.at[0],
                recv_sem=lat_recv.at[0],
                device_id=(lat_up, lon),
                device_id_type=MESH,
            )
        return pltpu.make_async_remote_copy(
            src_ref=pk_top.at[144:288],
            dst_ref=pk_bot.at[144:288],
            send_sem=lat_send.at[1],
            recv_sem=lat_recv.at[1],
            device_id=(lat_dn, lon),
            device_id_type=MESH,
        )

    def gather_edges():
        t = lax.broadcasted_iota(I32, (80, 288), 0)
        lane = lax.broadcasted_iota(I32, (80, 288), 1)
        place = jnp.where(t < WIN, t + 108 * (t >= 36).astype(I32), -1000)
        for j in range(4):
            select = (lane == place + 36 * j).astype(F32).astype(BF)
            for k, rows in enumerate((pk_top, pk_bot)):
                xwin[11 + 2 * k + j // 2, 80 * (j % 2) : 80 * (j % 2) + 80, :] = dot(
                    select, rows[...]
                ).astype(BF)

    lane128 = lax.broadcasted_iota(I32, (80, 128), 1)

    def attend(u):
        both = xwin[u, :, 0:C]
        qkv[:, 0:1024] = dot(both, wbuf[0]).astype(BF)
        qkv[:, 1024:1536] = dot(both, wbuf[1, :, 0:C]).astype(BF)
        for w in range(2):
            rows = slice(80 * w, 80 * w + 80)
            hot = xwin[u, rows, C:WIDE]
            differs = jnp.where(lane128 < 6, MASKED * (1.0 - hot.astype(F32)), 0.0).astype(BF)
            for g in range(4):
                query, key, value = (
                    qkv[rows, C * part + 128 * g : C * part + 128 * g + 128] for part in range(3)
                )
                keys = jnp.concatenate(
                    [jnp.concatenate([key * head_mask[k], hot], axis=1) for k in range(4)], axis=0
                )
                scores = dot_nt(keys, jnp.concatenate([query, differs], axis=1))
                s = scores.reshape(4, 80, 80) * SCALE + bias[4 * g : 4 * g + 4, :, 0:80]
                e = jnp.exp2(s - jnp.max(s, axis=1, keepdims=True))
                values = jnp.concatenate(
                    [
                        jnp.concatenate([value * head_mask[k], head_mask[k]], axis=1)
                        for k in range(4)
                    ],
                    axis=0,
                )
                summed = lax.dot_general(
                    e.reshape(320, 80).astype(BF), values, TN, preferred_element_type=F32
                )
                ctx[rows, 128 * g : 128 * g + 128] = (
                    summed[:, 0:128] * (1.0 / summed[:, 128:256])
                ).astype(BF)
        return dot(ctx[...], wbuf[1, :, 512:1024]).astype(BF)

    def unit(u, carry):
        @pl.when(u == 1)
        def _():
            forward(2)

        @pl.when(u == 7)
        def _():
            halo_chunk(0)
            pk_top[144:288, :] = pack(0, 0)
            lat_copy(False).start()
            for n in range(2):
                gather_pair(n, 0, 3, 7 + n)

        @pl.when(u == 9)
        def _():
            halo_chunk(1)
            pk_bot[0:144, :] = pack(32, 13)
            lat_copy(True).start()
            for n in range(2):
                gather_pair(5 + n, 0, 3, 9 + n)

        @pl.when(u == 11)
        def _():
            lat_copy(True).wait_recv()
            lat_copy(False).wait_recv()
            gather_edges()

        @pl.when(u == 15)
        def _():
            halo_chunk(2)
            for n in range(3):
                gather_pair(2 + n, 0, 3, 15 + n)

        att = attend(u)
        inner = u < 7
        edge = (u >= 11) & (u < 15)
        top = edge & (u < 13)
        bottom = edge & (u >= 13)
        i = jnp.where(inner, u, jnp.where(u < 9, u - 7, jnp.where(u < 11, u - 4, u - 13)))
        start, offset = start_and_offset(i)
        start = jnp.where(edge, jnp.where(top, 0, 32), start)
        offset = jnp.where(edge, jnp.where(top, -3, 13), offset)
        kind = jnp.where(top, 1, jnp.where(bottom, 2, 0))
        start = pl.multiple_of(start, 8)
        row = lax.broadcasted_iota(I32, (192, 80), 0)
        select = (row - offset == place_out[kind]).astype(F32).astype(BF)
        for w in range(2):
            j = jnp.where(inner, 1 + w, jnp.where(edge, 2 * ((u - 11) % 2) + w, 3 * w))
            back = dot(select, att[80 * w : 80 * w + 80])
            spot = (pl.ds(12 * j, 12), pl.ds(start, 16), slice(None))
            acc[spot] = acc[spot] + back.reshape(12, 16, C)
        return carry

    lax.fori_loop(0, UNITS, unit, 0)

    def finish(c, carry):
        xo[c] = acc[c + 6].astype(BF)
        return carry

    def store(k):
        part = pl.ds(9 * k, 9)
        return pltpu.make_async_copy(xo.at[part], out.at[part], out_sem.at[k])

    for k in range(4):
        lax.fori_loop(9 * k, 9 * k + 9, finish, 0, unroll=3)
        store(k).start()

    mirror_copy(lon).wait_send()

    def sent(d, carry):
        plane_copy(lon, lax.rem(m + d, plane), m, own_send.at[d], own_recv).wait_send()
        plane_copy(lon_pair, lax.rem(m + d, plane), m, par_send.at[d], par_recv).wait_send()
        return carry

    lax.fori_loop(1, plane, sent, 0)

    def sent_on(d, carry):
        sibling_copy(core, lax.rem(m + d, plane)).wait_send()
        return carry

    sibling_pair_copy(core).wait_send()
    lax.fori_loop(1, plane, sent_on, 0)
    for side in range(2):
        label_copy(side).wait_send()
        for k in range(3):
            leg_copy(side, k).wait_send()
            halo_copy(side, k).wait_send()
    lat_copy(True).wait_send()
    lat_copy(False).wait_send()
    for k in range(4):
        store(k).wait()


def local(tokens, region, ln_gain, qkv_weight, proj_weight, position_bias):
    nlat = lax.axis_size("lat")
    nlon = lax.axis_size("lon")
    plane = nlon // 2
    dma = pltpu.SemaphoreType.DMA
    vm = pltpu.VMEM
    mixed = pl.pallas_call(
        functools.partial(kernel, nlat, nlon),
        out_shape=jax.ShapeDtypeStruct((COLS, ROWS, C), BF),
        in_specs=[pl.BlockSpec(memory_space=pl.ANY)] * 6,
        out_specs=pl.BlockSpec(memory_space=pl.ANY),
        scratch_shapes=[
            vm((COLS, ROWS, C), BF),
            vm((2, 6, ROWS, C), BF),
            vm((2, 6, ROWS, C), BF),
            vm((COLS, ROWS), I32),
            vm((2, 8, 128), I32),
            vm((2, 8, 128), I32),
            vm((EXT, ROWS), I32),
            vm((ROWS, EXT), F32),
            vm((1, C), F32),
            vm((HEADS, WIN, WIN), F32),
            vm((HEADS, 80, 128), F32),
            vm((2, C, 1024), BF),
            vm((EXT, ROWS, WIDE), F32),
            vm((EXT, ROWS, C), F32),
            vm((UNITS, 160, WIDE), BF),
            vm((288, WIDE), BF),
            vm((288, WIDE), BF),
            vm((160, 3 * C), BF),
            vm((160, C), BF),
            vm((4, 80, 128), BF),
            vm((80, 192), I32),
            vm((3, 192, 80), I32),
            dma((7,)),
            dma((4,)),
            dma,
            dma,
            dma((plane,)),
            dma((plane,)),
            dma((plane,)),
            dma((plane,)),
            dma((plane,)),
            dma((plane,)),
            dma((2, 3)),
            dma((2, 3)),
            dma((2, 3)),
            dma((2, 3)),
            dma((2,)),
            dma((2,)),
            dma((2,)),
            dma((2,)),
        ],
        compiler_params=pltpu.CompilerParams(
            collective_id=0, has_side_effects=True, vmem_limit_bytes=56 * 2**20
        ),
        cost_estimate=pl.CostEstimate(
            flops=8_000_000_000, bytes_accessed=12_000_000, transcendentals=6_000_000
        ),
    )(
        jnp.transpose(tokens, (1, 0, 2)),
        jnp.transpose(region, (1, 0)),
        ln_gain.reshape(1, C),
        qkv_weight,
        proj_weight,
        position_bias,
    )
    return jnp.transpose(mixed, (1, 0, 2))


def solution(mesh):
    return jax.shard_map(
        local,
        mesh=mesh,
        in_specs=(P("lat", "lon", None), P("lat", "lon"), P(), P("lon", None), P("lon", None), P()),
        out_specs=P("lat", "lon", None),
        check_vma=False,
    )
```

```python
import functools
import math

import jax
import jax.numpy as jnp
from jax import lax
from jax.experimental import pallas as pl
from jax.experimental.pallas import tpu as pltpu
from jax.sharding import PartitionSpec as P

HEADS = 16
HD = 32
C = 512
WIN = 72
ROWS = 48
COLS = 36
EXT = 48
FEAT = 128
WIDE = C + FEAT
LOG2E = math.log2(math.e)
SCALE = HD**-0.5 * LOG2E
MASKED = -1e30
UNITS = 18
BF = jnp.bfloat16
F32 = jnp.float32
I32 = jnp.int32
MESH = pl.DeviceIdType.MESH
NT = (((1,), (1,)), ((), ()))
TN = (((0,), (0,)), ((), ()))


def dot(a, b):
    return jnp.dot(a, b, preferred_element_type=F32)


def dot_nt(a, b, precision=None):
    return lax.dot_general(a, b, NT, preferred_element_type=F32, precision=precision)


def token_parts(t):
    half = (t >= 36).astype(I32)
    u = t - 36 * half
    c = (u * 43) >> 7
    return half, c, u - 3 * c


def block_place(t):
    half, c, r = token_parts(t)
    return c * 16 + half * 3 + r


def normed_rows(x, gain):
    mean = jnp.sum(x, axis=-1, keepdims=True) * (1.0 / C)
    d = x - mean
    var = jnp.sum(d * d, axis=-1, keepdims=True) * (1.0 / C)
    return (d * lax.rsqrt(var + 1e-05) * gain).astype(BF).astype(F32)


def kernel(
    nlat,
    nlon,
    tok,
    reg,
    gain_hbm,
    wqkv,
    wproj,
    bias_hbm,
    out,
    xo,
    halo,
    relay,
    lab_own,
    lab_send,
    lab_recv,
    lab_ext,
    lab_t,
    gain,
    bias_raw,
    bias,
    wbuf,
    xn,
    acc,
    xwin,
    pk_top,
    pk_bot,
    qkv,
    ctx,
    head_mask,
    place_in,
    place_out,
    loc_sem,
    out_sem,
    z_send,
    z_recv,
    line_send,
    line_recv,
    block_send,
    block_recv,
    sib_send,
    sib_recv,
    leg_send,
    leg_recv,
    halo_send,
    halo_recv,
    lab_ssem,
    lab_rsem,
    lat_send,
    lat_recv,
):
    shard = C // nlon
    plane = nlon // 2
    lat = lax.axis_index("lat")
    lon = lax.axis_index("lon")
    core = lax.rem(lat, 2)
    zhi = lax.rem(lon, 2)
    m = lon // 2
    lat_up = lax.rem(lat + 1, nlat)
    lat_dn = lax.rem(lat + nlat - 1, nlat)
    lon_up = lax.rem(lon + 1, nlon)
    lon_dn = lax.rem(lon + nlon - 1, nlon)
    lon_pair = lon + 1 - 2 * zhi
    lat_mirror = (nlat // 2 - 1 - lat // 2) * 2 + core
    lat_sib = lat + 1 - 2 * core
    nx = min(4, plane)
    ny = plane // nx
    y, x = m // nx, lax.rem(m, nx)

    zlo = nlat // 2
    ring = 2 * zlo
    leg = zlo // 2
    z = zhi * zlo + lat // 2

    def chip_at(column, place):
        place = lax.rem(place + 2 * ring, ring)
        return lax.rem(place, zlo) * 2 + core, column * 2 + place // zlo

    above = chip_at(m, z + leg)
    below = chip_at(m, z - leg)

    def beyond(place, by):
        lat_s, lon_s = chip_at(m, place)
        return lat_s, lax.rem(lon_s + by + nlon, nlon)

    onward = (beyond(z - leg, 1), beyond(z + leg, -1))
    relays_here = (
        chip_at(lon_dn // 2, lax.rem(lon_dn, 2) * zlo + lat // 2 + leg),
        chip_at(lon_up // 2, lax.rem(lon_up, 2) * zlo + lat // 2 - leg),
    )

    own_rows = pl.ds(zhi * shard, shard)

    def quarter_load(k, source):
        return pltpu.make_async_copy(source, wbuf.at[k, y, x, own_rows, :], loc_sem.at[k % 2])

    quarters = (
        (quarter_load(0, wqkv.at[:, 0:C]), quarter_load(1, wqkv.at[:, C : 2 * C])),
        (quarter_load(2, wqkv.at[:, 2 * C : 3 * C]), quarter_load(3, wproj)),
    )
    for c in range(2):

        @pl.when(core == c)
        def _():
            for copy in quarters[c]:
                copy.start()

    loads = [
        pltpu.make_async_copy(reg, lab_own, loc_sem.at[2]),
        pltpu.make_async_copy(tok, xo, loc_sem.at[3]),
        pltpu.make_async_copy(gain_hbm, gain, loc_sem.at[4]),
        pltpu.make_async_copy(bias_hbm, bias_raw, loc_sem.at[5]),
    ]
    for copy in loads:
        copy.start()

    barrier = pltpu.get_barrier_semaphore()
    greeted = (
        (lat, lon_up),
        (lat, lon_dn),
        (lat_up, lon),
        (lat_dn, lon),
        (lat_mirror, lon_pair),
        above,
        below,
    )
    greeted = greeted + relays_here
    greeted = greeted + tuple((lat, (y * nx + lax.rem(x + d, nx)) * 2 + zhi) for d in range(1, nx))
    greeted = greeted + tuple((lat, (lax.rem(y + d, ny) * nx + x) * 2 + zhi) for d in range(1, ny))
    for there in greeted:
        pl.semaphore_signal(barrier, inc=1, device_id=there, device_id_type=MESH)
    pl.semaphore_wait(barrier, len(greeted))

    def plane_device(py, px):
        return lat, (py * nx + px) * 2 + zhi

    def at_x(d):
        return lax.rem(x + d, nx)

    def at_y(d):
        return lax.rem(y + d, ny)

    def mirror_copy(of):
        part = wbuf.at[pl.ds(2 * core, 2), y, x, pl.ds(of * shard, shard), :]
        return pltpu.make_async_remote_copy(
            src_ref=part,
            dst_ref=part,
            send_sem=z_send,
            recv_sem=z_recv,
            device_id=(lat_mirror, lon_pair),
            device_id_type=MESH,
        )

    def line_copy(a, d, owner):
        py, px = (y, owner) if a == 0 else (owner, x)
        part = wbuf.at[2 * core + a, py, px]
        return pltpu.make_async_remote_copy(
            src_ref=part,
            dst_ref=part,
            send_sem=line_send.at[a, d],
            recv_sem=line_recv.at[a, owner],
            device_id=plane_device(y, at_x(d)) if a == 0 else plane_device(at_y(d), x),
            device_id_type=MESH,
        )

    def block_of(half, a, owner):
        return wbuf.at[2 * half, owner] if a == 0 else wbuf.at[2 * half + 1, :, owner]

    def block_copy(a, d, owner):
        part = block_of(core, a, owner)
        return pltpu.make_async_remote_copy(
            src_ref=part,
            dst_ref=part,
            send_sem=block_send.at[a, d],
            recv_sem=block_recv.at[a, owner],
            device_id=plane_device(at_y(d), x) if a == 0 else plane_device(y, at_x(d)),
            device_id_type=MESH,
        )

    def sibling_copy(half, a, owner):
        part = block_of(half, a, owner)
        return pltpu.make_async_remote_copy(
            src_ref=part,
            dst_ref=part,
            send_sem=sib_send.at[a, owner],
            recv_sem=sib_recv.at[a, owner],
            device_id=(lat_sib, lon),
            device_id_type=MESH,
        )

    first_axis = ((nx, x, at_x), (ny, y, at_y))
    second_axis = ((ny, y, at_y), (nx, x, at_x))

    def send_lines():
        for a, (n, me, _) in enumerate(first_axis):
            for d in range(1, n):
                line_copy(a, d, me).start()

    def send_blocks():
        for a, (n, _, at) in enumerate(first_axis):
            for d in range(1, n):
                line_copy(a, d, at(d)).wait_recv()
        for a, (n, me, _) in enumerate(second_axis):
            for d in range(1, n):
                block_copy(a, d, me).start()
            sibling_copy(core, a, me).start()

    def pass_on():
        for d in range(1, max(nx, ny)):
            for a, (n, _, at) in enumerate(second_axis):
                if d < n:
                    block_copy(a, d, at(d)).wait_recv()
                    sibling_copy(core, a, at(d)).start()

    for c in range(2):

        @pl.when(core == c)
        def _():
            for copy in quarters[c]:
                copy.wait()

    mirror_copy(zhi).start()

    def leg_copy(side, k):
        rows = pl.ds((0, 32, 16)[k], 16)
        cols = pl.ds(COLS - 6, 6) if side == 0 else pl.ds(0, 6)
        return pltpu.make_async_remote_copy(
            src_ref=tok.at[cols, rows, :],
            dst_ref=relay.at[side, :, rows, :],
            send_sem=leg_send.at[side, k],
            recv_sem=leg_recv.at[side, k],
            device_id=(above, below)[side],
            device_id_type=MESH,
        )

    def halo_copy(side, k):
        rows = pl.ds((0, 32, 16)[k], 16)
        return pltpu.make_async_remote_copy(
            src_ref=relay.at[side, :, rows, :],
            dst_ref=halo.at[side, :, rows, :],
            send_sem=halo_send.at[side, k],
            recv_sem=halo_recv.at[side, k],
            device_id=onward[side],
            device_id_type=MESH,
        )

    def set_out(k):
        for side in range(2):
            leg_copy(side, k).start()

    def forward(k):
        for side in range(2):
            leg_copy(side, k).wait_recv()
            halo_copy(side, k).start()

    def label_copy(side):
        return pltpu.make_async_remote_copy(
            src_ref=lab_send.at[side],
            dst_ref=lab_recv.at[side],
            send_sem=lab_ssem.at[side],
            recv_sem=lab_rsem.at[side],
            device_id=(lat, lon_up if side == 0 else lon_dn),
            device_id_type=MESH,
        )

    loads[0].wait()
    lab_send[...] = jnp.zeros_like(lab_send)
    lab_send[0, 0:6, 0:ROWS] = lab_own[COLS - 6 : COLS, :]
    lab_send[1, 0:6, 0:ROWS] = lab_own[0:6, :]
    for side in range(2):
        label_copy(side).start()
    set_out(0)

    mirror_copy(1 - zhi).wait_recv()
    send_lines()
    set_out(1)

    lane80 = lax.broadcasted_iota(I32, (80, 128), 1)
    for k in range(4):
        head_mask[k] = ((lane80 >= HD * k) & (lane80 < HD * k + HD)).astype(F32).astype(BF)
    t_in = lax.broadcasted_iota(I32, (80, 192), 0)
    place_in[...] = jnp.where(t_in < WIN, block_place(t_in), -1000)
    t_out = lax.broadcasted_iota(I32, (192, 80), 1)
    for k, (least, most) in enumerate(((0, WIN), (36, WIN), (0, 36))):
        place_out[k] = jnp.where((t_out >= least) & (t_out < most), block_place(t_out), -1000)

    loads[1].wait()
    loads[2].wait()
    loads[3].wait()

    def own_column(c, carry):
        x = xo[c].astype(F32)
        acc[c + 6] = x
        xn[c + 6, :, 0:C] = normed_rows(x, gain[...])
        return carry

    lax.fori_loop(0, COLS, own_column, 0, unroll=2)
    send_blocks()
    forward(0)
    set_out(2)

    def place_rows(count):
        half, c, r = token_parts(lax.broadcasted_iota(I32, (count, WIN), 0))
        place = jnp.where(
            lax.broadcasted_iota(I32, (count, WIN), 0) < WIN, (half * 3 + r) * 12 + c, -1
        )
        return (lax.broadcasted_iota(I32, (count, WIN), 1) == place).astype(F32)

    padded = lax.broadcasted_iota(I32, (80, 128), 0) >= WIN

    def bias_of(h, carry):
        keys_first = dot_nt(place_rows(80), bias_raw[h], lax.Precision.HIGHEST)
        placed = dot_nt(keys_first, place_rows(128), lax.Precision.HIGHEST)
        bias[h] = jnp.where(padded, MASKED, placed * LOG2E)
        return carry

    lax.fori_loop(0, HEADS, bias_of, 0, unroll=4)
    forward(1)
    pass_on()
    forward(2)

    for side in range(2):
        label_copy(side).wait_recv()
    lab_ext[0:6, :] = lab_recv[0, 0:6, 0:ROWS]
    lab_ext[6 : 6 + COLS, :] = lab_own[...]
    lab_ext[6 + COLS : EXT, :] = lab_recv[1, 0:6, 0:ROWS]
    eye = (
        lax.broadcasted_iota(I32, (ROWS, ROWS), 0) == lax.broadcasted_iota(I32, (ROWS, ROWS), 1)
    ).astype(BF)
    low = ((lax.broadcasted_iota(I32, (ROWS, EXT), 0) < 3) & (lat == 0)).astype(F32)
    lab_t[...] = dot_nt(eye, lab_ext[...].astype(F32).astype(BF)) + 3.0 * low

    def features(e, carry):
        lane = lax.broadcasted_iota(I32, (ROWS, EXT), 1)
        code = jnp.sum(jnp.where(lane == e, lab_t[...], 0.0), axis=1, keepdims=True)
        wide = lax.broadcasted_iota(I32, (ROWS, FEAT), 1).astype(F32)
        xn[e, :, C:WIDE] = (wide == code).astype(F32)
        return carry

    lax.fori_loop(0, EXT, features, 0, unroll=4)

    def start_and_offset(i):
        start = 8 * ((13 * i) // 16)
        return start, 3 + 6 * i - start

    lane_in = lax.broadcasted_iota(I32, (80, 192), 1)

    def gather_pair(i, first, second, u):
        start, offset = start_and_offset(i)
        if not isinstance(i, int):
            start = pl.multiple_of(start, 8)
        select = (lane_in - offset == place_in[...]).astype(F32).astype(BF)
        for w, j in enumerate((first, second)):
            block = xn[12 * j : 12 * j + 12, pl.ds(start, 16), :].reshape(192, WIDE).astype(BF)
            xwin[u, 80 * w : 80 * w + 80, :] = dot(select, block).astype(BF)

    def gather_inner(i, carry):
        gather_pair(i, 1, 2, i)
        return carry

    lax.fori_loop(0, 7, gather_inner, 0)

    for a, (n, _, at) in enumerate(second_axis):
        for d in range(n):
            sibling_copy(1 - core, a, at(d)).wait_recv()

    def halo_chunk(k):
        row = (0, 32, 16)[k]
        for side in range(2):
            halo_copy(side, k).wait_recv()

        def one(c, carry):
            for side in range(2):
                x = halo[side, c, row : row + 16, :].astype(F32)
                xn[c + side * (EXT - 6), row : row + 16, 0:C] = normed_rows(x, gain[...])
            return carry

        lax.fori_loop(0, 6, one, 0)

    def pack(row, offset):
        block = xn[:, row : row + 16, :].reshape(EXT * 16, WIDE).astype(BF)
        u = lax.broadcasted_iota(I32, (144, EXT * 16), 0)
        c = (u * 171) >> 9
        place = c * 16 + (u - 3 * c) + offset
        select = (lax.broadcasted_iota(I32, (144, EXT * 16), 1) == place).astype(F32).astype(BF)
        return dot(select, block).astype(BF)

    def lat_copy(up):
        if up:
            return pltpu.make_async_remote_copy(
                src_ref=pk_bot.at[0:144],
                dst_ref=pk_top.at[0:144],
                send_sem=lat_send.at[0],
                recv_sem=lat_recv.at[0],
                device_id=(lat_up, lon),
                device_id_type=MESH,
            )
        return pltpu.make_async_remote_copy(
            src_ref=pk_top.at[144:288],
            dst_ref=pk_bot.at[144:288],
            send_sem=lat_send.at[1],
            recv_sem=lat_recv.at[1],
            device_id=(lat_dn, lon),
            device_id_type=MESH,
        )

    def gather_edges():
        t = lax.broadcasted_iota(I32, (80, 288), 0)
        lane = lax.broadcasted_iota(I32, (80, 288), 1)
        place = jnp.where(t < WIN, t + 108 * (t >= 36).astype(I32), -1000)
        for j in range(4):
            select = (lane == place + 36 * j).astype(F32).astype(BF)
            for k, rows in enumerate((pk_top, pk_bot)):
                xwin[11 + 2 * k + j // 2, 80 * (j % 2) : 80 * (j % 2) + 80, :] = dot(
                    select, rows[...]
                ).astype(BF)

    lane128 = lax.broadcasted_iota(I32, (80, 128), 1)

    def weight(k):
        return wbuf[k].reshape(C, C)

    def attend(u):
        both = xwin[u, :, 0:C]
        for part in range(3):
            qkv[:, C * part : C * part + C] = dot(both, weight(part)).astype(BF)
        for w in range(2):
            rows = slice(80 * w, 80 * w + 80)
            hot = xwin[u, rows, C:WIDE]
            differs = jnp.where(lane128 < 6, MASKED * (1.0 - hot.astype(F32)), 0.0).astype(BF)
            for g in range(4):
                query, key, value = (
                    qkv[rows, C * part + 128 * g : C * part + 128 * g + 128] for part in range(3)
                )
                keys = jnp.concatenate(
                    [jnp.concatenate([key * head_mask[k], hot], axis=1) for k in range(4)], axis=0
                )
                scores = dot_nt(keys, jnp.concatenate([query, differs], axis=1))
                s = scores.reshape(4, 80, 80) * SCALE + bias[4 * g : 4 * g + 4, :, 0:80]
                e = jnp.exp2(s - jnp.max(s, axis=1, keepdims=True))
                values = jnp.concatenate(
                    [
                        jnp.concatenate([value * head_mask[k], head_mask[k]], axis=1)
                        for k in range(4)
                    ],
                    axis=0,
                )
                summed = lax.dot_general(
                    e.reshape(320, 80).astype(BF), values, TN, preferred_element_type=F32
                )
                ctx[rows, 128 * g : 128 * g + 128] = (
                    summed[:, 0:128] * (1.0 / summed[:, 128:256])
                ).astype(BF)
        return dot(ctx[...], weight(3)).astype(BF)

    def unit(u, carry):
        @pl.when(u == 7)
        def _():
            halo_chunk(0)
            pk_top[144:288, :] = pack(0, 0)
            lat_copy(False).start()
            for n in range(2):
                gather_pair(n, 0, 3, 7 + n)

        @pl.when(u == 9)
        def _():
            halo_chunk(1)
            pk_bot[0:144, :] = pack(32, 13)
            lat_copy(True).start()
            for n in range(2):
                gather_pair(5 + n, 0, 3, 9 + n)

        @pl.when(u == 11)
        def _():
            lat_copy(True).wait_recv()
            lat_copy(False).wait_recv()
            gather_edges()

        @pl.when(u == 15)
        def _():
            halo_chunk(2)
            for n in range(3):
                gather_pair(2 + n, 0, 3, 15 + n)

        att = attend(u)
        inner = u < 7
        edge = (u >= 11) & (u < 15)
        top = edge & (u < 13)
        bottom = edge & (u >= 13)
        i = jnp.where(inner, u, jnp.where(u < 9, u - 7, jnp.where(u < 11, u - 4, u - 13)))
        start, offset = start_and_offset(i)
        start = jnp.where(edge, jnp.where(top, 0, 32), start)
        offset = jnp.where(edge, jnp.where(top, -3, 13), offset)
        kind = jnp.where(top, 1, jnp.where(bottom, 2, 0))
        start = pl.multiple_of(start, 8)
        row = lax.broadcasted_iota(I32, (192, 80), 0)
        select = (row - offset == place_out[kind]).astype(F32).astype(BF)
        for w in range(2):
            j = jnp.where(inner, 1 + w, jnp.where(edge, 2 * ((u - 11) % 2) + w, 3 * w))
            back = dot(select, att[80 * w : 80 * w + 80])
            spot = (pl.ds(12 * j, 12), pl.ds(start, 16), slice(None))
            acc[spot] = acc[spot] + back.reshape(12, 16, C)
        return carry

    lax.fori_loop(0, UNITS, unit, 0)

    def finish(c, carry):
        xo[c] = acc[c + 6].astype(BF)
        return carry

    def store(k):
        part = pl.ds(9 * k, 9)
        return pltpu.make_async_copy(xo.at[part], out.at[part], out_sem.at[k])

    for k in range(4):
        lax.fori_loop(9 * k, 9 * k + 9, finish, 0, unroll=3)
        store(k).start()

    mirror_copy(zhi).wait_send()
    for a, (n, me, _) in enumerate(first_axis):
        for d in range(1, n):
            line_copy(a, d, me).wait_send()
    for a, (n, me, at) in enumerate(second_axis):
        for d in range(1, n):
            block_copy(a, d, me).wait_send()
        for d in range(n):
            sibling_copy(core, a, at(d)).wait_send()
    for side in range(2):
        label_copy(side).wait_send()
        for k in range(3):
            leg_copy(side, k).wait_send()
            halo_copy(side, k).wait_send()
    lat_copy(True).wait_send()
    lat_copy(False).wait_send()
    for k in range(4):
        store(k).wait()


def local(tokens, region, ln_gain, qkv_weight, proj_weight, position_bias):
    nlat = lax.axis_size("lat")
    nlon = lax.axis_size("lon")
    plane = nlon // 2
    nx = min(4, plane)
    ny = plane // nx
    dma = pltpu.SemaphoreType.DMA
    vm = pltpu.VMEM
    mixed = pl.pallas_call(
        functools.partial(kernel, nlat, nlon),
        out_shape=jax.ShapeDtypeStruct((COLS, ROWS, C), BF),
        in_specs=[pl.BlockSpec(memory_space=pl.ANY)] * 6,
        out_specs=pl.BlockSpec(memory_space=pl.ANY),
        scratch_shapes=[
            vm((COLS, ROWS, C), BF),
            vm((2, 6, ROWS, C), BF),
            vm((2, 6, ROWS, C), BF),
            vm((COLS, ROWS), I32),
            vm((2, 8, 128), I32),
            vm((2, 8, 128), I32),
            vm((EXT, ROWS), I32),
            vm((ROWS, EXT), F32),
            vm((1, C), F32),
            vm((HEADS, WIN, WIN), F32),
            vm((HEADS, 80, 128), F32),
            vm((4, ny, nx, 2 * (C // nlon), C), BF),
            vm((EXT, ROWS, WIDE), F32),
            vm((EXT, ROWS, C), F32),
            vm((UNITS, 160, WIDE), BF),
            vm((288, WIDE), BF),
            vm((288, WIDE), BF),
            vm((160, 3 * C), BF),
            vm((160, C), BF),
            vm((4, 80, 128), BF),
            vm((80, 192), I32),
            vm((3, 192, 80), I32),
            dma((6,)),
            dma((4,)),
            dma,
            dma,
            dma((2, nx)),
            dma((2, nx)),
            dma((2, nx)),
            dma((2, nx)),
            dma((2, nx)),
            dma((2, nx)),
            dma((2, 3)),
            dma((2, 3)),
            dma((2, 3)),
            dma((2, 3)),
            dma((2,)),
            dma((2,)),
            dma((2,)),
            dma((2,)),
        ],
        compiler_params=pltpu.CompilerParams(
            collective_id=0, has_side_effects=True, vmem_limit_bytes=56 * 2**20
        ),
        cost_estimate=pl.CostEstimate(
            flops=8_000_000_000, bytes_accessed=12_000_000, transcendentals=6_000_000
        ),
    )(
        jnp.transpose(tokens, (1, 0, 2)),
        jnp.transpose(region, (1, 0)),
        ln_gain.reshape(1, C),
        qkv_weight,
        proj_weight,
        position_bias,
    )
    return jnp.transpose(mixed, (1, 0, 2))


def solution(mesh):
    return jax.shard_map(
        local,
        mesh=mesh,
        in_specs=(P("lat", "lon", None), P("lat", "lon"), P(), P("lon", None), P("lon", None), P()),
        out_specs=P("lat", "lon", None),
        check_vma=False,
    )
```

```python
import functools
import math

import jax
import jax.numpy as jnp
from jax import lax
from jax.experimental import pallas as pl
from jax.experimental.pallas import tpu as pltpu
from jax.sharding import PartitionSpec as P

HEADS = 16
HD = 32
C = 512
WIN = 72
ROWS = 48
COLS = 36
EXT = 48
FEAT = 128
WIDE = C + FEAT
LOG2E = math.log2(math.e)
SCALE = HD**-0.5 * LOG2E
MASKED = -1e30
UNITS = 18
BF = jnp.bfloat16
F32 = jnp.float32
I32 = jnp.int32
MESH = pl.DeviceIdType.MESH
NT = (((1,), (1,)), ((), ()))
TN = (((0,), (0,)), ((), ()))


def dot(a, b):
    return jnp.dot(a, b, preferred_element_type=F32)


def dot_nt(a, b, precision=None):
    return lax.dot_general(a, b, NT, preferred_element_type=F32, precision=precision)


def token_parts(t):
    half = (t >= 36).astype(I32)
    u = t - 36 * half
    c = (u * 43) >> 7
    return half, c, u - 3 * c


def block_place(t):
    half, c, r = token_parts(t)
    return c * 16 + half * 3 + r


def normed_rows(x, gain):
    mean = jnp.sum(x, axis=-1, keepdims=True) * (1.0 / C)
    d = x - mean
    var = jnp.sum(d * d, axis=-1, keepdims=True) * (1.0 / C)
    return (d * lax.rsqrt(var + 1e-05) * gain).astype(BF).astype(F32)


def kernel(
    nlat,
    nlon,
    tok,
    reg,
    gain_hbm,
    wqkv,
    wproj,
    bias_hbm,
    out,
    xo,
    halo,
    relay,
    lab_own,
    lab_send,
    lab_recv,
    lab_ext,
    lab_t,
    gain,
    bias_raw,
    bias,
    wbuf,
    xn,
    acc,
    xwin,
    pk_top,
    pk_bot,
    qkv,
    ctx,
    head_mask,
    place_in,
    place_out,
    second_owns,
    loc_sem,
    out_sem,
    z_send,
    z_recv,
    line_send,
    line_recv,
    block_send,
    block_recv,
    sib_send,
    sib_recv,
    leg_send,
    leg_recv,
    halo_send,
    halo_recv,
    lab_ssem,
    lab_rsem,
    lat_send,
    lat_recv,
):
    shard = C // nlon
    plane = nlon // 2
    lat = lax.axis_index("lat")
    lon = lax.axis_index("lon")
    core = lax.rem(lat, 2)
    zhi = lax.rem(lon, 2)
    m = lon // 2
    lat_up = lax.rem(lat + 1, nlat)
    lat_dn = lax.rem(lat + nlat - 1, nlat)
    lon_up = lax.rem(lon + 1, nlon)
    lon_dn = lax.rem(lon + nlon - 1, nlon)
    lon_pair = lon + 1 - 2 * zhi
    lat_mirror = (nlat // 2 - 1 - lat // 2) * 2 + core
    lat_sib = lat + 1 - 2 * core
    nx = min(4, plane)
    ny = plane // nx
    y, x = m // nx, lax.rem(m, nx)

    zlo = nlat // 2
    ring = 2 * zlo
    leg = zlo // 2
    z = zhi * zlo + lat // 2

    def chip_at(column, place):
        place = lax.rem(place + 2 * ring, ring)
        return lax.rem(place, zlo) * 2 + core, column * 2 + place // zlo

    above = chip_at(m, z + leg)
    below = chip_at(m, z - leg)

    def beyond(place, by):
        lat_s, lon_s = chip_at(m, place)
        return lat_s, lax.rem(lon_s + by + nlon, nlon)

    onward = (beyond(z - leg, 1), beyond(z + leg, -1))
    relays_here = (
        chip_at(lon_dn // 2, lax.rem(lon_dn, 2) * zlo + lat // 2 + leg),
        chip_at(lon_up // 2, lax.rem(lon_up, 2) * zlo + lat // 2 - leg),
    )

    own_rows = pl.ds(zhi * shard, shard)

    def quarter_load(k, source):
        return pltpu.make_async_copy(source, wbuf.at[k, y, x, own_rows, :], loc_sem.at[k % 2])

    quarters = (
        (quarter_load(0, wqkv.at[:, 0:C]), quarter_load(1, wqkv.at[:, C : 2 * C])),
        (quarter_load(2, wqkv.at[:, 2 * C : 3 * C]), quarter_load(3, wproj)),
    )
    for c in range(2):

        @pl.when(core == c)
        def _():
            for copy in quarters[c]:
                copy.start()

    loads = [
        pltpu.make_async_copy(reg, lab_own, loc_sem.at[2]),
        pltpu.make_async_copy(tok, xo, loc_sem.at[3]),
        pltpu.make_async_copy(gain_hbm, gain, loc_sem.at[4]),
        pltpu.make_async_copy(bias_hbm, bias_raw, loc_sem.at[5]),
    ]
    for copy in loads:
        copy.start()

    barrier = pltpu.get_barrier_semaphore()
    greeted = (
        (lat, lon_up),
        (lat, lon_dn),
        (lat_up, lon),
        (lat_dn, lon),
        (lat_mirror, lon_pair),
        above,
        below,
    )
    greeted = greeted + relays_here
    greeted = greeted + tuple((lat, (y * nx + lax.rem(x + d, nx)) * 2 + zhi) for d in range(1, nx))
    greeted = greeted + tuple((lat, (lax.rem(y + d, ny) * nx + x) * 2 + zhi) for d in range(1, ny))
    for there in greeted:
        pl.semaphore_signal(barrier, inc=1, device_id=there, device_id_type=MESH)
    pl.semaphore_wait(barrier, len(greeted))

    def plane_device(py, px):
        return lat, (py * nx + px) * 2 + zhi

    def at_x(d):
        return lax.rem(x + d, nx)

    def at_y(d):
        return lax.rem(y + d, ny)

    def mirror_copy(of):
        part = wbuf.at[pl.ds(2 * core, 2), y, x, pl.ds(of * shard, shard), :]
        return pltpu.make_async_remote_copy(
            src_ref=part,
            dst_ref=part,
            send_sem=z_send,
            recv_sem=z_recv,
            device_id=(lat_mirror, lon_pair),
            device_id_type=MESH,
        )

    def line_copy(a, d, owner):
        py, px = (y, owner) if a == 0 else (owner, x)
        part = wbuf.at[2 * core + a, py, px]
        return pltpu.make_async_remote_copy(
            src_ref=part,
            dst_ref=part,
            send_sem=line_send.at[a, d],
            recv_sem=line_recv.at[a, owner],
            device_id=plane_device(y, at_x(d)) if a == 0 else plane_device(at_y(d), x),
            device_id_type=MESH,
        )

    def block_of(half, a, owner):
        return wbuf.at[2 * half, owner] if a == 0 else wbuf.at[2 * half + 1, :, owner]

    def block_copy(a, d, owner):
        part = block_of(core, a, owner)
        return pltpu.make_async_remote_copy(
            src_ref=part,
            dst_ref=part,
            send_sem=block_send.at[a, d],
            recv_sem=block_recv.at[a, owner],
            device_id=plane_device(at_y(d), x) if a == 0 else plane_device(y, at_x(d)),
            device_id_type=MESH,
        )

    def sibling_copy(half, a, owner):
        part = block_of(half, a, owner)
        return pltpu.make_async_remote_copy(
            src_ref=part,
            dst_ref=part,
            send_sem=sib_send.at[a, owner],
            recv_sem=sib_recv.at[a, owner],
            device_id=(lat_sib, lon),
            device_id_type=MESH,
        )

    first_axis = ((nx, x, at_x), (ny, y, at_y))
    second_axis = ((ny, y, at_y), (nx, x, at_x))

    def send_lines():
        for a, (n, me, _) in enumerate(first_axis):
            for d in range(1, n):
                line_copy(a, d, me).start()

    def send_blocks():
        for a, (n, _, at) in enumerate(first_axis):
            for d in range(1, n):
                line_copy(a, d, at(d)).wait_recv()
        for a, (n, me, _) in enumerate(second_axis):
            for d in range(1, n):
                block_copy(a, d, me).start()
            sibling_copy(core, a, me).start()

    def pass_on():
        for d in range(1, max(nx, ny)):
            for a, (n, _, at) in enumerate(second_axis):
                if d < n:
                    block_copy(a, d, at(d)).wait_recv()
                    sibling_copy(core, a, at(d)).start()

    for c in range(2):

        @pl.when(core == c)
        def _():
            for copy in quarters[c]:
                copy.wait()

    mirror_copy(zhi).start()

    def leg_copy(side, k):
        rows = pl.ds((0, 32, 16)[k], 16)
        cols = pl.ds(COLS - 6, 6) if side == 0 else pl.ds(0, 6)
        return pltpu.make_async_remote_copy(
            src_ref=tok.at[cols, rows, :],
            dst_ref=relay.at[side, :, rows, :],
            send_sem=leg_send.at[side, k],
            recv_sem=leg_recv.at[side, k],
            device_id=(above, below)[side],
            device_id_type=MESH,
        )

    def halo_copy(side, k):
        rows = pl.ds((0, 32, 16)[k], 16)
        return pltpu.make_async_remote_copy(
            src_ref=relay.at[side, :, rows, :],
            dst_ref=halo.at[side, :, rows, :],
            send_sem=halo_send.at[side, k],
            recv_sem=halo_recv.at[side, k],
            device_id=onward[side],
            device_id_type=MESH,
        )

    def set_out(k):
        for side in range(2):
            leg_copy(side, k).start()

    def forward(k):
        for side in range(2):
            leg_copy(side, k).wait_recv()
            halo_copy(side, k).start()

    def label_copy(side):
        return pltpu.make_async_remote_copy(
            src_ref=lab_send.at[side],
            dst_ref=lab_recv.at[side],
            send_sem=lab_ssem.at[side],
            recv_sem=lab_rsem.at[side],
            device_id=(lat, lon_up if side == 0 else lon_dn),
            device_id_type=MESH,
        )

    loads[0].wait()
    lab_send[...] = jnp.zeros_like(lab_send)
    lab_send[0, 0:6, 0:ROWS] = lab_own[COLS - 6 : COLS, :]
    lab_send[1, 0:6, 0:ROWS] = lab_own[0:6, :]
    for side in range(2):
        label_copy(side).start()
    set_out(0)

    lane80 = lax.broadcasted_iota(I32, (80, 128), 1)
    for k in range(4):
        head_mask[k] = ((lane80 >= HD * k) & (lane80 < HD * k + HD)).astype(F32).astype(BF)
    t_in = lax.broadcasted_iota(I32, (80, 192), 0)
    place_in[...] = jnp.where(t_in < WIN, block_place(t_in), -1000)
    t_out = lax.broadcasted_iota(I32, (192, 80), 1)
    t_row = lax.broadcasted_iota(I32, (80, 128), 0)
    within = t_row - 36 * (t_row >= 36).astype(I32)
    second_owns[0] = (within < 18).astype(F32)
    second_owns[1] = (t_row < 36).astype(F32)
    for k, (least, most) in enumerate(((0, WIN), (36, WIN), (0, 36))):
        place_out[k] = jnp.where((t_out >= least) & (t_out < most), block_place(t_out), -1000)

    loads[1].wait()
    loads[2].wait()
    loads[3].wait()

    def own_column(c, carry):
        x = xo[c].astype(F32)
        acc[c + 6] = x
        xn[c + 6, :, 0:C] = normed_rows(x, gain[...])
        return carry

    lax.fori_loop(0, COLS // 2, own_column, 0, unroll=2)
    mirror_copy(1 - zhi).wait_recv()
    send_lines()
    set_out(1)
    lax.fori_loop(COLS // 2, COLS, own_column, 0, unroll=2)
    send_blocks()
    forward(0)
    set_out(2)

    def place_rows(count):
        half, c, r = token_parts(lax.broadcasted_iota(I32, (count, WIN), 0))
        place = jnp.where(
            lax.broadcasted_iota(I32, (count, WIN), 0) < WIN, (half * 3 + r) * 12 + c, -1
        )
        return (lax.broadcasted_iota(I32, (count, WIN), 1) == place).astype(F32)

    padded = lax.broadcasted_iota(I32, (80, 128), 0) >= WIN

    def bias_of(h, carry):
        keys_first = dot_nt(place_rows(80), bias_raw[h], lax.Precision.HIGHEST)
        placed = dot_nt(keys_first, place_rows(128), lax.Precision.HIGHEST)
        bias[h] = jnp.where(padded, MASKED, placed * LOG2E)
        return carry

    lax.fori_loop(0, HEADS, bias_of, 0, unroll=4)
    forward(1)
    pass_on()
    forward(2)

    for side in range(2):
        label_copy(side).wait_recv()
    lab_ext[0:6, :] = lab_recv[0, 0:6, 0:ROWS]
    lab_ext[6 : 6 + COLS, :] = lab_own[...]
    lab_ext[6 + COLS : EXT, :] = lab_recv[1, 0:6, 0:ROWS]
    eye = (
        lax.broadcasted_iota(I32, (ROWS, ROWS), 0) == lax.broadcasted_iota(I32, (ROWS, ROWS), 1)
    ).astype(BF)
    low = ((lax.broadcasted_iota(I32, (ROWS, EXT), 0) < 3) & (lat == 0)).astype(F32)
    lab_t[...] = dot_nt(eye, lab_ext[...].astype(F32).astype(BF)) + 3.0 * low

    def features(e, carry):
        lane = lax.broadcasted_iota(I32, (ROWS, EXT), 1)
        code = jnp.sum(jnp.where(lane == e, lab_t[...], 0.0), axis=1, keepdims=True)
        wide = lax.broadcasted_iota(I32, (ROWS, FEAT), 1).astype(F32)
        xn[e, :, C:WIDE] = (wide == code).astype(F32)
        return carry

    lax.fori_loop(0, EXT, features, 0, unroll=4)

    def start_and_offset(i):
        start = 8 * ((13 * i) // 16)
        return start, 3 + 6 * i - start

    lane_in = lax.broadcasted_iota(I32, (80, 192), 1)

    def gather_pair(i, first, second, u):
        start, offset = start_and_offset(i)
        if not isinstance(i, int):
            start = pl.multiple_of(start, 8)
        select = (lane_in - offset == place_in[...]).astype(F32).astype(BF)
        for w, j in enumerate((first, second)):
            block = xn[12 * j : 12 * j + 12, pl.ds(start, 16), :].reshape(192, WIDE).astype(BF)
            xwin[u, 80 * w : 80 * w + 80, :] = dot(select, block).astype(BF)

    def gather_inner(i, carry):
        gather_pair(i, 1, 2, i)
        return carry

    lax.fori_loop(0, 7, gather_inner, 0)

    for a, (n, _, at) in enumerate(second_axis):
        for d in range(n):
            sibling_copy(1 - core, a, at(d)).wait_recv()

    def halo_chunk(k):
        row = (0, 32, 16)[k]
        for side in range(2):
            halo_copy(side, k).wait_recv()

        def one(c, carry):
            for side in range(2):
                x = halo[side, c, row : row + 16, :].astype(F32)
                xn[c + side * (EXT - 6), row : row + 16, 0:C] = normed_rows(x, gain[...])
            return carry

        lax.fori_loop(0, 6, one, 0)

    def pack(row, offset):
        block = xn[:, row : row + 16, :].reshape(EXT * 16, WIDE).astype(BF)
        u = lax.broadcasted_iota(I32, (144, EXT * 16), 0)
        c = (u * 171) >> 9
        place = c * 16 + (u - 3 * c) + offset
        select = (lax.broadcasted_iota(I32, (144, EXT * 16), 1) == place).astype(F32).astype(BF)
        return dot(select, block).astype(BF)

    def lat_copy(up):
        if up:
            return pltpu.make_async_remote_copy(
                src_ref=pk_bot.at[0:144],
                dst_ref=pk_top.at[0:144],
                send_sem=lat_send.at[0],
                recv_sem=lat_recv.at[0],
                device_id=(lat_up, lon),
                device_id_type=MESH,
            )
        return pltpu.make_async_remote_copy(
            src_ref=pk_top.at[144:288],
            dst_ref=pk_bot.at[144:288],
            send_sem=lat_send.at[1],
            recv_sem=lat_recv.at[1],
            device_id=(lat_dn, lon),
            device_id_type=MESH,
        )

    def gather_edges():
        t = lax.broadcasted_iota(I32, (80, 288), 0)
        lane = lax.broadcasted_iota(I32, (80, 288), 1)
        place = jnp.where(t < WIN, t + 108 * (t >= 36).astype(I32), -1000)
        for j in range(4):
            select = (lane == place + 36 * j).astype(F32).astype(BF)
            for k, rows in enumerate((pk_top, pk_bot)):
                xwin[11 + j, 80 * k : 80 * k + 80, :] = dot(
                    select, rows[...]
                ).astype(BF)

    lane128 = lax.broadcasted_iota(I32, (80, 128), 1)

    def weight(k):
        return wbuf[k].reshape(C, C)

    def project(u):
        both = xwin[u, :, 0:C]
        for part in range(3):
            qkv[:, C * part : C * part + C] = dot(both, weight(part)).astype(BF)

    def mask_features(u, w):
        hot = xwin[u, 80 * w : 80 * w + 80, C:WIDE]
        differs = jnp.where(lane128 < 6, MASKED * (1.0 - hot.astype(F32)), 0.0).astype(BF)
        return hot, differs

    def parts_of(w, g):
        rows = slice(80 * w, 80 * w + 80)
        return (qkv[rows, C * part + 128 * g : C * part + 128 * g + 128] for part in range(3))

    def stack(pieces):
        return jnp.concatenate(
            [jnp.concatenate(pieces(head_mask[k]), axis=1) for k in range(4)], axis=0
        )

    def weights_of(scores, g):
        s = scores.reshape(4, 80, 80) * SCALE + bias[4 * g : 4 * g + 4, :, 0:80]
        e = jnp.exp2(s - jnp.max(s, axis=1, keepdims=True))
        return e.reshape(320, 80).astype(BF)

    def over_keys(e, values):
        return lax.dot_general(e, values, TN, preferred_element_type=F32)

    def attend_two(u):
        project(u)
        for w in range(2):
            hot, differs = mask_features(u, w)
            for g in range(4):
                query, key, value = parts_of(w, g)
                scores = dot_nt(
                    stack(lambda mask: [key * mask, hot]),
                    jnp.concatenate([query, differs], axis=1),
                )
                summed = over_keys(weights_of(scores, g), stack(lambda mask: [value * mask, mask]))
                ctx[80 * w : 80 * w + 80, 128 * g : 128 * g + 128] = (
                    summed[:, 0:128] * (1.0 / summed[:, 128:256])
                ).astype(BF)
        return dot(ctx[...], weight(3)).astype(BF)

    def attend_merged(u, kind):
        project(u)
        of_second = second_owns[kind]
        keep1 = of_second.astype(BF)
        keep0 = (1.0 - of_second).astype(BF)
        hot0, differs0 = mask_features(u, 0)
        hot1, differs1 = mask_features(u, 1)
        differs0 = differs0 * keep0
        differs1 = differs1 * keep1
        for g in range(4):
            query0, key0, value0 = parts_of(0, g)
            query1, key1, value1 = parts_of(1, g)
            scores = dot_nt(
                stack(lambda mask: [key0 * mask, hot0, key1 * mask, hot1]),
                jnp.concatenate([query0 * keep0, differs0, query1 * keep1, differs1], axis=1),
            )
            summed = over_keys(
                weights_of(scores, g), stack(lambda mask: [value0 * mask, value1 * mask, mask])
            )
            own = jnp.where(of_second > 0.5, summed[:, 128:256], summed[:, 0:128])
            ctx[0:80, 128 * g : 128 * g + 128] = (own * (1.0 / summed[:, 256:384])).astype(BF)
        return dot(ctx[0:80, :], weight(3)).astype(BF)

    row_out = lax.broadcasted_iota(I32, (192, 80), 0)

    def add_back(att, j, start, offset, kind):
        select = (row_out - offset == place_out[kind]).astype(F32).astype(BF)
        spot = (pl.ds(12 * j, 12), pl.ds(pl.multiple_of(start, 8), 16), slice(None))
        acc[spot] = acc[spot] + dot(select, att).reshape(12, 16, C)

    def inner_unit(u, carry):
        att = attend_two(u)
        start, offset = start_and_offset(u)
        for w in range(2):
            add_back(att[80 * w : 80 * w + 80], 1 + w, start, offset, 0)
        return carry

    lax.fori_loop(0, 7, inner_unit, 0)

    def finish(c, carry):
        xo[c] = acc[c + 6].astype(BF)
        return carry

    def store(k):
        part = (pl.ds(0, 6), pl.ds(6, COLS - 12), pl.ds(COLS - 6, 6))[k]
        return pltpu.make_async_copy(xo.at[part], out.at[part], out_sem.at[k])

    def merged_unit(v, carry):
        @pl.when(v == 0)
        def _():
            halo_chunk(0)
            pk_top[144:288, :] = pack(0, 0)
            lat_copy(False).start()
            for n in range(2):
                gather_pair(n, 0, 3, 7 + n)

        @pl.when(v == 2)
        def _():
            halo_chunk(1)
            pk_bot[0:144, :] = pack(32, 13)
            lat_copy(True).start()
            for n in range(2):
                gather_pair(5 + n, 0, 3, 9 + n)

        @pl.when(v == 4)
        def _():
            lat_copy(True).wait_recv()
            lat_copy(False).wait_recv()
            gather_edges()

        @pl.when(v == 8)
        def _():
            lax.fori_loop(6, COLS - 6, finish, 0, unroll=3)
            store(1).start()
            halo_chunk(2)
            for n in range(3):
                gather_pair(2 + n, 0, 3, 15 + n)

        edge = ((v >= 4) & (v < 8)).astype(I32)
        att = attend_merged(7 + v, edge)
        i = jnp.where(v < 2, v, jnp.where(v < 4, v + 3, v - 6))
        start, offset = start_and_offset(i)
        for w in range(2):
            j = jnp.where(edge == 1, v - 4, 3 * w)
            add_back(
                att,
                j,
                jnp.where(edge == 1, 32 * w, start),
                jnp.where(edge == 1, 16 * w - 3, offset),
                jnp.where(edge == 1, 1 + w, 0),
            )
        return carry

    lax.fori_loop(0, 11, merged_unit, 0)
    for k, first in ((0, 0), (2, COLS - 6)):
        lax.fori_loop(first, first + 6, finish, 0, unroll=3)
        store(k).start()

    mirror_copy(zhi).wait_send()
    for a, (n, me, _) in enumerate(first_axis):
        for d in range(1, n):
            line_copy(a, d, me).wait_send()
    for a, (n, me, at) in enumerate(second_axis):
        for d in range(1, n):
            block_copy(a, d, me).wait_send()
        for d in range(n):
            sibling_copy(core, a, at(d)).wait_send()
    for side in range(2):
        label_copy(side).wait_send()
        for k in range(3):
            leg_copy(side, k).wait_send()
            halo_copy(side, k).wait_send()
    lat_copy(True).wait_send()
    lat_copy(False).wait_send()
    for k in range(3):
        store(k).wait()


def local(tokens, region, ln_gain, qkv_weight, proj_weight, position_bias):
    nlat = lax.axis_size("lat")
    nlon = lax.axis_size("lon")
    plane = nlon // 2
    nx = min(4, plane)
    ny = plane // nx
    dma = pltpu.SemaphoreType.DMA
    vm = pltpu.VMEM
    mixed = pl.pallas_call(
        functools.partial(kernel, nlat, nlon),
        out_shape=jax.ShapeDtypeStruct((COLS, ROWS, C), BF),
        in_specs=[pl.BlockSpec(memory_space=pl.ANY)] * 6,
        out_specs=pl.BlockSpec(memory_space=pl.ANY),
        scratch_shapes=[
            vm((COLS, ROWS, C), BF),
            vm((2, 6, ROWS, C), BF),
            vm((2, 6, ROWS, C), BF),
            vm((COLS, ROWS), I32),
            vm((2, 8, 128), I32),
            vm((2, 8, 128), I32),
            vm((EXT, ROWS), I32),
            vm((ROWS, EXT), F32),
            vm((1, C), F32),
            vm((HEADS, WIN, WIN), F32),
            vm((HEADS, 80, 128), F32),
            vm((4, ny, nx, 2 * (C // nlon), C), BF),
            vm((EXT, ROWS, WIDE), F32),
            vm((EXT, ROWS, C), F32),
            vm((UNITS, 160, WIDE), BF),
            vm((288, WIDE), BF),
            vm((288, WIDE), BF),
            vm((160, 3 * C), BF),
            vm((160, C), BF),
            vm((4, 80, 128), BF),
            vm((80, 192), I32),
            vm((3, 192, 80), I32),
            vm((2, 80, 128), F32),
            dma((6,)),
            dma((4,)),
            dma,
            dma,
            dma((2, nx)),
            dma((2, nx)),
            dma((2, nx)),
            dma((2, nx)),
            dma((2, nx)),
            dma((2, nx)),
            dma((2, 3)),
            dma((2, 3)),
            dma((2, 3)),
            dma((2, 3)),
            dma((2,)),
            dma((2,)),
            dma((2,)),
            dma((2,)),
        ],
        compiler_params=pltpu.CompilerParams(
            collective_id=0, has_side_effects=True, vmem_limit_bytes=56 * 2**20
        ),
        cost_estimate=pl.CostEstimate(
            flops=8_000_000_000, bytes_accessed=12_000_000, transcendentals=6_000_000
        ),
    )(
        jnp.transpose(tokens, (1, 0, 2)),
        jnp.transpose(region, (1, 0)),
        ln_gain.reshape(1, C),
        qkv_weight,
        proj_weight,
        position_bias,
    )
    return jnp.transpose(mixed, (1, 0, 2))


def solution(mesh):
    return jax.shard_map(
        local,
        mesh=mesh,
        in_specs=(P("lat", "lon", None), P("lat", "lon"), P(), P("lon", None), P("lon", None), P()),
        out_specs=P("lat", "lon", None),
        check_vma=False,
    )
```

```python
import functools
import math

import jax
import jax.numpy as jnp
from jax import lax
from jax.experimental import pallas as pl
from jax.experimental.pallas import tpu as pltpu
from jax.sharding import PartitionSpec as P

HEADS = 16
HD = 32
C = 512
WIN = 72
ROWS = 48
COLS = 36
EXT = 48
FEAT = 128
WIDE = C + FEAT
LOG2E = math.log2(math.e)
SCALE = HD**-0.5 * LOG2E
MASKED = -1e30
UNITS = 18
BF = jnp.bfloat16
F32 = jnp.float32
I32 = jnp.int32
MESH = pl.DeviceIdType.MESH
NT = (((1,), (1,)), ((), ()))
TN = (((0,), (0,)), ((), ()))


def dot(a, b):
    return jnp.dot(a, b, preferred_element_type=F32)


def dot_nt(a, b, precision=None):
    return lax.dot_general(a, b, NT, preferred_element_type=F32, precision=precision)


def token_parts(t):
    half = (t >= 36).astype(I32)
    u = t - 36 * half
    c = (u * 43) >> 7
    return half, c, u - 3 * c


def block_place(t):
    half, c, r = token_parts(t)
    return c * 16 + half * 3 + r


def normed_rows(x, gain):
    mean = jnp.sum(x, axis=-1, keepdims=True) * (1.0 / C)
    d = x - mean
    var = jnp.sum(d * d, axis=-1, keepdims=True) * (1.0 / C)
    return (d * lax.rsqrt(var + 1e-05) * gain).astype(BF).astype(F32)


def kernel(
    nlat,
    nlon,
    tok,
    reg,
    gain_hbm,
    wqkv,
    wproj,
    bias_hbm,
    out,
    xo,
    halo,
    relay,
    lab_own,
    lab_send,
    lab_recv,
    lab_ext,
    lab_t,
    gain,
    bias_raw,
    bias,
    wbuf,
    xn,
    acc,
    xwin,
    pk_top,
    pk_bot,
    qkv,
    ctx,
    head_mask,
    place_in,
    place_out,
    second_owns,
    loc_sem,
    out_sem,
    z_send,
    z_recv,
    plane_send,
    plane_recv,
    sib_send,
    sib_recv,
    leg_send,
    leg_recv,
    halo_send,
    halo_recv,
    lab_ssem,
    lab_rsem,
    lat_send,
    lat_recv,
):
    shard = C // nlon
    plane = nlon // 2
    lat = lax.axis_index("lat")
    lon = lax.axis_index("lon")
    core = lax.rem(lat, 2)
    zhi = lax.rem(lon, 2)
    m = lon // 2
    lat_up = lax.rem(lat + 1, nlat)
    lat_dn = lax.rem(lat + nlat - 1, nlat)
    lon_up = lax.rem(lon + 1, nlon)
    lon_dn = lax.rem(lon + nlon - 1, nlon)
    lon_pair = lon + 1 - 2 * zhi
    lat_mirror = (nlat // 2 - 1 - lat // 2) * 2 + core
    lat_sib = lat + 1 - 2 * core
    nx = min(4, plane)
    ny = plane // nx
    y, x = m // nx, lax.rem(m, nx)

    zlo = nlat // 2
    ring = 2 * zlo
    leg = zlo // 2
    z = zhi * zlo + lat // 2

    def chip_at(column, place):
        place = lax.rem(place + 2 * ring, ring)
        return lax.rem(place, zlo) * 2 + core, column * 2 + place // zlo

    above = chip_at(m, z + leg)
    below = chip_at(m, z - leg)

    def beyond(place, by):
        lat_s, lon_s = chip_at(m, place)
        return lat_s, lax.rem(lon_s + by + nlon, nlon)

    onward = (beyond(z - leg, 1), beyond(z + leg, -1))
    relays_here = (
        chip_at(lon_dn // 2, lax.rem(lon_dn, 2) * zlo + lat // 2 + leg),
        chip_at(lon_up // 2, lax.rem(lon_up, 2) * zlo + lat // 2 - leg),
    )

    own_rows = pl.ds(zhi * shard, shard)

    def quarter_load(k, source):
        return pltpu.make_async_copy(source, wbuf.at[k, y, x, own_rows, :], loc_sem.at[k % 2])

    quarters = (
        (quarter_load(0, wqkv.at[:, 0:C]), quarter_load(1, wqkv.at[:, C : 2 * C])),
        (quarter_load(2, wqkv.at[:, 2 * C : 3 * C]), quarter_load(3, wproj)),
    )
    for c in range(2):

        @pl.when(core == c)
        def _():
            for copy in quarters[c]:
                copy.start()

    loads = [
        pltpu.make_async_copy(reg, lab_own, loc_sem.at[2]),
        pltpu.make_async_copy(tok, xo, loc_sem.at[3]),
        pltpu.make_async_copy(gain_hbm, gain, loc_sem.at[4]),
        pltpu.make_async_copy(bias_hbm, bias_raw, loc_sem.at[5]),
    ]
    for copy in loads:
        copy.start()

    barrier = pltpu.get_barrier_semaphore()
    greeted = (
        (lat, lon_up),
        (lat, lon_dn),
        (lat_up, lon),
        (lat_dn, lon),
        (lat_mirror, lon_pair),
        above,
        below,
    )
    greeted = greeted + relays_here
    for there in greeted:
        pl.semaphore_signal(barrier, inc=1, device_id=there, device_id_type=MESH)

    def greet(d, carry):
        there = (lat, lax.rem(m + d, plane) * 2 + zhi)
        pl.semaphore_signal(barrier, inc=1, device_id=there, device_id_type=MESH)
        return carry

    lax.fori_loop(1, plane, greet, 0)
    pl.semaphore_wait(barrier, len(greeted) + plane - 1)

    def shard_of(half, source, zh):
        rows = pl.ds(zh * shard, shard)
        return wbuf.at[pl.ds(2 * half, 2), source // nx, lax.rem(source, nx), rows, :]

    def mirror_copy(of):
        part = shard_of(core, m, of)
        return pltpu.make_async_remote_copy(
            src_ref=part,
            dst_ref=part,
            send_sem=z_send,
            recv_sem=z_recv,
            device_id=(lat_mirror, lon_pair),
            device_id_type=MESH,
        )

    def plane_copy(k, d, source):
        part = shard_of(core, source, zhi if k == 0 else 1 - zhi)
        return pltpu.make_async_remote_copy(
            src_ref=part,
            dst_ref=part,
            send_sem=plane_send.at[k, d],
            recv_sem=plane_recv.at[k, source],
            device_id=(lat, lax.rem(m + d, plane) * 2 + zhi),
            device_id_type=MESH,
        )

    def sibling_copy(half, source):
        part = wbuf.at[pl.ds(2 * half, 2), source // nx, lax.rem(source, nx)]
        return pltpu.make_async_remote_copy(
            src_ref=part,
            dst_ref=part,
            send_sem=sib_send.at[source],
            recv_sem=sib_recv.at[source],
            device_id=(lat_sib, lon),
            device_id_type=MESH,
        )

    def over_plane(first, body):
        def step(d, carry):
            body(d, lax.rem(m + d, plane))
            return carry

        lax.fori_loop(first, plane, step, 0)

    def pass_on(d, source):
        plane_copy(0, d, source).wait_recv()
        plane_copy(1, d, source).wait_recv()
        sibling_copy(core, source).start()

    for c in range(2):

        @pl.when(core == c)
        def _():
            for copy in quarters[c]:
                copy.wait()

    mirror_copy(zhi).start()

    def leg_copy(side, k):
        rows = pl.ds((0, 32, 16)[k], 16)
        cols = pl.ds(COLS - 6, 6) if side == 0 else pl.ds(0, 6)
        return pltpu.make_async_remote_copy(
            src_ref=tok.at[cols, rows, :],
            dst_ref=relay.at[side, :, rows, :],
            send_sem=leg_send.at[side, k],
            recv_sem=leg_recv.at[side, k],
            device_id=(above, below)[side],
            device_id_type=MESH,
        )

    def halo_copy(side, k):
        rows = pl.ds((0, 32, 16)[k], 16)
        return pltpu.make_async_remote_copy(
            src_ref=relay.at[side, :, rows, :],
            dst_ref=halo.at[side, :, rows, :],
            send_sem=halo_send.at[side, k],
            recv_sem=halo_recv.at[side, k],
            device_id=onward[side],
            device_id_type=MESH,
        )

    def set_out(k):
        for side in range(2):
            leg_copy(side, k).start()

    def forward(k):
        for side in range(2):
            leg_copy(side, k).wait_recv()
            halo_copy(side, k).start()

    def label_copy(side):
        return pltpu.make_async_remote_copy(
            src_ref=lab_send.at[side],
            dst_ref=lab_recv.at[side],
            send_sem=lab_ssem.at[side],
            recv_sem=lab_rsem.at[side],
            device_id=(lat, lon_up if side == 0 else lon_dn),
            device_id_type=MESH,
        )

    loads[0].wait()
    lab_send[...] = jnp.zeros_like(lab_send)
    lab_send[0, 0:6, 0:ROWS] = lab_own[COLS - 6 : COLS, :]
    lab_send[1, 0:6, 0:ROWS] = lab_own[0:6, :]
    set_out(0)
    for side in range(2):
        label_copy(side).start()
    over_plane(1, lambda d, source: plane_copy(0, d, m).start())
    set_out(1)
    set_out(2)

    lane80 = lax.broadcasted_iota(I32, (80, 128), 1)
    for k in range(4):
        head_mask[k] = ((lane80 >= HD * k) & (lane80 < HD * k + HD)).astype(F32).astype(BF)
    t_in = lax.broadcasted_iota(I32, (80, 192), 0)
    place_in[...] = jnp.where(t_in < WIN, block_place(t_in), -1000)
    t_out = lax.broadcasted_iota(I32, (192, 80), 1)
    t_row = lax.broadcasted_iota(I32, (80, 128), 0)
    within = t_row - 36 * (t_row >= 36).astype(I32)
    second_owns[0] = (within < 18).astype(F32)
    second_owns[1] = (t_row < 36).astype(F32)
    for k, (least, most) in enumerate(((0, WIN), (36, WIN), (0, 36))):
        place_out[k] = jnp.where((t_out >= least) & (t_out < most), block_place(t_out), -1000)

    loads[1].wait()
    loads[2].wait()
    loads[3].wait()

    def own_column(c, carry):
        x = xo[c].astype(F32)
        acc[c + 6] = x
        xn[c + 6, :, 0:C] = normed_rows(x, gain[...])
        return carry

    lax.fori_loop(0, COLS // 2, own_column, 0, unroll=2)
    mirror_copy(1 - zhi).wait_recv()
    over_plane(1, lambda d, source: plane_copy(1, d, m).start())
    sibling_copy(core, m).start()
    lax.fori_loop(COLS // 2, COLS, own_column, 0, unroll=2)
    forward(0)

    def place_rows(count):
        half, c, r = token_parts(lax.broadcasted_iota(I32, (count, WIN), 0))
        place = jnp.where(
            lax.broadcasted_iota(I32, (count, WIN), 0) < WIN, (half * 3 + r) * 12 + c, -1
        )
        return (lax.broadcasted_iota(I32, (count, WIN), 1) == place).astype(F32)

    padded = lax.broadcasted_iota(I32, (80, 128), 0) >= WIN

    def bias_of(h, carry):
        keys_first = dot_nt(place_rows(80), bias_raw[h], lax.Precision.HIGHEST)
        placed = dot_nt(keys_first, place_rows(128), lax.Precision.HIGHEST)
        bias[h] = jnp.where(padded, MASKED, placed * LOG2E)
        return carry

    lax.fori_loop(0, HEADS, bias_of, 0, unroll=4)
    forward(1)

    for side in range(2):
        label_copy(side).wait_recv()
    lab_ext[0:6, :] = lab_recv[0, 0:6, 0:ROWS]
    lab_ext[6 : 6 + COLS, :] = lab_own[...]
    lab_ext[6 + COLS : EXT, :] = lab_recv[1, 0:6, 0:ROWS]
    eye = (
        lax.broadcasted_iota(I32, (ROWS, ROWS), 0) == lax.broadcasted_iota(I32, (ROWS, ROWS), 1)
    ).astype(BF)
    low = ((lax.broadcasted_iota(I32, (ROWS, EXT), 0) < 3) & (lat == 0)).astype(F32)
    lab_t[...] = dot_nt(eye, lab_ext[...].astype(F32).astype(BF)) + 3.0 * low

    def features(e, carry):
        lane = lax.broadcasted_iota(I32, (ROWS, EXT), 1)
        code = jnp.sum(jnp.where(lane == e, lab_t[...], 0.0), axis=1, keepdims=True)
        wide = lax.broadcasted_iota(I32, (ROWS, FEAT), 1).astype(F32)
        xn[e, :, C:WIDE] = (wide == code).astype(F32)
        return carry

    lax.fori_loop(0, EXT, features, 0, unroll=4)
    forward(2)
    over_plane(1, pass_on)

    def start_and_offset(i):
        start = 8 * ((13 * i) // 16)
        return start, 3 + 6 * i - start

    lane_in = lax.broadcasted_iota(I32, (80, 192), 1)

    def gather_pair(i, first, second, u):
        start, offset = start_and_offset(i)
        if not isinstance(i, int):
            start = pl.multiple_of(start, 8)
        select = (lane_in - offset == place_in[...]).astype(F32).astype(BF)
        for w, j in enumerate((first, second)):
            block = xn[12 * j : 12 * j + 12, pl.ds(start, 16), :].reshape(192, WIDE).astype(BF)
            xwin[u, 80 * w : 80 * w + 80, :] = dot(select, block).astype(BF)

    def gather_inner(i, carry):
        gather_pair(i, 1, 2, i)
        return carry

    lax.fori_loop(0, 7, gather_inner, 0)

    over_plane(0, lambda d, source: sibling_copy(1 - core, source).wait_recv())

    def halo_chunk(k):
        row = (0, 32, 16)[k]
        for side in range(2):
            halo_copy(side, k).wait_recv()

        def one(c, carry):
            for side in range(2):
                x = halo[side, c, row : row + 16, :].astype(F32)
                xn[c + side * (EXT - 6), row : row + 16, 0:C] = normed_rows(x, gain[...])
            return carry

        lax.fori_loop(0, 6, one, 0)

    def pack(row, offset):
        block = xn[:, row : row + 16, :].reshape(EXT * 16, WIDE).astype(BF)
        u = lax.broadcasted_iota(I32, (144, EXT * 16), 0)
        c = (u * 171) >> 9
        place = c * 16 + (u - 3 * c) + offset
        select = (lax.broadcasted_iota(I32, (144, EXT * 16), 1) == place).astype(F32).astype(BF)
        return dot(select, block).astype(BF)

    def lat_copy(up):
        if up:
            return pltpu.make_async_remote_copy(
                src_ref=pk_bot.at[0:144],
                dst_ref=pk_top.at[0:144],
                send_sem=lat_send.at[0],
                recv_sem=lat_recv.at[0],
                device_id=(lat_up, lon),
                device_id_type=MESH,
            )
        return pltpu.make_async_remote_copy(
            src_ref=pk_top.at[144:288],
            dst_ref=pk_bot.at[144:288],
            send_sem=lat_send.at[1],
            recv_sem=lat_recv.at[1],
            device_id=(lat_dn, lon),
            device_id_type=MESH,
        )

    def gather_edges():
        t = lax.broadcasted_iota(I32, (80, 288), 0)
        lane = lax.broadcasted_iota(I32, (80, 288), 1)
        place = jnp.where(t < WIN, t + 108 * (t >= 36).astype(I32), -1000)
        for j in range(4):
            select = (lane == place + 36 * j).astype(F32).astype(BF)
            for k, rows in enumerate((pk_top, pk_bot)):
                xwin[11 + j, 80 * k : 80 * k + 80, :] = dot(
                    select, rows[...]
                ).astype(BF)

    lane128 = lax.broadcasted_iota(I32, (80, 128), 1)

    def weight(k):
        return wbuf[k].reshape(C, C)

    def project(u):
        both = xwin[u, :, 0:C]
        for part in range(3):
            qkv[:, C * part : C * part + C] = dot(both, weight(part)).astype(BF)

    def mask_features(u, w):
        hot = xwin[u, 80 * w : 80 * w + 80, C:WIDE]
        differs = jnp.where(lane128 < 6, MASKED * (1.0 - hot.astype(F32)), 0.0).astype(BF)
        return hot, differs

    def parts_of(w, g):
        rows = slice(80 * w, 80 * w + 80)
        return (qkv[rows, C * part + 128 * g : C * part + 128 * g + 128] for part in range(3))

    def stack(pieces):
        return jnp.concatenate(
            [jnp.concatenate(pieces(head_mask[k]), axis=1) for k in range(4)], axis=0
        )

    def weights_of(scores, g):
        s = scores.reshape(4, 80, 80) * SCALE + bias[4 * g : 4 * g + 4, :, 0:80]
        e = jnp.exp2(s - jnp.max(s, axis=1, keepdims=True))
        return e.reshape(320, 80).astype(BF)

    def over_keys(e, values):
        return lax.dot_general(e, values, TN, preferred_element_type=F32)

    def attend_two(u):
        project(u)
        for w in range(2):
            hot, differs = mask_features(u, w)
            for g in range(4):
                query, key, value = parts_of(w, g)
                scores = dot_nt(
                    stack(lambda mask: [key * mask, hot]),
                    jnp.concatenate([query, differs], axis=1),
                )
                summed = over_keys(weights_of(scores, g), stack(lambda mask: [value * mask, mask]))
                ctx[80 * w : 80 * w + 80, 128 * g : 128 * g + 128] = (
                    summed[:, 0:128] * (1.0 / summed[:, 128:256])
                ).astype(BF)
        return dot(ctx[...], weight(3)).astype(BF)

    def attend_merged(u, kind):
        project(u)
        of_second = second_owns[kind]
        keep1 = of_second.astype(BF)
        keep0 = (1.0 - of_second).astype(BF)
        hot0, differs0 = mask_features(u, 0)
        hot1, differs1 = mask_features(u, 1)
        differs0 = differs0 * keep0
        differs1 = differs1 * keep1
        for g in range(4):
            query0, key0, value0 = parts_of(0, g)
            query1, key1, value1 = parts_of(1, g)
            scores = dot_nt(
                stack(lambda mask: [key0 * mask, hot0, key1 * mask, hot1]),
                jnp.concatenate([query0 * keep0, differs0, query1 * keep1, differs1], axis=1),
            )
            summed = over_keys(
                weights_of(scores, g), stack(lambda mask: [value0 * mask, value1 * mask, mask])
            )
            own = jnp.where(of_second > 0.5, summed[:, 128:256], summed[:, 0:128])
            ctx[0:80, 128 * g : 128 * g + 128] = (own * (1.0 / summed[:, 256:384])).astype(BF)
        return dot(ctx[0:80, :], weight(3)).astype(BF)

    row_out = lax.broadcasted_iota(I32, (192, 80), 0)

    def add_back(att, j, start, offset, kind):
        select = (row_out - offset == place_out[kind]).astype(F32).astype(BF)
        spot = (pl.ds(12 * j, 12), pl.ds(pl.multiple_of(start, 8), 16), slice(None))
        acc[spot] = acc[spot] + dot(select, att).reshape(12, 16, C)

    def inner_unit(u, carry):
        att = attend_two(u)
        start, offset = start_and_offset(u)
        for w in range(2):
            add_back(att[80 * w : 80 * w + 80], 1 + w, start, offset, 0)
        return carry

    lax.fori_loop(0, 7, inner_unit, 0)

    def finish(c, carry):
        xo[c] = acc[c + 6].astype(BF)
        return carry

    def store(k):
        part = (pl.ds(0, 6), pl.ds(6, COLS - 12), pl.ds(COLS - 6, 6))[k]
        return pltpu.make_async_copy(xo.at[part], out.at[part], out_sem.at[k])

    def merged_unit(v, carry):
        @pl.when(v == 0)
        def _():
            halo_chunk(0)
            pk_top[144:288, :] = pack(0, 0)
            lat_copy(False).start()
            for n in range(2):
                gather_pair(n, 0, 3, 7 + n)

        @pl.when(v == 2)
        def _():
            halo_chunk(1)
            pk_bot[0:144, :] = pack(32, 13)
            lat_copy(True).start()
            for n in range(2):
                gather_pair(5 + n, 0, 3, 9 + n)

        @pl.when(v == 4)
        def _():
            lat_copy(True).wait_recv()
            lat_copy(False).wait_recv()
            gather_edges()

        @pl.when(v == 8)
        def _():
            lax.fori_loop(6, COLS - 6, finish, 0, unroll=3)
            store(1).start()
            halo_chunk(2)
            for n in range(3):
                gather_pair(2 + n, 0, 3, 15 + n)

        edge = ((v >= 4) & (v < 8)).astype(I32)
        att = attend_merged(7 + v, edge)
        i = jnp.where(v < 2, v, jnp.where(v < 4, v + 3, v - 6))
        start, offset = start_and_offset(i)
        for w in range(2):
            j = jnp.where(edge == 1, v - 4, 3 * w)
            add_back(
                att,
                j,
                jnp.where(edge == 1, 32 * w, start),
                jnp.where(edge == 1, 16 * w - 3, offset),
                jnp.where(edge == 1, 1 + w, 0),
            )
        return carry

    lax.fori_loop(0, 11, merged_unit, 0)
    for k, first in ((0, 0), (2, COLS - 6)):
        lax.fori_loop(first, first + 6, finish, 0, unroll=3)
        store(k).start()

    mirror_copy(zhi).wait_send()
    over_plane(1, lambda d, source: plane_copy(0, d, m).wait_send())
    over_plane(1, lambda d, source: plane_copy(1, d, m).wait_send())
    over_plane(0, lambda d, source: sibling_copy(core, source).wait_send())
    for side in range(2):
        label_copy(side).wait_send()
        for k in range(3):
            leg_copy(side, k).wait_send()
            halo_copy(side, k).wait_send()
    lat_copy(True).wait_send()
    lat_copy(False).wait_send()
    for k in range(3):
        store(k).wait()


def local(tokens, region, ln_gain, qkv_weight, proj_weight, position_bias):
    nlat = lax.axis_size("lat")
    nlon = lax.axis_size("lon")
    plane = nlon // 2
    nx = min(4, plane)
    ny = plane // nx
    dma = pltpu.SemaphoreType.DMA
    vm = pltpu.VMEM
    mixed = pl.pallas_call(
        functools.partial(kernel, nlat, nlon),
        out_shape=jax.ShapeDtypeStruct((COLS, ROWS, C), BF),
        in_specs=[pl.BlockSpec(memory_space=pl.ANY)] * 6,
        out_specs=pl.BlockSpec(memory_space=pl.ANY),
        scratch_shapes=[
            vm((COLS, ROWS, C), BF),
            vm((2, 6, ROWS, C), BF),
            vm((2, 6, ROWS, C), BF),
            vm((COLS, ROWS), I32),
            vm((2, 8, 128), I32),
            vm((2, 8, 128), I32),
            vm((EXT, ROWS), I32),
            vm((ROWS, EXT), F32),
            vm((1, C), F32),
            vm((HEADS, WIN, WIN), F32),
            vm((HEADS, 80, 128), F32),
            vm((4, ny, nx, 2 * (C // nlon), C), BF),
            vm((EXT, ROWS, WIDE), F32),
            vm((EXT, ROWS, C), F32),
            vm((UNITS, 160, WIDE), BF),
            vm((288, WIDE), BF),
            vm((288, WIDE), BF),
            vm((160, 3 * C), BF),
            vm((160, C), BF),
            vm((4, 80, 128), BF),
            vm((80, 192), I32),
            vm((3, 192, 80), I32),
            vm((2, 80, 128), F32),
            dma((6,)),
            dma((4,)),
            dma,
            dma,
            dma((2, plane)),
            dma((2, plane)),
            dma((plane,)),
            dma((plane,)),
            dma((2, 3)),
            dma((2, 3)),
            dma((2, 3)),
            dma((2, 3)),
            dma((2,)),
            dma((2,)),
            dma((2,)),
            dma((2,)),
        ],
        compiler_params=pltpu.CompilerParams(
            collective_id=0, has_side_effects=True, vmem_limit_bytes=56 * 2**20
        ),
        cost_estimate=pl.CostEstimate(
            flops=8_000_000_000, bytes_accessed=12_000_000, transcendentals=6_000_000
        ),
    )(
        jnp.transpose(tokens, (1, 0, 2)),
        jnp.transpose(region, (1, 0)),
        ln_gain.reshape(1, C),
        qkv_weight,
        proj_weight,
        position_bias,
    )
    return jnp.transpose(mixed, (1, 0, 2))


def solution(mesh):
    return jax.shard_map(
        local,
        mesh=mesh,
        in_specs=(P("lat", "lon", None), P("lat", "lon"), P(), P("lon", None), P("lon", None), P()),
        out_specs=P("lat", "lon", None),
        check_vma=False,
    )
```

```python
import functools
import math

import jax
import jax.numpy as jnp
from jax import lax
from jax.experimental import pallas as pl
from jax.experimental.pallas import tpu as pltpu
from jax.sharding import PartitionSpec as P

HEADS = 16
HD = 32
C = 512
WIN = 72
ROWS = 48
COLS = 36
EXT = 48
FEAT = 128
WIDE = C + FEAT
LOG2E = math.log2(math.e)
SCALE = HD**-0.5 * LOG2E
MASKED = -1e30
UNITS = 18
BF = jnp.bfloat16
F32 = jnp.float32
I32 = jnp.int32
MESH = pl.DeviceIdType.MESH
NT = (((1,), (1,)), ((), ()))
TN = (((0,), (0,)), ((), ()))


def dot(a, b):
    return jnp.dot(a, b, preferred_element_type=F32)


def dot_nt(a, b, precision=None):
    return lax.dot_general(a, b, NT, preferred_element_type=F32, precision=precision)


def token_parts(t):
    half = (t >= 36).astype(I32)
    u = t - 36 * half
    c = (u * 43) >> 7
    return half, c, u - 3 * c


def block_place(t):
    half, c, r = token_parts(t)
    return c * 16 + half * 3 + r


def normed_rows(x, gain):
    mean = jnp.sum(x, axis=-1, keepdims=True) * (1.0 / C)
    d = x - mean
    var = jnp.sum(d * d, axis=-1, keepdims=True) * (1.0 / C)
    return (d * lax.rsqrt(var + 1e-05) * gain).astype(BF).astype(F32)


def kernel(
    nlat,
    nlon,
    tok,
    reg,
    gain_hbm,
    wqkv,
    wproj,
    bias_hbm,
    out,
    xo,
    halo,
    relay,
    lab_own,
    lab_send,
    lab_recv,
    lab_ext,
    lab_t,
    gain,
    bias_raw,
    bias,
    wbuf,
    xn,
    acc,
    xwin,
    pk_top,
    pk_bot,
    qkv,
    ctx,
    head_mask,
    place_in,
    place_out,
    second_owns,
    loc_sem,
    out_sem,
    z_send,
    z_recv,
    fan_send,
    plane_send,
    plane_recv,
    sib_send,
    sib_recv,
    leg_send,
    leg_recv,
    halo_send,
    halo_recv,
    lab_ssem,
    lab_rsem,
    lat_send,
    lat_recv,
):
    shard = C // nlon
    plane = nlon // 2
    lat = lax.axis_index("lat")
    lon = lax.axis_index("lon")
    core = lax.rem(lat, 2)
    zhi = lax.rem(lon, 2)
    m = lon // 2
    lat_up = lax.rem(lat + 1, nlat)
    lat_dn = lax.rem(lat + nlat - 1, nlat)
    lon_up = lax.rem(lon + 1, nlon)
    lon_dn = lax.rem(lon + nlon - 1, nlon)
    lon_pair = lon + 1 - 2 * zhi
    lat_mirror = (nlat // 2 - 1 - lat // 2) * 2 + core
    lat_sib = lat + 1 - 2 * core
    nx = min(4, plane)
    ny = plane // nx
    y, x = m // nx, lax.rem(m, nx)

    zlo = nlat // 2
    ring = 2 * zlo
    leg = zlo // 2
    z = zhi * zlo + lat // 2

    def chip_at(column, place):
        place = lax.rem(place + 2 * ring, ring)
        return lax.rem(place, zlo) * 2 + core, column * 2 + place // zlo

    zedge = (1 - zhi) * (zlo - 1)
    lat_edge = zedge * 2 + core
    at_edge = lat == lat_edge

    above = chip_at(m, z + leg)
    below = chip_at(m, z - leg)

    def beyond(place, by):
        lat_s, lon_s = chip_at(m, place)
        return lat_s, lax.rem(lon_s + by + nlon, nlon)

    onward = (beyond(z - leg, 1), beyond(z + leg, -1))
    relays_here = (
        chip_at(lon_dn // 2, lax.rem(lon_dn, 2) * zlo + lat // 2 + leg),
        chip_at(lon_up // 2, lax.rem(lon_up, 2) * zlo + lat // 2 - leg),
    )

    own_rows = pl.ds(zhi * shard, shard)

    def quarter_load(k, source):
        return pltpu.make_async_copy(source, wbuf.at[k, y, x, own_rows, :], loc_sem.at[k % 2])

    quarters = (
        (quarter_load(0, wqkv.at[:, 0:C]), quarter_load(1, wqkv.at[:, C : 2 * C])),
        (quarter_load(2, wqkv.at[:, 2 * C : 3 * C]), quarter_load(3, wproj)),
    )
    for c in range(2):

        @pl.when(core == c)
        def _():
            for copy in quarters[c]:
                copy.start()

    loads = [
        pltpu.make_async_copy(reg, lab_own, loc_sem.at[2]),
        pltpu.make_async_copy(tok, xo, loc_sem.at[3]),
        pltpu.make_async_copy(gain_hbm, gain, loc_sem.at[4]),
        pltpu.make_async_copy(bias_hbm, bias_raw, loc_sem.at[5]),
    ]
    for copy in loads:
        copy.start()

    barrier = pltpu.get_barrier_semaphore()
    greeted = (
        (lat, lon_up),
        (lat, lon_dn),
        (lat_up, lon),
        (lat_dn, lon),
        (jnp.where(at_edge, lat_mirror, lat_edge), jnp.where(at_edge, lon_pair, lon)),
        above,
        below,
    )
    greeted = greeted + relays_here
    for there in greeted:
        pl.semaphore_signal(barrier, inc=1, device_id=there, device_id_type=MESH)

    def greet(d, carry):
        there = (lat, lax.rem(m + d, plane) * 2 + zhi)
        pl.semaphore_signal(barrier, inc=1, device_id=there, device_id_type=MESH)
        return carry

    lax.fori_loop(1, plane, greet, 0)
    pl.semaphore_wait(barrier, len(greeted) - 1 + plane - 1 + zlo * at_edge.astype(I32))

    def shard_of(half, source, zh):
        rows = pl.ds(zh * shard, shard)
        return wbuf.at[pl.ds(2 * half, 2), source // nx, lax.rem(source, nx), rows, :]

    def mirror_copy(of):
        part = shard_of(core, m, of)
        return pltpu.make_async_remote_copy(
            src_ref=part,
            dst_ref=part,
            send_sem=z_send,
            recv_sem=z_recv,
            device_id=(lat_mirror, lon_pair),
            device_id_type=MESH,
        )

    def fan_copy(d):
        part = shard_of(core, m, 1 - zhi)
        return pltpu.make_async_remote_copy(
            src_ref=part,
            dst_ref=part,
            send_sem=fan_send.at[d],
            recv_sem=z_recv,
            device_id=(lax.rem(zedge + d, zlo) * 2 + core, lon),
            device_id_type=MESH,
        )

    def plane_copy(k, d, source):
        part = shard_of(core, source, zhi if k == 0 else 1 - zhi)
        return pltpu.make_async_remote_copy(
            src_ref=part,
            dst_ref=part,
            send_sem=plane_send.at[k, d],
            recv_sem=plane_recv.at[k, source],
            device_id=(lat, lax.rem(m + d, plane) * 2 + zhi),
            device_id_type=MESH,
        )

    def sibling_copy(half, source):
        part = wbuf.at[pl.ds(2 * half, 2), source // nx, lax.rem(source, nx)]
        return pltpu.make_async_remote_copy(
            src_ref=part,
            dst_ref=part,
            send_sem=sib_send.at[source],
            recv_sem=sib_recv.at[source],
            device_id=(lat_sib, lon),
            device_id_type=MESH,
        )

    def over_plane(first, body):
        def step(d, carry):
            body(d, lax.rem(m + d, plane))
            return carry

        lax.fori_loop(first, plane, step, 0)

    def pass_on(d, source):
        plane_copy(0, d, source).wait_recv()
        plane_copy(1, d, source).wait_recv()
        sibling_copy(core, source).start()

    def leg_copy(side, k):
        rows = pl.ds((0, 32, 16)[k], 16)
        cols = pl.ds(COLS - 6, 6) if side == 0 else pl.ds(0, 6)
        return pltpu.make_async_remote_copy(
            src_ref=tok.at[cols, rows, :],
            dst_ref=relay.at[side, :, rows, :],
            send_sem=leg_send.at[side, k],
            recv_sem=leg_recv.at[side, k],
            device_id=(above, below)[side],
            device_id_type=MESH,
        )

    def halo_copy(side, k):
        rows = pl.ds((0, 32, 16)[k], 16)
        return pltpu.make_async_remote_copy(
            src_ref=relay.at[side, :, rows, :],
            dst_ref=halo.at[side, :, rows, :],
            send_sem=halo_send.at[side, k],
            recv_sem=halo_recv.at[side, k],
            device_id=onward[side],
            device_id_type=MESH,
        )

    def set_out(k):
        for side in range(2):
            leg_copy(side, k).start()

    def forward(k):
        for side in range(2):
            leg_copy(side, k).wait_recv()
            halo_copy(side, k).start()

    set_out(0)

    for c in range(2):

        @pl.when(core == c)
        def _():
            for copy in quarters[c]:
                copy.wait()

    @pl.when(at_edge)
    def _():
        mirror_copy(zhi).start()


    def label_copy(side):
        return pltpu.make_async_remote_copy(
            src_ref=lab_send.at[side],
            dst_ref=lab_recv.at[side],
            send_sem=lab_ssem.at[side],
            recv_sem=lab_rsem.at[side],
            device_id=(lat, lon_up if side == 0 else lon_dn),
            device_id_type=MESH,
        )

    loads[0].wait()
    lab_send[...] = jnp.zeros_like(lab_send)
    lab_send[0, 0:6, 0:ROWS] = lab_own[COLS - 6 : COLS, :]
    lab_send[1, 0:6, 0:ROWS] = lab_own[0:6, :]
    for side in range(2):
        label_copy(side).start()
    over_plane(1, lambda d, source: plane_copy(0, d, m).start())
    set_out(1)
    set_out(2)

    lane80 = lax.broadcasted_iota(I32, (80, 128), 1)
    for k in range(4):
        head_mask[k] = ((lane80 >= HD * k) & (lane80 < HD * k + HD)).astype(F32).astype(BF)
    t_in = lax.broadcasted_iota(I32, (80, 192), 0)
    place_in[...] = jnp.where(t_in < WIN, block_place(t_in), -1000)
    t_out = lax.broadcasted_iota(I32, (192, 80), 1)
    t_row = lax.broadcasted_iota(I32, (80, 128), 0)
    within = t_row - 36 * (t_row >= 36).astype(I32)
    second_owns[0] = (within < 18).astype(F32)
    second_owns[1] = (t_row < 36).astype(F32)
    for k, (least, most) in enumerate(((0, WIN), (36, WIN), (0, 36))):
        place_out[k] = jnp.where((t_out >= least) & (t_out < most), block_place(t_out), -1000)

    loads[1].wait()
    loads[2].wait()
    loads[3].wait()

    def own_column(c, carry):
        x = xo[c].astype(F32)
        acc[c + 6] = x
        xn[c + 6, :, 0:C] = normed_rows(x, gain[...])
        return carry

    lax.fori_loop(0, COLS // 2, own_column, 0, unroll=2)
    mirror_copy(1 - zhi).wait_recv()

    @pl.when(at_edge)
    def _():
        for d in range(1, zlo):
            fan_copy(d).start()

    over_plane(1, lambda d, source: plane_copy(1, d, m).start())
    sibling_copy(core, m).start()
    lax.fori_loop(COLS // 2, COLS, own_column, 0, unroll=2)
    forward(0)

    def place_rows(count):
        half, c, r = token_parts(lax.broadcasted_iota(I32, (count, WIN), 0))
        place = jnp.where(
            lax.broadcasted_iota(I32, (count, WIN), 0) < WIN, (half * 3 + r) * 12 + c, -1
        )
        return (lax.broadcasted_iota(I32, (count, WIN), 1) == place).astype(F32)

    padded = lax.broadcasted_iota(I32, (80, 128), 0) >= WIN

    def bias_of(h, carry):
        keys_first = dot_nt(place_rows(80), bias_raw[h], lax.Precision.HIGHEST)
        placed = dot_nt(keys_first, place_rows(128), lax.Precision.HIGHEST)
        bias[h] = jnp.where(padded, MASKED, placed * LOG2E)
        return carry

    lax.fori_loop(0, HEADS, bias_of, 0, unroll=4)
    forward(1)

    for side in range(2):
        label_copy(side).wait_recv()
    lab_ext[0:6, :] = lab_recv[0, 0:6, 0:ROWS]
    lab_ext[6 : 6 + COLS, :] = lab_own[...]
    lab_ext[6 + COLS : EXT, :] = lab_recv[1, 0:6, 0:ROWS]
    eye = (
        lax.broadcasted_iota(I32, (ROWS, ROWS), 0) == lax.broadcasted_iota(I32, (ROWS, ROWS), 1)
    ).astype(BF)
    low = ((lax.broadcasted_iota(I32, (ROWS, EXT), 0) < 3) & (lat == 0)).astype(F32)
    lab_t[...] = dot_nt(eye, lab_ext[...].astype(F32).astype(BF)) + 3.0 * low

    def features(e, carry):
        lane = lax.broadcasted_iota(I32, (ROWS, EXT), 1)
        code = jnp.sum(jnp.where(lane == e, lab_t[...], 0.0), axis=1, keepdims=True)
        wide = lax.broadcasted_iota(I32, (ROWS, FEAT), 1).astype(F32)
        xn[e, :, C:WIDE] = (wide == code).astype(F32)
        return carry

    lax.fori_loop(0, EXT, features, 0, unroll=4)
    forward(2)
    over_plane(1, pass_on)

    def start_and_offset(i):
        start = 8 * ((13 * i) // 16)
        return start, 3 + 6 * i - start

    lane_in = lax.broadcasted_iota(I32, (80, 192), 1)

    def gather_pair(i, first, second, u):
        start, offset = start_and_offset(i)
        if not isinstance(i, int):
            start = pl.multiple_of(start, 8)
        select = (lane_in - offset == place_in[...]).astype(F32).astype(BF)
        for w, j in enumerate((first, second)):
            block = xn[12 * j : 12 * j + 12, pl.ds(start, 16), :].reshape(192, WIDE).astype(BF)
            xwin[u, 80 * w : 80 * w + 80, :] = dot(select, block).astype(BF)

    def gather_inner(i, carry):
        gather_pair(i, 1, 2, i)
        return carry

    lax.fori_loop(0, 7, gather_inner, 0)

    over_plane(0, lambda d, source: sibling_copy(1 - core, source).wait_recv())

    def halo_chunk(k):
        row = (0, 32, 16)[k]
        for side in range(2):
            halo_copy(side, k).wait_recv()

        def one(c, carry):
            for side in range(2):
                x = halo[side, c, row : row + 16, :].astype(F32)
                xn[c + side * (EXT - 6), row : row + 16, 0:C] = normed_rows(x, gain[...])
            return carry

        lax.fori_loop(0, 6, one, 0, unroll=3)

    def pack(row, offset):
        block = xn[:, row : row + 16, :].reshape(EXT * 16, WIDE).astype(BF)
        u = lax.broadcasted_iota(I32, (144, EXT * 16), 0)
        c = (u * 171) >> 9
        place = c * 16 + (u - 3 * c) + offset
        select = (lax.broadcasted_iota(I32, (144, EXT * 16), 1) == place).astype(F32).astype(BF)
        return dot(select, block).astype(BF)

    def lat_copy(up):
        if up:
            return pltpu.make_async_remote_copy(
                src_ref=pk_bot.at[0:144],
                dst_ref=pk_top.at[0:144],
                send_sem=lat_send.at[0],
                recv_sem=lat_recv.at[0],
                device_id=(lat_up, lon),
                device_id_type=MESH,
            )
        return pltpu.make_async_remote_copy(
            src_ref=pk_top.at[144:288],
            dst_ref=pk_bot.at[144:288],
            send_sem=lat_send.at[1],
            recv_sem=lat_recv.at[1],
            device_id=(lat_dn, lon),
            device_id_type=MESH,
        )

    def gather_edges():
        t = lax.broadcasted_iota(I32, (80, 288), 0)
        lane = lax.broadcasted_iota(I32, (80, 288), 1)
        place = jnp.where(t < WIN, t + 108 * (t >= 36).astype(I32), -1000)
        for j in range(4):
            select = (lane == place + 36 * j).astype(F32).astype(BF)
            for k, rows in enumerate((pk_top, pk_bot)):
                xwin[11 + j, 80 * k : 80 * k + 80, :] = dot(
                    select, rows[...]
                ).astype(BF)

    lane128 = lax.broadcasted_iota(I32, (80, 128), 1)

    def weight(k):
        return wbuf[k].reshape(C, C)

    def project(u):
        both = xwin[u, :, 0:C]
        for part in range(3):
            qkv[:, C * part : C * part + C] = dot(both, weight(part)).astype(BF)

    def mask_features(u, w):
        hot = xwin[u, 80 * w : 80 * w + 80, C:WIDE]
        differs = jnp.where(lane128 < 6, MASKED * (1.0 - hot.astype(F32)), 0.0).astype(BF)
        return hot, differs

    def parts_of(w, g):
        rows = slice(80 * w, 80 * w + 80)
        return (qkv[rows, C * part + 128 * g : C * part + 128 * g + 128] for part in range(3))

    def stack(pieces):
        return jnp.concatenate(
            [jnp.concatenate(pieces(head_mask[k]), axis=1) for k in range(4)], axis=0
        )

    def weights_of(scores, g):
        s = scores.reshape(4, 80, 80) * SCALE + bias[4 * g : 4 * g + 4, :, 0:80]
        e = jnp.exp2(s - jnp.max(s, axis=1, keepdims=True))
        return e.reshape(320, 80).astype(BF)

    def over_keys(e, values):
        return lax.dot_general(e, values, TN, preferred_element_type=F32)

    def attend_two(u):
        project(u)
        for w in range(2):
            hot, differs = mask_features(u, w)
            for g in range(4):
                query, key, value = parts_of(w, g)
                scores = dot_nt(
                    stack(lambda mask: [key * mask, hot]),
                    jnp.concatenate([query, differs], axis=1),
                )
                summed = over_keys(weights_of(scores, g), stack(lambda mask: [value * mask, mask]))
                ctx[80 * w : 80 * w + 80, 128 * g : 128 * g + 128] = (
                    summed[:, 0:128] * (1.0 / summed[:, 128:256])
                ).astype(BF)
        return dot(ctx[...], weight(3)).astype(BF)

    def attend_merged(u, kind):
        project(u)
        of_second = second_owns[kind]
        keep1 = of_second.astype(BF)
        keep0 = (1.0 - of_second).astype(BF)
        hot0, differs0 = mask_features(u, 0)
        hot1, differs1 = mask_features(u, 1)
        differs0 = differs0 * keep0
        differs1 = differs1 * keep1
        for g in range(4):
            query0, key0, value0 = parts_of(0, g)
            query1, key1, value1 = parts_of(1, g)
            scores = dot_nt(
                stack(lambda mask: [key0 * mask, hot0, key1 * mask, hot1]),
                jnp.concatenate([query0 * keep0, differs0, query1 * keep1, differs1], axis=1),
            )
            summed = over_keys(
                weights_of(scores, g), stack(lambda mask: [value0 * mask, value1 * mask, mask])
            )
            own = jnp.where(of_second > 0.5, summed[:, 128:256], summed[:, 0:128])
            ctx[0:80, 128 * g : 128 * g + 128] = (own * (1.0 / summed[:, 256:384])).astype(BF)
        return dot(ctx[0:80, :], weight(3)).astype(BF)

    row_out = lax.broadcasted_iota(I32, (192, 80), 0)

    def add_back(att, j, start, offset, kind):
        select = (row_out - offset == place_out[kind]).astype(F32).astype(BF)
        spot = (pl.ds(12 * j, 12), pl.ds(pl.multiple_of(start, 8), 16), slice(None))
        acc[spot] = acc[spot] + dot(select, att).reshape(12, 16, C)

    def inner_unit(u, carry):
        att = attend_two(u)
        start, offset = start_and_offset(u)
        for w in range(2):
            add_back(att[80 * w : 80 * w + 80], 1 + w, start, offset, 0)
        return carry

    lax.fori_loop(0, 7, inner_unit, 0)

    def finish(c, carry):
        xo[c] = acc[c + 6].astype(BF)
        return carry

    def store(k):
        part = (pl.ds(0, 6), pl.ds(6, COLS - 12), pl.ds(COLS - 6, 6))[k]
        return pltpu.make_async_copy(xo.at[part], out.at[part], out_sem.at[k])

    def merged_unit(v, carry):
        @pl.when(v == 0)
        def _():
            halo_chunk(0)
            pk_top[144:288, :] = pack(0, 0)
            lat_copy(False).start()
            for n in range(2):
                gather_pair(n, 0, 3, 7 + n)

        @pl.when(v == 2)
        def _():
            halo_chunk(1)
            pk_bot[0:144, :] = pack(32, 13)
            lat_copy(True).start()
            for n in range(2):
                gather_pair(5 + n, 0, 3, 9 + n)

        @pl.when(v == 4)
        def _():
            lat_copy(True).wait_recv()
            lat_copy(False).wait_recv()
            gather_edges()

        @pl.when(v == 8)
        def _():
            lax.fori_loop(6, COLS - 6, finish, 0, unroll=3)
            store(1).start()
            halo_chunk(2)
            for n in range(3):
                gather_pair(2 + n, 0, 3, 15 + n)

        edge = ((v >= 4) & (v < 8)).astype(I32)
        att = attend_merged(7 + v, edge)
        i = jnp.where(v < 2, v, jnp.where(v < 4, v + 3, v - 6))
        start, offset = start_and_offset(i)
        for w in range(2):
            j = jnp.where(edge == 1, v - 4, 3 * w)
            add_back(
                att,
                j,
                jnp.where(edge == 1, 32 * w, start),
                jnp.where(edge == 1, 16 * w - 3, offset),
                jnp.where(edge == 1, 1 + w, 0),
            )
        return carry

    lax.fori_loop(0, 11, merged_unit, 0)
    for k, first in ((0, 0), (2, COLS - 6)):
        lax.fori_loop(first, first + 6, finish, 0, unroll=3)
        store(k).start()

    @pl.when(at_edge)
    def _():
        mirror_copy(zhi).wait_send()
        for d in range(1, zlo):
            fan_copy(d).wait_send()

    over_plane(1, lambda d, source: plane_copy(0, d, m).wait_send())
    over_plane(1, lambda d, source: plane_copy(1, d, m).wait_send())
    over_plane(0, lambda d, source: sibling_copy(core, source).wait_send())
    for side in range(2):
        label_copy(side).wait_send()
        for k in range(3):
            leg_copy(side, k).wait_send()
            halo_copy(side, k).wait_send()
    lat_copy(True).wait_send()
    lat_copy(False).wait_send()
    for k in range(3):
        store(k).wait()


def local(tokens, region, ln_gain, qkv_weight, proj_weight, position_bias):
    nlat = lax.axis_size("lat")
    nlon = lax.axis_size("lon")
    plane = nlon // 2
    nx = min(4, plane)
    ny = plane // nx
    dma = pltpu.SemaphoreType.DMA
    vm = pltpu.VMEM
    mixed = pl.pallas_call(
        functools.partial(kernel, nlat, nlon),
        out_shape=jax.ShapeDtypeStruct((COLS, ROWS, C), BF),
        in_specs=[pl.BlockSpec(memory_space=pl.ANY)] * 6,
        out_specs=pl.BlockSpec(memory_space=pl.ANY),
        scratch_shapes=[
            vm((COLS, ROWS, C), BF),
            vm((2, 6, ROWS, C), BF),
            vm((2, 6, ROWS, C), BF),
            vm((COLS, ROWS), I32),
            vm((2, 8, 128), I32),
            vm((2, 8, 128), I32),
            vm((EXT, ROWS), I32),
            vm((ROWS, EXT), F32),
            vm((1, C), F32),
            vm((HEADS, WIN, WIN), F32),
            vm((HEADS, 80, 128), F32),
            vm((4, ny, nx, 2 * (C // nlon), C), BF),
            vm((EXT, ROWS, WIDE), F32),
            vm((EXT, ROWS, C), F32),
            vm((UNITS, 160, WIDE), BF),
            vm((288, WIDE), BF),
            vm((288, WIDE), BF),
            vm((160, 3 * C), BF),
            vm((160, C), BF),
            vm((4, 80, 128), BF),
            vm((80, 192), I32),
            vm((3, 192, 80), I32),
            vm((2, 80, 128), F32),
            dma((6,)),
            dma((4,)),
            dma,
            dma,
            dma((nlat // 2,)),
            dma((2, plane)),
            dma((2, plane)),
            dma((plane,)),
            dma((plane,)),
            dma((2, 3)),
            dma((2, 3)),
            dma((2, 3)),
            dma((2, 3)),
            dma((2,)),
            dma((2,)),
            dma((2,)),
            dma((2,)),
        ],
        compiler_params=pltpu.CompilerParams(
            collective_id=0, has_side_effects=True, vmem_limit_bytes=56 * 2**20
        ),
        cost_estimate=pl.CostEstimate(
            flops=8_000_000_000, bytes_accessed=12_000_000, transcendentals=6_000_000
        ),
    )(
        jnp.transpose(tokens, (1, 0, 2)),
        jnp.transpose(region, (1, 0)),
        ln_gain.reshape(1, C),
        qkv_weight,
        proj_weight,
        position_bias,
    )
    return jnp.transpose(mixed, (1, 0, 2))


def solution(mesh):
    return jax.shard_map(
        local,
        mesh=mesh,
        in_specs=(P("lat", "lon", None), P("lat", "lon"), P(), P("lon", None), P("lon", None), P()),
        out_specs=P("lat", "lon", None),
        check_vma=False,
    )
```

```python
import functools
import math

import jax
import jax.numpy as jnp
from jax import lax
from jax.experimental import pallas as pl
from jax.experimental.pallas import tpu as pltpu
from jax.sharding import PartitionSpec as P

HEADS = 16
HD = 32
C = 512
WIN = 72
ROWS = 48
COLS = 36
EXT = 48
FEAT = 128
WIDE = C + FEAT
LOG2E = math.log2(math.e)
SCALE = HD**-0.5 * LOG2E
MASKED = -1e30
UNITS = 18
BF = jnp.bfloat16
F32 = jnp.float32
I32 = jnp.int32
MESH = pl.DeviceIdType.MESH
NT = (((1,), (1,)), ((), ()))
TN = (((0,), (0,)), ((), ()))


def dot(a, b):
    return jnp.dot(a, b, preferred_element_type=F32)


def dot_nt(a, b, precision=None):
    return lax.dot_general(a, b, NT, preferred_element_type=F32, precision=precision)


def token_parts(t):
    half = (t >= 36).astype(I32)
    u = t - 36 * half
    c = (u * 43) >> 7
    return half, c, u - 3 * c


def block_place(t):
    half, c, r = token_parts(t)
    return c * 16 + half * 3 + r


def normed_rows(x, gain):
    mean = jnp.sum(x, axis=-1, keepdims=True) * (1.0 / C)
    d = x - mean
    var = jnp.sum(d * d, axis=-1, keepdims=True) * (1.0 / C)
    return (d * lax.rsqrt(var + 1e-05) * gain).astype(BF).astype(F32)


def kernel(
    nlat,
    nlon,
    tok,
    reg,
    gain_hbm,
    wqkv,
    wproj,
    bias_hbm,
    out,
    xo,
    halo,
    relay,
    lab_own,
    lab_send,
    lab_recv,
    lab_ext,
    lab_t,
    gain,
    bias_raw,
    bias,
    wbuf,
    xn,
    acc,
    xwin,
    pk_top,
    pk_bot,
    qkv,
    ctx,
    head_mask,
    place_in,
    place_out,
    second_owns,
    loc_sem,
    out_sem,
    z_send,
    z_recv,
    plane_send,
    plane_recv,
    sib_send,
    sib_recv,
    leg_send,
    leg_recv,
    halo_send,
    halo_recv,
    lab_ssem,
    lab_rsem,
    lat_send,
    lat_recv,
):
    shard = C // nlon
    plane = nlon // 2
    lat = lax.axis_index("lat")
    lon = lax.axis_index("lon")
    core = lax.rem(lat, 2)
    zhi = lax.rem(lon, 2)
    m = lon // 2
    lat_up = lax.rem(lat + 1, nlat)
    lat_dn = lax.rem(lat + nlat - 1, nlat)
    lon_up = lax.rem(lon + 1, nlon)
    lon_dn = lax.rem(lon + nlon - 1, nlon)
    lon_pair = lon + 1 - 2 * zhi
    lat_mirror = (nlat // 2 - 1 - lat // 2) * 2 + core
    lat_sib = lat + 1 - 2 * core
    nx = min(4, plane)
    ny = plane // nx
    y, x = m // nx, lax.rem(m, nx)

    zlo = nlat // 2
    ring = 2 * zlo
    leg = zlo // 2
    z = zhi * zlo + lat // 2

    def chip_at(column, place):
        place = lax.rem(place + 2 * ring, ring)
        return lax.rem(place, zlo) * 2 + core, column * 2 + place // zlo

    above = chip_at(m, z + leg)
    below = chip_at(m, z - leg)

    def beyond(place, by):
        lat_s, lon_s = chip_at(m, place)
        return lat_s, lax.rem(lon_s + by + nlon, nlon)

    onward = (beyond(z - leg, 1), beyond(z + leg, -1))
    relays_here = (
        chip_at(lon_dn // 2, lax.rem(lon_dn, 2) * zlo + lat // 2 + leg),
        chip_at(lon_up // 2, lax.rem(lon_up, 2) * zlo + lat // 2 - leg),
    )

    own_rows = pl.ds(zhi * shard, shard)

    def quarter_load(k, source):
        return pltpu.make_async_copy(source, wbuf.at[k, y, x, own_rows, :], loc_sem.at[k % 2])

    quarters = (
        (quarter_load(0, wqkv.at[:, 0:C]), quarter_load(1, wqkv.at[:, C : 2 * C])),
        (quarter_load(2, wqkv.at[:, 2 * C : 3 * C]), quarter_load(3, wproj)),
    )
    for c in range(2):

        @pl.when(core == c)
        def _():
            for copy in quarters[c]:
                copy.start()

    loads = [
        pltpu.make_async_copy(reg, lab_own, loc_sem.at[2]),
        pltpu.make_async_copy(tok, xo, loc_sem.at[3]),
        pltpu.make_async_copy(gain_hbm, gain, loc_sem.at[4]),
        pltpu.make_async_copy(bias_hbm, bias_raw, loc_sem.at[5]),
    ]
    for copy in loads:
        copy.start()

    barrier = pltpu.get_barrier_semaphore()
    greeted = (
        (lat, lon_up),
        (lat, lon_dn),
        (lat_up, lon),
        (lat_dn, lon),
        (lat_mirror, lon_pair),
        above,
        below,
    )
    greeted = greeted + relays_here
    for there in greeted:
        pl.semaphore_signal(barrier, inc=1, device_id=there, device_id_type=MESH)

    def greet(d, carry):
        there = (lat, lax.rem(m + d, plane) * 2 + zhi)
        pl.semaphore_signal(barrier, inc=1, device_id=there, device_id_type=MESH)
        return carry

    lax.fori_loop(1, plane, greet, 0)
    pl.semaphore_wait(barrier, len(greeted) + plane - 1)

    def shard_of(half, source, zh):
        rows = pl.ds(zh * shard, shard)
        return wbuf.at[pl.ds(2 * half, 2), source // nx, lax.rem(source, nx), rows, :]

    def mirror_copy(of):
        part = shard_of(core, m, of)
        return pltpu.make_async_remote_copy(
            src_ref=part,
            dst_ref=part,
            send_sem=z_send,
            recv_sem=z_recv,
            device_id=(lat_mirror, lon_pair),
            device_id_type=MESH,
        )

    def plane_copy(k, d, source):
        part = shard_of(core, source, zhi if k == 0 else 1 - zhi)
        return pltpu.make_async_remote_copy(
            src_ref=part,
            dst_ref=part,
            send_sem=plane_send.at[k, d],
            recv_sem=plane_recv.at[k, source],
            device_id=(lat, lax.rem(m + d, plane) * 2 + zhi),
            device_id_type=MESH,
        )

    def sibling_copy(half, source):
        part = wbuf.at[pl.ds(2 * half, 2), source // nx, lax.rem(source, nx)]
        return pltpu.make_async_remote_copy(
            src_ref=part,
            dst_ref=part,
            send_sem=sib_send.at[source],
            recv_sem=sib_recv.at[source],
            device_id=(lat_sib, lon),
            device_id_type=MESH,
        )

    def over_plane(first, body):
        def step(d, carry):
            body(d, lax.rem(m + d, plane))
            return carry

        lax.fori_loop(first, plane, step, 0)

    def pass_on(d, source):
        plane_copy(0, d, source).wait_recv()
        plane_copy(1, d, source).wait_recv()
        sibling_copy(core, source).start()

    for c in range(2):

        @pl.when(core == c)
        def _():
            for copy in quarters[c]:
                copy.wait()

    mirror_copy(zhi).start()

    def leg_copy(side, k):
        rows = pl.ds((0, 32, 16)[k], 16)
        cols = pl.ds(COLS - 6, 6) if side == 0 else pl.ds(0, 6)
        return pltpu.make_async_remote_copy(
            src_ref=tok.at[cols, rows, :],
            dst_ref=relay.at[side, :, rows, :],
            send_sem=leg_send.at[side, k],
            recv_sem=leg_recv.at[side, k],
            device_id=(above, below)[side],
            device_id_type=MESH,
        )

    def halo_copy(side, k):
        rows = pl.ds((0, 32, 16)[k], 16)
        return pltpu.make_async_remote_copy(
            src_ref=relay.at[side, :, rows, :],
            dst_ref=halo.at[side, :, rows, :],
            send_sem=halo_send.at[side, k],
            recv_sem=halo_recv.at[side, k],
            device_id=onward[side],
            device_id_type=MESH,
        )

    def set_out(k):
        for side in range(2):
            leg_copy(side, k).start()

    def forward(k):
        for side in range(2):
            leg_copy(side, k).wait_recv()
            halo_copy(side, k).start()

    def label_copy(side):
        return pltpu.make_async_remote_copy(
            src_ref=lab_send.at[side],
            dst_ref=lab_recv.at[side],
            send_sem=lab_ssem.at[side],
            recv_sem=lab_rsem.at[side],
            device_id=(lat, lon_up if side == 0 else lon_dn),
            device_id_type=MESH,
        )

    loads[0].wait()
    lab_send[...] = jnp.zeros_like(lab_send)
    lab_send[0, 0:6, 0:ROWS] = lab_own[COLS - 6 : COLS, :]
    lab_send[1, 0:6, 0:ROWS] = lab_own[0:6, :]
    set_out(0)
    for side in range(2):
        label_copy(side).start()
    over_plane(1, lambda d, source: plane_copy(0, d, m).start())

    lane80 = lax.broadcasted_iota(I32, (80, 128), 1)
    for k in range(4):
        head_mask[k] = ((lane80 >= HD * k) & (lane80 < HD * k + HD)).astype(F32).astype(BF)
    t_in = lax.broadcasted_iota(I32, (80, 192), 0)
    place_in[...] = jnp.where(t_in < WIN, block_place(t_in), -1000)
    t_out = lax.broadcasted_iota(I32, (192, 80), 1)
    t_row = lax.broadcasted_iota(I32, (80, 128), 0)
    within = t_row - 36 * (t_row >= 36).astype(I32)
    second_owns[0] = (within < 18).astype(F32)
    second_owns[1] = (t_row < 36).astype(F32)
    for k, (least, most) in enumerate(((0, WIN), (36, WIN), (0, 36))):
        place_out[k] = jnp.where((t_out >= least) & (t_out < most), block_place(t_out), -1000)

    loads[1].wait()
    loads[2].wait()
    loads[3].wait()

    def own_column(c, carry):
        x = xo[c].astype(F32)
        acc[c + 6] = x
        xn[c + 6, :, 0:C] = normed_rows(x, gain[...])
        return carry

    lax.fori_loop(0, COLS // 2, own_column, 0, unroll=2)
    mirror_copy(1 - zhi).wait_recv()
    over_plane(1, lambda d, source: plane_copy(1, d, m).start())
    sibling_copy(core, m).start()
    set_out(1)
    set_out(2)
    lax.fori_loop(COLS // 2, COLS, own_column, 0, unroll=2)
    forward(0)

    def place_rows(count):
        half, c, r = token_parts(lax.broadcasted_iota(I32, (count, WIN), 0))
        place = jnp.where(
            lax.broadcasted_iota(I32, (count, WIN), 0) < WIN, (half * 3 + r) * 12 + c, -1
        )
        return (lax.broadcasted_iota(I32, (count, WIN), 1) == place).astype(F32)

    padded = lax.broadcasted_iota(I32, (80, 128), 0) >= WIN

    def bias_of(h, carry):
        keys_first = dot_nt(place_rows(80), bias_raw[h], lax.Precision.HIGHEST)
        placed = dot_nt(keys_first, place_rows(128), lax.Precision.HIGHEST)
        bias[h] = jnp.where(padded, MASKED, placed * LOG2E)
        return carry

    lax.fori_loop(0, HEADS, bias_of, 0, unroll=4)
    forward(1)

    for side in range(2):
        label_copy(side).wait_recv()
    lab_ext[0:6, :] = lab_recv[0, 0:6, 0:ROWS]
    lab_ext[6 : 6 + COLS, :] = lab_own[...]
    lab_ext[6 + COLS : EXT, :] = lab_recv[1, 0:6, 0:ROWS]
    eye = (
        lax.broadcasted_iota(I32, (ROWS, ROWS), 0) == lax.broadcasted_iota(I32, (ROWS, ROWS), 1)
    ).astype(BF)
    low = ((lax.broadcasted_iota(I32, (ROWS, EXT), 0) < 3) & (lat == 0)).astype(F32)
    lab_t[...] = dot_nt(eye, lab_ext[...].astype(F32).astype(BF)) + 3.0 * low

    def features(e, carry):
        lane = lax.broadcasted_iota(I32, (ROWS, EXT), 1)
        code = jnp.sum(jnp.where(lane == e, lab_t[...], 0.0), axis=1, keepdims=True)
        wide = lax.broadcasted_iota(I32, (ROWS, FEAT), 1).astype(F32)
        xn[e, :, C:WIDE] = (wide == code).astype(F32)
        return carry

    lax.fori_loop(0, EXT, features, 0, unroll=4)
    over_plane(1, pass_on)
    forward(2)

    def start_and_offset(i):
        start = 8 * ((13 * i) // 16)
        return start, 3 + 6 * i - start

    lane_in = lax.broadcasted_iota(I32, (80, 192), 1)

    def gather_pair(i, first, second, u):
        start, offset = start_and_offset(i)
        if not isinstance(i, int):
            start = pl.multiple_of(start, 8)
        select = (lane_in - offset == place_in[...]).astype(F32).astype(BF)
        for w, j in enumerate((first, second)):
            block = xn[12 * j : 12 * j + 12, pl.ds(start, 16), :].reshape(192, WIDE).astype(BF)
            xwin[u, 80 * w : 80 * w + 80, :] = dot(select, block).astype(BF)

    def gather_inner(i, carry):
        gather_pair(i, 1, 2, i)
        return carry

    lax.fori_loop(0, 7, gather_inner, 0)

    over_plane(0, lambda d, source: sibling_copy(1 - core, source).wait_recv())

    def halo_chunk(k):
        row = (0, 32, 16)[k]
        for side in range(2):
            halo_copy(side, k).wait_recv()

        def one(c, carry):
            for side in range(2):
                x = halo[side, c, row : row + 16, :].astype(F32)
                xn[c + side * (EXT - 6), row : row + 16, 0:C] = normed_rows(x, gain[...])
            return carry

        lax.fori_loop(0, 6, one, 0, unroll=3)

    def pack(row, offset):
        block = xn[:, row : row + 16, :].reshape(EXT * 16, WIDE).astype(BF)
        u = lax.broadcasted_iota(I32, (144, EXT * 16), 0)
        c = (u * 171) >> 9
        place = c * 16 + (u - 3 * c) + offset
        select = (lax.broadcasted_iota(I32, (144, EXT * 16), 1) == place).astype(F32).astype(BF)
        return dot(select, block).astype(BF)

    def lat_copy(up):
        if up:
            return pltpu.make_async_remote_copy(
                src_ref=pk_bot.at[0:144],
                dst_ref=pk_top.at[0:144],
                send_sem=lat_send.at[0],
                recv_sem=lat_recv.at[0],
                device_id=(lat_up, lon),
                device_id_type=MESH,
            )
        return pltpu.make_async_remote_copy(
            src_ref=pk_top.at[144:288],
            dst_ref=pk_bot.at[144:288],
            send_sem=lat_send.at[1],
            recv_sem=lat_recv.at[1],
            device_id=(lat_dn, lon),
            device_id_type=MESH,
        )

    def gather_edges():
        t = lax.broadcasted_iota(I32, (80, 288), 0)
        lane = lax.broadcasted_iota(I32, (80, 288), 1)
        place = jnp.where(t < WIN, t + 108 * (t >= 36).astype(I32), -1000)
        for j in range(4):
            select = (lane == place + 36 * j).astype(F32).astype(BF)
            for k, rows in enumerate((pk_top, pk_bot)):
                xwin[11 + j, 80 * k : 80 * k + 80, :] = dot(
                    select, rows[...]
                ).astype(BF)

    lane128 = lax.broadcasted_iota(I32, (80, 128), 1)

    def weight(k):
        return wbuf[k].reshape(C, C)

    def project(u):
        both = xwin[u, :, 0:C]
        for part in range(3):
            qkv[:, C * part : C * part + C] = dot(both, weight(part)).astype(BF)

    def mask_features(u, w):
        hot = xwin[u, 80 * w : 80 * w + 80, C:WIDE]
        differs = jnp.where(lane128 < 6, MASKED * (1.0 - hot.astype(F32)), 0.0).astype(BF)
        return hot, differs

    def parts_of(w, g):
        rows = slice(80 * w, 80 * w + 80)
        return (qkv[rows, C * part + 128 * g : C * part + 128 * g + 128] for part in range(3))

    def stack(pieces):
        return jnp.concatenate(
            [jnp.concatenate(pieces(head_mask[k]), axis=1) for k in range(4)], axis=0
        )

    def weights_of(scores, g):
        s = scores.reshape(4, 80, 80) * SCALE + bias[4 * g : 4 * g + 4, :, 0:80]
        e = jnp.exp2(s - jnp.max(s, axis=1, keepdims=True))
        return e.reshape(320, 80).astype(BF)

    def over_keys(e, values):
        return lax.dot_general(e, values, TN, preferred_element_type=F32)

    def attend_two(u):
        project(u)
        for w in range(2):
            hot, differs = mask_features(u, w)
            for g in range(4):
                query, key, value = parts_of(w, g)
                scores = dot_nt(
                    stack(lambda mask: [key * mask, hot]),
                    jnp.concatenate([query, differs], axis=1),
                )
                summed = over_keys(weights_of(scores, g), stack(lambda mask: [value * mask, mask]))
                ctx[80 * w : 80 * w + 80, 128 * g : 128 * g + 128] = (
                    summed[:, 0:128] * (1.0 / summed[:, 128:256])
                ).astype(BF)
        return dot(ctx[...], weight(3)).astype(BF)

    def attend_merged(u, kind):
        project(u)
        of_second = second_owns[kind]
        keep1 = of_second.astype(BF)
        keep0 = (1.0 - of_second).astype(BF)
        hot0, differs0 = mask_features(u, 0)
        hot1, differs1 = mask_features(u, 1)
        differs0 = differs0 * keep0
        differs1 = differs1 * keep1
        for g in range(4):
            query0, key0, value0 = parts_of(0, g)
            query1, key1, value1 = parts_of(1, g)
            scores = dot_nt(
                stack(lambda mask: [key0 * mask, hot0, key1 * mask, hot1]),
                jnp.concatenate([query0 * keep0, differs0, query1 * keep1, differs1], axis=1),
            )
            summed = over_keys(
                weights_of(scores, g), stack(lambda mask: [value0 * mask, value1 * mask, mask])
            )
            own = jnp.where(of_second > 0.5, summed[:, 128:256], summed[:, 0:128])
            ctx[0:80, 128 * g : 128 * g + 128] = (own * (1.0 / summed[:, 256:384])).astype(BF)
        return dot(ctx[0:80, :], weight(3)).astype(BF)

    row_out = lax.broadcasted_iota(I32, (192, 80), 0)

    def add_back(att, j, start, offset, kind):
        select = (row_out - offset == place_out[kind]).astype(F32).astype(BF)
        spot = (pl.ds(12 * j, 12), pl.ds(pl.multiple_of(start, 8), 16), slice(None))
        acc[spot] = acc[spot] + dot(select, att).reshape(12, 16, C)

    def inner_unit(u, carry):
        att = attend_two(u)
        start, offset = start_and_offset(u)
        for w in range(2):
            add_back(att[80 * w : 80 * w + 80], 1 + w, start, offset, 0)
        return carry

    lax.fori_loop(0, 7, inner_unit, 0)

    def finish(c, carry):
        xo[c] = acc[c + 6].astype(BF)
        return carry

    def store(k):
        part = (pl.ds(0, 6), pl.ds(6, COLS - 12), pl.ds(COLS - 6, 6))[k]
        return pltpu.make_async_copy(xo.at[part], out.at[part], out_sem.at[k])

    def merged_unit(v, carry):
        @pl.when(v == 0)
        def _():
            halo_chunk(0)
            pk_top[144:288, :] = pack(0, 0)
            lat_copy(False).start()
            for n in range(2):
                gather_pair(n, 0, 3, 7 + n)

        @pl.when(v == 2)
        def _():
            halo_chunk(1)
            pk_bot[0:144, :] = pack(32, 13)
            lat_copy(True).start()
            for n in range(2):
                gather_pair(5 + n, 0, 3, 9 + n)

        @pl.when(v == 4)
        def _():
            lat_copy(True).wait_recv()
            lat_copy(False).wait_recv()
            gather_edges()

        @pl.when(v == 8)
        def _():
            lax.fori_loop(6, COLS - 6, finish, 0, unroll=3)
            store(1).start()
            halo_chunk(2)
            for n in range(3):
                gather_pair(2 + n, 0, 3, 15 + n)

        edge = ((v >= 4) & (v < 8)).astype(I32)
        att = attend_merged(7 + v, edge)
        i = jnp.where(v < 2, v, jnp.where(v < 4, v + 3, v - 6))
        start, offset = start_and_offset(i)
        for w in range(2):
            j = jnp.where(edge == 1, v - 4, 3 * w)
            add_back(
                att,
                j,
                jnp.where(edge == 1, 32 * w, start),
                jnp.where(edge == 1, 16 * w - 3, offset),
                jnp.where(edge == 1, 1 + w, 0),
            )
        return carry

    lax.fori_loop(0, 11, merged_unit, 0)
    for k, first in ((0, 0), (2, COLS - 6)):
        lax.fori_loop(first, first + 6, finish, 0, unroll=3)
        store(k).start()

    mirror_copy(zhi).wait_send()
    over_plane(1, lambda d, source: plane_copy(0, d, m).wait_send())
    over_plane(1, lambda d, source: plane_copy(1, d, m).wait_send())
    over_plane(0, lambda d, source: sibling_copy(core, source).wait_send())
    for side in range(2):
        label_copy(side).wait_send()
        for k in range(3):
            leg_copy(side, k).wait_send()
            halo_copy(side, k).wait_send()
    lat_copy(True).wait_send()
    lat_copy(False).wait_send()
    for k in range(3):
        store(k).wait()


def local(tokens, region, ln_gain, qkv_weight, proj_weight, position_bias):
    nlat = lax.axis_size("lat")
    nlon = lax.axis_size("lon")
    plane = nlon // 2
    nx = min(4, plane)
    ny = plane // nx
    dma = pltpu.SemaphoreType.DMA
    vm = pltpu.VMEM
    mixed = pl.pallas_call(
        functools.partial(kernel, nlat, nlon),
        out_shape=jax.ShapeDtypeStruct((COLS, ROWS, C), BF),
        in_specs=[pl.BlockSpec(memory_space=pl.ANY)] * 6,
        out_specs=pl.BlockSpec(memory_space=pl.ANY),
        scratch_shapes=[
            vm((COLS, ROWS, C), BF),
            vm((2, 6, ROWS, C), BF),
            vm((2, 6, ROWS, C), BF),
            vm((COLS, ROWS), I32),
            vm((2, 8, 128), I32),
            vm((2, 8, 128), I32),
            vm((EXT, ROWS), I32),
            vm((ROWS, EXT), F32),
            vm((1, C), F32),
            vm((HEADS, WIN, WIN), F32),
            vm((HEADS, 80, 128), F32),
            vm((4, ny, nx, 2 * (C // nlon), C), BF),
            vm((EXT, ROWS, WIDE), F32),
            vm((EXT, ROWS, C), F32),
            vm((UNITS, 160, WIDE), BF),
            vm((288, WIDE), BF),
            vm((288, WIDE), BF),
            vm((160, 3 * C), BF),
            vm((160, C), BF),
            vm((4, 80, 128), BF),
            vm((80, 192), I32),
            vm((3, 192, 80), I32),
            vm((2, 80, 128), F32),
            dma((6,)),
            dma((4,)),
            dma,
            dma,
            dma((2, plane)),
            dma((2, plane)),
            dma((plane,)),
            dma((plane,)),
            dma((2, 3)),
            dma((2, 3)),
            dma((2, 3)),
            dma((2, 3)),
            dma((2,)),
            dma((2,)),
            dma((2,)),
            dma((2,)),
        ],
        compiler_params=pltpu.CompilerParams(
            collective_id=0, has_side_effects=True, vmem_limit_bytes=56 * 2**20
        ),
        cost_estimate=pl.CostEstimate(
            flops=8_000_000_000, bytes_accessed=12_000_000, transcendentals=6_000_000
        ),
    )(
        jnp.transpose(tokens, (1, 0, 2)),
        jnp.transpose(region, (1, 0)),
        ln_gain.reshape(1, C),
        qkv_weight,
        proj_weight,
        position_bias,
    )
    return jnp.transpose(mixed, (1, 0, 2))


def solution(mesh):
    return jax.shard_map(
        local,
        mesh=mesh,
        in_specs=(P("lat", "lon", None), P("lat", "lon"), P(), P("lon", None), P("lon", None), P()),
        out_specs=P("lat", "lon", None),
        check_vma=False,
    )
```
